32 devices in a mesh: tok: 8 (over y, x, core), fac: 4 (over z).
Axes of the slice: x: 2, y: 2, z: 4, core: 2. Of those that a mesh axis runs over, the one named last changes fastest.
Arguments:
- grad_rows: bfloat16 [4096, 6144], P('tok', 'fac'), may hold values from -6 to 6
- routes: int32 [4096, 1], P('tok'), may hold values from 0 to 1; in each aligned block of 512 rows (0 to 511, 512 to 1023, ...) at most 320 rows name the same one
- counts: int32 [8], P('tok'), may hold values from 64 to 512, as said below
- factor_old: float32 [12288, 6144], P('tok', 'fac'), as said below
- damping: float32 [2], replicated, may hold values from 0.1 to 1
- weight_grad: bfloat16 [12288, 8192], P('tok', 'fac'), may hold values from -6 to 6
Outputs:
- running: float32 [12288, 6144], P('tok', 'fac')
- factored: float32 [12288, 6144], P('tok', 'fac')
- preconditioned: float32 [12288, 8192], P('tok', 'fac')
The draws below stay inside these ranges and needn't reach their ends.
Inputs may be any that keep to these rules, and one draw needn't show every extreme that they name: `routes`: in the rows of one device, at most 320 rows name the same expert. The first counts[j] rows of index j of tok are live; the others take no part. `factor_old`: symmetric and positive definite.
All inputs are finite; a program needn't handle non-finite values.
Results may differ from the reference program's by a relative error of at most 0.0015.
Values may be sent and summed in bfloat16 or wider, within the bound.
No kernel may reach another device: no remote copies, remote signals or barrier semaphores. Data moves between devices by JAX's collectives and lax.ppermute only.
A program may use at most 192 MiB of HBM per device.

```python
import math
import jax
import jax.numpy as jnp
import numpy as np
from jax import lax

D = 6144
FF = 8192
PB = 256
TOK_DEV = 512
CAP = 320
TOKENS = 4096
SHARDS = 8


def draw_counts(key, part):
    key = jax.random.fold_in(key, 11)
    device_place = jnp.arange(SHARDS)
    baseline = TOK_DEV // 4 + 3 * TOK_DEV // 4 * (device_place + 1) // SHARDS
    jitter = jax.random.randint(key, (SHARDS,), 0, TOK_DEV // 8)
    return jnp.where(device_place == SHARDS - 1, TOK_DEV, baseline - jitter).astype(jnp.int32)


def draw_factor_old(key, part):
    key = jax.random.fold_in(key, 23)
    key_noise, key_diag = jax.random.split(key)
    random_part = jax.random.normal(key_noise, (2, D, D), jnp.float32)
    diagonal = jax.random.uniform(key_diag, (2, D), jnp.float32, 1.0, 2.0)
    symmetric = (random_part + jnp.swapaxes(random_part, 1, 2)) * (0.25 / math.sqrt(D))
    identity = jnp.arange(D)[:, None] == jnp.arange(D)[None, :]
    assembled = jnp.where(identity[None], diagonal[:, :, None], symmetric)
    return assembled.reshape(2 * D, D).astype(jnp.float32)


def block_scale(key, extent, shards, least, high):
    factor_of, own = 1.0, jax.random.fold_in(key, 6)
    for dim, shards_of in shards:
        draws = jnp.exp(jax.random.uniform(jax.random.fold_in(own, dim), (shards_of,), jnp.float32, least / len(shards), high / len(shards)))
        factor_of = factor_of * jnp.repeat(draws, extent[dim] // shards_of).reshape([-1 if axis == dim else 1 for axis in range(len(extent))])
    return factor_of


def assign_block(stream_key, own, number, rows, amount, top, most, slope):
    order = jax.random.permutation(stream_key, amount)
    packed, ordinary = shares(amount, rows * top, most, slope, True), shares(amount, rows * top, most, slope, False)
    places = jnp.arange(amount)

    def named(lengths, offset_by):
        used = int((lengths > 0).sum())
        fixed = max(1, used // 4)
        passed = fixed + (places - fixed + offset_by * (used - fixed)) % max(1, amount - fixed)
        return jnp.zeros((amount,), jnp.int32).at[order[jnp.where(places < fixed, places, passed)]].set(jnp.asarray(lengths, jnp.int32))

    lengths = jnp.where(number % 4 == 0, named(packed, number // 4), named(ordinary, number - number // 4 - 1))
    mixed = jax.random.permutation(jax.random.fold_in(own, 3), amount)
    donor, taker = mixed[0:amount // 2 * 2:2], mixed[1:amount // 2 * 2:2]
    room = jnp.minimum(lengths[donor] - 1, most - lengths[taker]) // 2
    room = jnp.where((donor == order[0]) | (taker == order[0]) | (lengths[taker] == 0), 0, jnp.maximum(room, 0))
    passed = jax.random.randint(jax.random.fold_in(own, 4), (amount // 2,), 0, 1 << 20) % (room + 1)
    lengths = lengths.at[donor].add(-passed).at[taker].add(passed)
    members = jnp.searchsorted(jnp.cumsum(lengths), jnp.arange(rows * top), side="right").astype(jnp.int32)
    grid = members.reshape(top, rows).T
    grid = grid[jax.random.permutation(jax.random.fold_in(own, 1), rows)]
    offset_by = jax.random.randint(jax.random.fold_in(own, 2), (rows, 1), 0, top)
    return jnp.take_along_axis(grid, (jnp.arange(top)[None, :] + offset_by) % top, axis=1)


def shares(amount, total, reach, slope, full):
    portions = [(1 << 20) // math.isqrt(standing ** slope) + 1 for standing in range(1, amount + 1)]
    largest = reach if full else min(reach, max(-(-total // amount), total * portions[0] // sum(portions)))
    least = 1 if total - largest >= amount - 1 else 0
    given, surplus = [largest] + [least] * (amount - 1), total - largest - least * (amount - 1)
    while surplus > 0:
        movable = [i for i in range(1, amount) if given[i] < largest] or [i for i in range(1, amount) if given[i] < reach]
        whole, remaining = sum([portions[i] for i in movable]), surplus
        for i in movable:
            addition = min(reach - given[i], max(1, remaining * portions[i] // whole), surplus)
            given[i] = given[i] + addition
            surplus = surplus - addition
    return np.array(given)


def gaussian(own_key, extent, scale, limit, shards=(), kind=jnp.bfloat16):
    loudness = block_scale(own_key, extent, shards, -0.22, 0.18) if shards else 1.0
    values = jax.random.normal(own_key, extent, jnp.float32) * scale * loudness
    return jnp.minimum(jnp.maximum(values, -limit), limit).astype(kind)


def setup_inputs(seed: int = 0) -> dict:
    splits = jax.random.split(jax.random.key(seed), 7)
    grad_rows = gaussian(splits[0], (TOKENS, D), 1.0, 6.0, ((0, 8), (1, 4)))
    routes_keys = jax.random.split(jax.random.fold_in(splits[1], 1), TOKENS // TOK_DEV)
    routes_turns = jax.random.permutation(jax.random.fold_in(splits[1], 3), TOKENS // TOK_DEV)
    routes = jax.vmap(lambda own, number: assign_block(jax.random.fold_in(splits[1], 2), own, number, TOK_DEV, 2, 1, CAP, 0))(routes_keys, routes_turns).reshape((TOKENS, 1))
    counts = draw_counts(jax.random.fold_in(splits[6], 71), 0)
    factor_old = draw_factor_old(jax.random.fold_in(splits[6], 71), 0)
    damping = jnp.clip(jnp.exp(jax.random.uniform(splits[4], (2,), jnp.float32, math.log(0.1), math.log(1.0))), 0.1, 1.0)
    weight_grad = gaussian(splits[5], (2 * D, FF), 1.0, 6.0, ((0, 8), (1, 4)))
    return {"grad_rows": grad_rows, "routes": routes, "counts": counts, "factor_old": factor_old, "damping": damping, "weight_grad": weight_grad}


DECAY = 0.8

def lower_solve(factor, values):
    return jax.scipy.linalg.solve_triangular(factor, values, lower=True)

def highest(left_side, right_side):
    return jnp.dot(left_side, right_side, precision=lax.Precision.HIGHEST)

def reference(grad_rows, routes, counts, factor_old, damping, weight_grad):
    positions = jnp.arange(TOKENS)
    live_rows = positions % TOK_DEV < counts[positions // TOK_DEV]
    indices = jnp.arange(D)
    running_parts = []
    factored_parts = []
    precond_parts = []
    for expert in range(2):
        chosen = live_rows & (routes[:, 0] == expert)
        masked = jnp.where(chosen[:, None], grad_rows, jnp.zeros_like(grad_rows)).astype(jnp.float32)
        gram_sum = highest(masked.T, masked)
        token_total = jnp.sum(chosen.astype(jnp.float32))
        old_block = factor_old[expert * D:(expert + 1) * D]
        running = DECAY * old_block + (1.0 - DECAY) * (gram_sum / token_total)
        matrix = running + jnp.where(indices[:, None] == indices[None, :], damping[expert], 0.0)
        lowers = []
        panels = []
        for panel_step in range(2):
            begin_col = panel_step * PB
            end_col = begin_col + PB
            diag_factor = jnp.linalg.cholesky(matrix[begin_col:end_col, begin_col:end_col])
            solved = lower_solve(diag_factor, matrix[:, begin_col:end_col].T).T
            lower_panel = jnp.where(indices[:, None] >= end_col, solved, 0.0)
            lower_panel = lower_panel.at[begin_col:end_col].set(diag_factor)
            trailing = (indices[:, None] >= end_col) & (indices[None, :] >= end_col)
            matrix = jnp.where(trailing, matrix - highest(lower_panel, lower_panel.T), matrix)
            matrix = matrix.at[:, begin_col:end_col].set(lower_panel)
            matrix = matrix.at[begin_col:end_col, end_col:].set(0.0)
            lowers.append(diag_factor)
            panels.append(lower_panel)
        gradient = weight_grad[expert * D:(expert + 1) * D].astype(jnp.float32)
        first_solve = lower_solve(lowers[0], gradient[0:PB])
        second_in = gradient[PB:2 * PB] - highest(panels[0][PB:2 * PB], first_solve)
        second = lower_solve(lowers[1], second_in)
        remainder = gradient - highest(panels[0], first_solve) - highest(panels[1], second)
        precond = remainder.at[0:2 * PB].set(jnp.concatenate([first_solve, second], 0))
        running_parts.append(running)
        factored_parts.append(matrix)
        precond_parts.append(precond)
    return (jnp.concatenate(running_parts, 0), jnp.concatenate(factored_parts, 0), jnp.concatenate(precond_parts, 0))
```

```python
import jax
import jax.numpy as jnp
from jax import lax
from jax.experimental import pallas as pl
from jax.experimental.pallas import tpu as pltpu
from jax.sharding import PartitionSpec as P

CAP = 320
LEAD = 512
TILE = 128
GROUP = 8
DECAY = 0.8

HIGHEST = lax.Precision.HIGHEST
BF16 = jnp.bfloat16
F32 = jnp.float32


def dot_t(left, right, precision=None):
    return lax.dot_general(
        left, right, (((0,), (0,)), ((), ())), precision=precision, preferred_element_type=F32
    )


def splat(rows, lane):
    return jnp.broadcast_to(rows[:, lane : lane + 1], rows.shape)


def eliminate_tile(rows):
    lanes = lax.broadcasted_iota(jnp.int32, (GROUP, TILE), 1)
    subs = lax.broadcasted_iota(jnp.int32, (GROUP, TILE), 0)
    upper, inverse = [], []
    for step in range(TILE // GROUP):
        base = step * GROUP
        inside = (lanes >= base) & (lanes < base + GROUP)
        block = rows[step]
        first = [jnp.broadcast_to(block[t : t + 1, :], (GROUP, TILE)) for t in range(GROUP)]
        second = [
            jnp.where(inside, jnp.where(lanes == base + t, 1.0, 0.0), first[t])
            for t in range(GROUP)
        ]
        pivot = [
            [splat(first[t], base + u) if u >= t else None for u in range(GROUP)]
            for t in range(GROUP)
        ]
        scale = [None] * GROUP
        for t in range(GROUP):
            scale[t] = lax.rsqrt(pivot[t][t])
            for u in range(t + 1, GROUP):
                pivot[t][u] = pivot[t][u] * scale[t]
            for u in range(t + 1, GROUP):
                for w in range(u, GROUP):
                    pivot[u][w] = pivot[u][w] - pivot[t][u] * pivot[t][w]
            first[t] = first[t] * scale[t]
            second[t] = second[t] * scale[t]
            for u in range(t + 1, GROUP):
                first[u] = first[u] - pivot[t][u] * first[t]
                second[u] = second[u] - pivot[t][u] * second[t]
        solved = [None] * GROUP
        for t in reversed(range(GROUP)):
            value = second[t]
            for u in range(t + 1, GROUP):
                value = value - pivot[t][u] * solved[u]
            solved[t] = value * scale[t]
        for later in range(step + 1, TILE // GROUP):
            value = jnp.where(inside, 0.0, rows[later])
            for t in range(GROUP):
                value = value - splat(rows[later], base + t) * solved[t]
            rows[later] = value
        upper_rows, inverse_rows = first[0], second[0]
        for t in range(1, GROUP):
            upper_rows = jnp.where(subs == t, first[t], upper_rows)
            inverse_rows = jnp.where(subs == t, second[t], inverse_rows)
        upper.append(upper_rows)
        inverse.append(inverse_rows)
    return upper, inverse


def factor_kernel(matrix_ref, upper_ref, inverse_ref, work_ref):
    steps = LEAD // TILE
    work_ref[...] = matrix_ref[...]
    upper_ref[...] = jnp.zeros_like(upper_ref)
    inverse_ref[...] = jnp.zeros_like(inverse_ref)
    lanes = lax.broadcasted_iota(jnp.int32, (GROUP, TILE), 1)
    subs = lax.broadcasted_iota(jnp.int32, (GROUP, TILE), 0)

    def tile_step(k, carry):
        begin = pl.multiple_of(k * TILE, TILE)
        rows = [
            work_ref[pl.ds(begin + g * GROUP, GROUP), pl.ds(begin, TILE)]
            for g in range(TILE // GROUP)
        ]
        upper, inverse = eliminate_tile(rows)
        upper_tile = jnp.concatenate(
            [jnp.where(lanes >= subs + g * GROUP, part, 0.0) for g, part in enumerate(upper)], 0
        )
        inverse_tile = jnp.concatenate(
            [jnp.where(lanes <= subs + g * GROUP, part, 0.0) for g, part in enumerate(inverse)], 0
        )
        band = jnp.dot(
            inverse_tile,
            work_ref[pl.ds(begin, TILE), :],
            precision=HIGHEST,
            preferred_element_type=F32,
        )
        work_ref[pl.ds(begin, TILE), :] = band
        work_ref[pl.ds(begin, TILE), pl.ds(begin, TILE)] = inverse_tile
        upper_ref[pl.ds(begin, TILE), pl.ds(begin, TILE)] = upper_tile
        inverse_ref[pl.ds(begin, TILE), pl.ds(begin, TILE)] = inverse_tile
        for other in range(steps):

            @pl.when(other < k)
            def _():
                inverse_ref[pl.ds(begin, TILE), other * TILE : (other + 1) * TILE] = work_ref[
                    pl.ds(begin, TILE), other * TILE : (other + 1) * TILE
                ]

            @pl.when(other > k)
            def _():
                span = slice(other * TILE, (other + 1) * TILE)
                part = work_ref[pl.ds(begin, TILE), span]
                upper_ref[pl.ds(begin, TILE), span] = part
                work_ref[span, pl.ds(begin, TILE)] = jnp.zeros((TILE, TILE), F32)
                work_ref[span, :] = work_ref[span, :] - dot_t(
                    part, work_ref[pl.ds(begin, TILE), :], HIGHEST
                )

        return carry

    lax.fori_loop(0, steps, tile_step, 0)


def factor_lead(matrix):
    shape = jax.ShapeDtypeStruct((LEAD, LEAD), F32)
    return pl.pallas_call(
        factor_kernel,
        out_shape=(shape, shape),
        in_specs=[pl.BlockSpec(memory_space=pltpu.VMEM)],
        out_specs=(pl.BlockSpec(memory_space=pltpu.VMEM), pl.BlockSpec(memory_space=pltpu.VMEM)),
        scratch_shapes=[pltpu.VMEM((LEAD, LEAD), F32)],
        compiler_params=pltpu.CompilerParams(vmem_limit_bytes=32 * 1024 * 1024),
        cost_estimate=pl.CostEstimate(
            flops=20_000_000_000, bytes_accessed=3 * LEAD * LEAD * 4, transcendentals=LEAD
        ),
    )(matrix)


def swapped(value, mask):
    size = lax.axis_size("tok")
    return lax.ppermute(value, "tok", [(source, source ^ mask) for source in range(size)])


def gather_members(value, bits):
    for bit in reversed(range(bits)):
        value = jnp.concatenate([value, swapped(value, 1 << bit)], 0)
    return value


def exchange_members(blocks, member, bits):
    for bit in reversed(range(bits)):
        half = blocks.shape[0] // 2
        mine = member >> bit & 1
        keep = lax.dynamic_slice_in_dim(blocks, mine * half, half, 0)
        send = lax.dynamic_slice_in_dim(blocks, (1 - mine) * half, half, 0)
        blocks = jnp.concatenate([keep, swapped(send, 1 << bit)], 1)
    return blocks[0]


def from_first_member(value, member, group, bits):
    value = jnp.where(member == 0, value, jnp.zeros_like(value))
    for bit in reversed(range(bits)):
        mask = 1 << bit
        pairs = [
            (source, source + mask)
            for source in range(lax.axis_size("tok"))
            if source % group % (2 * mask) == 0
        ]
        value = value + lax.ppermute(value, "tok", pairs)
    return value


def lines(hops, group):
    toks, facs = lax.axis_size("tok"), lax.axis_size("fac")
    pairs = []
    for tok in range(toks):
        root = tok % group
        for before, after in hops:
            if 0 <= root + before < facs and 0 <= root + after < facs:
                pairs.append((tok * facs + root + before, tok * facs + root + after))
    return pairs


def from_own_column(value, member, column, group):
    axes = ("tok", "fac")
    facs = lax.axis_size("fac")
    upward = lax.ppermute(value, axes, lines([(0, 1)], group))
    downward = lax.ppermute(value, axes, lines([(0, -1)], group))
    moving = upward + downward
    total = jnp.where(member == column, value, moving)
    for distance in range(1, facs - 1):
        pairs = lines([(distance, distance + 1), (-distance, -distance - 1)], group)
        moving = lax.ppermute(moving, axes, pairs)
        total = total + moving
    return total


def local(grad_rows, routes, counts, factor_old, damping, weight_grad):
    group = lax.axis_size("tok") // 2
    facs = lax.axis_size("fac")
    bits = group.bit_length() - 1
    position = lax.axis_index("tok")
    expert = position // group
    member = position % group
    column = lax.axis_index("fac")
    tok_rows, width = grad_rows.shape
    grad_cols = weight_grad.shape[1]
    damp = jnp.where(expert == 0, damping[0], damping[1])

    near = from_first_member(
        jnp.concatenate([factor_old[:LEAD].astype(BF16), weight_grad[:LEAD]], 1),
        member,
        group,
        bits,
    )
    near_factor, near_grad = near[:, :width], near[:, width:]
    corner = jnp.where(column == 0, factor_old[:LEAD, :LEAD], 0.0)
    moving = corner
    for place in range(facs - 1):
        moving = lax.ppermute(moving, "fac", [(place, place + 1)])
        corner = corner + moving
    corner = from_first_member(corner, member, group, bits)

    live = jnp.arange(tok_rows) < counts[0]
    named = routes[:, 0]
    own = live & (named == expert)
    away = live & (named != expert)
    flags = jnp.stack([own, away])
    ranks = jnp.cumsum(flags.astype(jnp.int32), 1) - 1
    picker = (ranks[:, None, :] == jnp.arange(CAP)[None, :, None]) & flags[:, None, :]
    packed = jnp.dot(
        picker.reshape(2 * CAP, tok_rows).astype(BF16), grad_rows, preferred_element_type=F32
    ).astype(BF16)
    tally = jnp.sum(flags.astype(F32), 1)
    tally = jnp.broadcast_to(tally[:, None], (2, 128))
    other = swapped(tally, group)
    total = tally[0] + other[1]
    for bit in range(bits):
        total = total + swapped(total, 1 << bit)
    share = (1.0 - DECAY) / total[0]

    chunks = [(begin, min(begin + LEAD, width)) for begin in range(0, width, LEAD)]
    quarters = []
    for begin, end in chunks:
        incoming = swapped(packed[CAP:, begin:end], group)
        quarters.append(jnp.concatenate([packed[:CAP, begin:end], incoming], 0))
    spread = [lax.all_gather(quarter, "fac") for quarter in quarters]
    lead = gather_members(spread[0][0][:, :LEAD], bits)
    across = gather_members(jnp.concatenate(quarters, 1), bits)
    down = [exchange_members(part, member, bits) for part in spread]

    eye = jnp.eye(LEAD, dtype=F32)
    top = DECAY * corner + share * dot_t(lead, lead) + damp * eye
    upper, inverse = factor_lead(top)
    lower = upper.T
    beside = DECAY * near_factor.astype(F32) + share * dot_t(lead, across)
    panel_cols = jnp.dot(inverse, beside, precision=lax.Precision.HIGH).astype(BF16)
    panel_rows = from_own_column(panel_cols, member, column, group)
    solution_rows = jnp.dot(inverse, near_grad.astype(F32), precision=lax.Precision.HIGH)

    gram = jnp.concatenate([dot_t(part, across) for part in down], 0)
    running = DECAY * factor_old + share * gram

    row_index = jnp.arange(width)[:, None]
    col_index = jnp.arange(width)[None, :]
    diagonal = member * width + row_index == column * width + col_index
    matrix = running + jnp.where(diagonal, damp, 0.0)
    head = (member == 0) & (row_index < LEAD)
    updated = jnp.where(head, 0.0, matrix - dot_t(panel_rows, panel_cols))
    first = lax.dot_general(
        matrix[:, :LEAD],
        inverse,
        (((1,), (1,)), ((), ())),
        precision=lax.Precision.HIGH,
        preferred_element_type=F32,
    )
    first = jnp.where(head, jnp.pad(lower, ((0, width - LEAD), (0, 0))), first)
    factored = lax.dynamic_update_slice(
        updated, jnp.where(column == 0, first, updated[:, :LEAD]), (0, 0)
    )

    minus = jnp.pad(-jnp.eye(LEAD, dtype=BF16), ((0, 0), (0, width - LEAD)))
    weights = jnp.where(head.T, minus, panel_rows)
    high = solution_rows.astype(BF16)
    low = (solution_rows - high.astype(F32)).astype(BF16)
    product = dot_t(jnp.concatenate([weights, weights], 0), jnp.concatenate([high, low], 0))
    precond = jnp.where(head, 0.0, weight_grad.astype(F32)) - product
    return (running, factored, precond)


def solution(mesh):
    placed = (P("tok", "fac"), P("tok", None), P("tok"), P("tok", "fac"), P(), P("tok", "fac"))
    return jax.shard_map(
        local,
        mesh=mesh,
        in_specs=placed,
        out_specs=(P("tok", "fac"), P("tok", "fac"), P("tok", "fac")),
        check_vma=False,
    )
```

```python
import jax
import jax.numpy as jnp
from jax import lax
from jax.experimental import pallas as pl
from jax.experimental.pallas import tpu as pltpu
from jax.sharding import PartitionSpec as P

CAP = 320
LEAD = 512
TILE = 128
GROUP = 8
ROWS = 256
COLS = 512
DECAY = 0.8

HIGHEST = lax.Precision.HIGHEST
BF16 = jnp.bfloat16
F32 = jnp.float32


def dot_t(left, right, precision=None):
    return lax.dot_general(
        left, right, (((0,), (0,)), ((), ())), precision=precision, preferred_element_type=F32
    )


def splat(rows, lane):
    return jnp.broadcast_to(rows[:, lane : lane + 1], rows.shape)


def eliminate_tile(rows):
    lanes = lax.broadcasted_iota(jnp.int32, (GROUP, TILE), 1)
    subs = lax.broadcasted_iota(jnp.int32, (GROUP, TILE), 0)
    upper, inverse = [], []
    for step in range(TILE // GROUP):
        base = step * GROUP
        inside = (lanes >= base) & (lanes < base + GROUP)
        block = rows[step]
        first = [jnp.broadcast_to(block[t : t + 1, :], (GROUP, TILE)) for t in range(GROUP)]
        second = [
            jnp.where(inside, jnp.where(lanes == base + t, 1.0, 0.0), first[t])
            for t in range(GROUP)
        ]
        pivot = [
            [splat(first[t], base + u) if u >= t else None for u in range(GROUP)]
            for t in range(GROUP)
        ]
        scale = [None] * GROUP
        for t in range(GROUP):
            scale[t] = lax.rsqrt(pivot[t][t])
            for u in range(t + 1, GROUP):
                pivot[t][u] = pivot[t][u] * scale[t]
            for u in range(t + 1, GROUP):
                for w in range(u, GROUP):
                    pivot[u][w] = pivot[u][w] - pivot[t][u] * pivot[t][w]
            first[t] = first[t] * scale[t]
            second[t] = second[t] * scale[t]
            for u in range(t + 1, GROUP):
                first[u] = first[u] - pivot[t][u] * first[t]
                second[u] = second[u] - pivot[t][u] * second[t]
        solved = [None] * GROUP
        for t in reversed(range(GROUP)):
            value = second[t]
            for u in range(t + 1, GROUP):
                value = value - pivot[t][u] * solved[u]
            solved[t] = value * scale[t]
        for later in range(step + 1, TILE // GROUP):
            value = jnp.where(inside, 0.0, rows[later])
            for t in range(GROUP):
                value = value - splat(rows[later], base + t) * solved[t]
            rows[later] = value
        upper_rows, inverse_rows = first[0], second[0]
        for t in range(1, GROUP):
            upper_rows = jnp.where(subs == t, first[t], upper_rows)
            inverse_rows = jnp.where(subs == t, second[t], inverse_rows)
        upper.append(upper_rows)
        inverse.append(inverse_rows)
    return upper, inverse


def factor_kernel(scalars_ref, corner_ref, *refs):
    *lead_refs, upper_ref, inverse_ref, work_ref = refs
    steps = LEAD // TILE
    gram = sum(dot_t(lead[...], lead[...]) for lead in lead_refs)
    rows = lax.broadcasted_iota(jnp.int32, (LEAD, LEAD), 0)
    cols = lax.broadcasted_iota(jnp.int32, (LEAD, LEAD), 1)
    work_ref[...] = (
        DECAY * corner_ref[...]
        + scalars_ref[0] * gram
        + jnp.where(rows == cols, scalars_ref[1], 0.0)
    )
    upper_ref[...] = jnp.zeros_like(upper_ref)
    inverse_ref[...] = jnp.zeros_like(inverse_ref)
    lanes = lax.broadcasted_iota(jnp.int32, (GROUP, TILE), 1)
    subs = lax.broadcasted_iota(jnp.int32, (GROUP, TILE), 0)

    def tile_step(k, carry):
        begin = pl.multiple_of(k * TILE, TILE)
        rows = [
            work_ref[pl.ds(begin + g * GROUP, GROUP), pl.ds(begin, TILE)]
            for g in range(TILE // GROUP)
        ]
        upper, inverse = eliminate_tile(rows)
        upper_tile = jnp.concatenate(
            [jnp.where(lanes >= subs + g * GROUP, part, 0.0) for g, part in enumerate(upper)], 0
        )
        inverse_tile = jnp.concatenate(
            [jnp.where(lanes <= subs + g * GROUP, part, 0.0) for g, part in enumerate(inverse)], 0
        )
        band = jnp.dot(
            inverse_tile,
            work_ref[pl.ds(begin, TILE), :],
            precision=HIGHEST,
            preferred_element_type=F32,
        )
        work_ref[pl.ds(begin, TILE), :] = band
        work_ref[pl.ds(begin, TILE), pl.ds(begin, TILE)] = inverse_tile
        upper_ref[pl.ds(begin, TILE), pl.ds(begin, TILE)] = upper_tile
        inverse_ref[pl.ds(begin, TILE), pl.ds(begin, TILE)] = inverse_tile
        for other in range(steps):

            @pl.when(other < k)
            def _():
                inverse_ref[pl.ds(begin, TILE), other * TILE : (other + 1) * TILE] = work_ref[
                    pl.ds(begin, TILE), other * TILE : (other + 1) * TILE
                ]

            @pl.when(other > k)
            def _():
                span = slice(other * TILE, (other + 1) * TILE)
                part = work_ref[pl.ds(begin, TILE), span]
                upper_ref[pl.ds(begin, TILE), span] = part
                work_ref[span, pl.ds(begin, TILE)] = jnp.zeros((TILE, TILE), F32)
                work_ref[span, :] = work_ref[span, :] - dot_t(
                    part, work_ref[pl.ds(begin, TILE), :], HIGHEST
                )

        return carry

    lax.fori_loop(0, steps, tile_step, 0)


def factor_lead(scalars, corner, lead):
    shape = jax.ShapeDtypeStruct((LEAD, LEAD), F32)
    vmem = pl.BlockSpec(memory_space=pltpu.VMEM)
    return pl.pallas_call(
        factor_kernel,
        out_shape=(shape, shape),
        in_specs=[pl.BlockSpec(memory_space=pltpu.SMEM)] + [vmem] * (1 + len(lead)),
        out_specs=(vmem, vmem),
        scratch_shapes=[pltpu.VMEM((LEAD, LEAD), F32)],
        compiler_params=pltpu.CompilerParams(vmem_limit_bytes=32 * 1024 * 1024),
        cost_estimate=pl.CostEstimate(
            flops=25_000_000_000, bytes_accessed=6 * LEAD * LEAD * 4, transcendentals=LEAD
        ),
    )(scalars, corner, *lead)


def panel_kernel(scalars_ref, inverse_ref, factor_ref, *refs):
    *pieces, out_ref = refs
    half = len(pieces) // 2
    gram = sum(dot_t(pieces[q][...], pieces[half + q][...]) for q in range(half))
    beside = DECAY * factor_ref[...].astype(F32) + scalars_ref[0] * gram
    out_ref[...] = jnp.dot(
        inverse_ref[...], beside, precision=HIGHEST, preferred_element_type=F32
    ).astype(BF16)


def panel_columns(scalars, inverse, near_factor, lead, across):
    width = near_factor.shape[1]
    cols = COLS if width % COLS == 0 else ROWS
    rows = lead[0].shape[0]
    whole = lambda height: pl.BlockSpec((height, LEAD), lambda j: (0, 0))
    tiled = lambda height: pl.BlockSpec((height, cols), lambda j: (0, j))
    return pl.pallas_call(
        panel_kernel,
        grid=(width // cols,),
        out_shape=jax.ShapeDtypeStruct((LEAD, width), BF16),
        in_specs=[pl.BlockSpec(memory_space=pltpu.SMEM), whole(LEAD), tiled(LEAD)]
        + [whole(rows)] * len(lead)
        + [tiled(rows)] * len(across),
        out_specs=tiled(LEAD),
        compiler_params=pltpu.CompilerParams(vmem_limit_bytes=48 * 1024 * 1024),
        cost_estimate=pl.CostEstimate(
            flops=2 * width * LEAD * (rows * len(lead) + 6 * LEAD),
            bytes_accessed=2 * rows * len(lead) * (width + LEAD) + 4 * LEAD * width,
            transcendentals=0,
        ),
    )(scalars, inverse, near_factor, *lead, *across)


def finish_kernel(
    count,
    gram_steps,
    first_chunk,
    aliased,
    places_ref,
    scalars_ref,
    factor_ref,
    first_ref,
    grad_ref,
    panel_ref,
    inverse_ref,
    lower_ref,
    high_ref,
    low_ref,
    *refs,
):
    mine, lead, across = refs[:count], refs[count : 2 * count], refs[2 * count : 3 * count]
    running_ref, factored_ref, precond_ref, mine_ref, rows_ref = refs[3 * count + aliased :]
    j, i = pl.program_id(0), pl.program_id(1)
    member, column, base = places_ref[0], places_ref[1], places_ref[2]
    share, damp = scalars_ref[0], scalars_ref[1]
    height = ROWS
    depth = mine[0].shape[1]
    cols = running_ref.shape[1]
    span = pl.ds(pl.multiple_of(i * height, height), height)
    head = (member == 0) & first_chunk

    @pl.when(j == 0)
    def _():
        for q in range(count):
            mine_ref[span, q * depth : (q + 1) * depth] = mine[q][0].T
        source = first_ref[...].astype(F32)
        if cols == LEAD:
            source = jnp.where(column == 0, factor_ref[...], source)
        stacked = jnp.concatenate([part[...] for part in lead], 0)
        gram = jnp.dot(mine_ref[span, :], stacked, preferred_element_type=F32)
        row = base + i * height + lax.broadcasted_iota(jnp.int32, (height, LEAD), 0)
        col = lax.broadcasted_iota(jnp.int32, (height, LEAD), 1)
        source = DECAY * source + share * gram
        source = source + jnp.where(row == col, damp, 0.0)
        rows_ref[span, :] = lax.dot_general(
            source,
            inverse_ref[...],
            (((1,), (1,)), ((), ())),
            precision=HIGHEST,
            preferred_element_type=F32,
        )

    panel = rows_ref[span, :].astype(BF16)

    @pl.when(j < gram_steps)
    def _():
        stacked = jnp.concatenate([part[...] for part in across], 0)
        gram = jnp.dot(mine_ref[span, :], stacked, preferred_element_type=F32)
        running = DECAY * factor_ref[...] + share * gram
        running_ref[...] = running
        row = base + i * height + lax.broadcasted_iota(jnp.int32, (height, cols), 0)
        col = (column * gram_steps + j) * cols + lax.broadcasted_iota(jnp.int32, (height, cols), 1)
        matrix = running + jnp.where(row == col, damp, 0.0)
        factored = matrix - jnp.dot(panel, panel_ref[...], preferred_element_type=F32)
        factored_ref[...] = jnp.where(head, 0.0, factored)

        for part in range(LEAD // cols):
            side = slice(part * cols, (part + 1) * cols)

            @pl.when((column == 0) & (j == part))
            def _():
                factored_ref[...] = rows_ref[span, side]

                @pl.when(head)
                def _():
                    factored_ref[...] = lower_ref[span, side]

    high, low = high_ref[...], low_ref[...]
    product = jnp.dot(panel, high, preferred_element_type=F32)
    product = product + jnp.dot(panel, low, preferred_element_type=F32)
    precond_ref[...] = grad_ref[...].astype(F32) - product

    @pl.when(head)
    def _():
        precond_ref[...] = high_ref[span, :].astype(F32) + low_ref[span, :].astype(F32)


def finish_rows(
    begin, places, scalars, factor, first, grad, panel, inverse, lower, high, low,
    mine, lead, across, earlier,
):
    count = len(mine)
    depth, rows = mine[0].shape[1:]
    width, grad_cols = factor.shape[0], grad.shape[1]
    tiles = rows // ROWS
    start = begin // ROWS
    cols = COLS if width % COLS == 0 else ROWS
    gram_steps = width // cols
    grad_tile = cols
    steps = max(gram_steps, grad_cols // grad_tile)
    grad_steps = grad_cols // grad_tile
    assert steps == grad_steps and rows % ROWS == 0

    def once(j, i):
        return jnp.where(j == 0, i, tiles - 1)

    def mine_spec(q):
        return pl.BlockSpec((1, depth, ROWS), lambda j, i, p: (p[3 + q], 0, once(j, i)))

    def gram_col(j):
        return jnp.minimum(j, gram_steps - 1)

    def gram_tile(j, i, p):
        return (start + jnp.where(j < gram_steps, i, tiles - 1), gram_col(j))

    grad_spec = pl.BlockSpec((ROWS, grad_tile), lambda j, i, p: (start + i, j))
    factor_spec = pl.BlockSpec((ROWS, cols), gram_tile)
    lead_whole = pl.BlockSpec((LEAD, LEAD), lambda j, i, p: (0, 0))
    in_specs = [
        pl.BlockSpec(memory_space=pltpu.SMEM),
        factor_spec,
        pl.BlockSpec((ROWS, LEAD), lambda j, i, p: (start + once(j, i), 0)),
        grad_spec,
        pl.BlockSpec((LEAD, cols), lambda j, i, p: (0, gram_col(j))),
        lead_whole,
        lead_whole,
        pl.BlockSpec((LEAD, grad_tile), lambda j, i, p: (0, j)),
        pl.BlockSpec((LEAD, grad_tile), lambda j, i, p: (0, j)),
    ]
    in_specs += [mine_spec(q) for q in range(count)]
    in_specs += [pl.BlockSpec((depth, LEAD), lambda j, i, p: (0, 0))] * count
    in_specs += [pl.BlockSpec((depth, cols), lambda j, i, p: (0, gram_col(j)))] * count
    in_specs += [pl.BlockSpec(memory_space=pl.ANY)] * len(earlier)
    operands = [scalars, factor, first, grad, panel, inverse, lower, high, low]
    operands += [*mine, *lead, *across, *earlier]
    aliases = {1 + len(operands) - len(earlier) + k: k for k in range(len(earlier))}
    tall = depth * count
    return pl.pallas_call(
        lambda *refs: finish_kernel(count, gram_steps, begin == 0, len(earlier), *refs),
        grid_spec=pltpu.PrefetchScalarGridSpec(
            num_scalar_prefetch=1,
            grid=(steps, tiles),
            in_specs=in_specs,
            out_specs=(factor_spec, factor_spec, grad_spec),
            scratch_shapes=[pltpu.VMEM((rows, tall), BF16), pltpu.VMEM((rows, LEAD), F32)],
        ),
        out_shape=(
            jax.ShapeDtypeStruct(factor.shape, F32),
            jax.ShapeDtypeStruct(factor.shape, F32),
            jax.ShapeDtypeStruct(grad.shape, F32),
        ),
        input_output_aliases=aliases,
        compiler_params=pltpu.CompilerParams(vmem_limit_bytes=56 * 1024 * 1024),
        cost_estimate=pl.CostEstimate(
            flops=2 * rows * (tall * (width + LEAD) + LEAD * (6 * LEAD + width + 2 * grad_cols)),
            bytes_accessed=2 * tall * (width + LEAD + rows)
            + rows * (12 * width + 6 * grad_cols)
            + LEAD * (4 * grad_cols + 8 * LEAD + 2 * width),
            transcendentals=0,
        ),
    )(places, *operands)


def after(value, earlier):
    mark = earlier[(0,) * earlier.ndim]
    return jnp.where(mark == mark, value, jnp.zeros_like(value))


def swapped(value, mask):
    size = lax.axis_size("tok")
    return lax.ppermute(value, "tok", [(source, source ^ mask) for source in range(size)])


def gather_members(value, bits):
    pieces = [value]
    for bit in reversed(range(bits)):
        pieces = pieces + [swapped(piece, 1 << bit) for piece in pieces]
    return pieces


def exchange_members(blocks, member, bits, earlier):
    views = [(blocks, 0)]
    count = blocks.shape[0]
    for bit in reversed(range(bits)):
        count = count // 2
        mine = member >> bit & 1
        sent = [
            after(lax.dynamic_slice_in_dim(array, at + (1 - mine) * count, count, 0), earlier)
            for array, at in views
        ]
        kept = [(array, at + mine * count) for array, at in views]
        views = kept + [(swapped(part, 1 << bit), 0) for part in sent]
    return views


def from_first_member(value, member, group, bits):
    value = jnp.where(member == 0, value, jnp.zeros_like(value))
    for bit in reversed(range(bits)):
        mask = 1 << bit
        pairs = [
            (source, source + mask)
            for source in range(lax.axis_size("tok"))
            if source % group % (2 * mask) == 0
        ]
        value = value + lax.ppermute(value, "tok", pairs)
    return value


def up_columns(value, column, toks):
    facs = lax.axis_size("fac")
    total = jnp.where(column == 0, value, jnp.zeros_like(value))
    moving = total
    for place in range(facs - 1):
        pairs = [(tok * facs + place, tok * facs + place + 1) for tok in toks]
        moving = lax.ppermute(moving, ("tok", "fac"), pairs)
        total = total + moving
    return total


def local(grad_rows, routes, counts, factor_old, damping, weight_grad):
    toks = lax.axis_size("tok")
    group = toks // 2
    bits = group.bit_length() - 1
    position = lax.axis_index("tok")
    expert = position // group
    member = position % group
    column = lax.axis_index("fac")
    tok_rows, width = grad_rows.shape
    damp = jnp.where(expert == 0, damping[0], damping[1])

    corner = up_columns(factor_old[:LEAD, :LEAD], column, [0, group])
    corner = from_first_member(corner, member, group, bits)
    first_cols = up_columns(factor_old[:, :LEAD].astype(BF16), column, range(toks))
    near_factor = from_first_member(factor_old[:LEAD].astype(BF16), member, group, bits)

    live = jnp.arange(tok_rows) < counts[0]
    named = routes[:, 0]
    own = live & (named == expert)
    away = live & (named != expert)
    flags = jnp.stack([own, away])
    ranks = jnp.cumsum(flags.astype(jnp.int32), 1) - 1
    picker = (ranks[:, None, :] == jnp.arange(CAP)[None, :, None]) & flags[:, None, :]
    packed = jnp.dot(
        picker.reshape(2 * CAP, tok_rows).astype(BF16), grad_rows, preferred_element_type=F32
    ).astype(BF16)
    tally = jnp.sum(flags.astype(F32), 1)
    tally = jnp.broadcast_to(tally[:, None], (2, 128))
    other = swapped(tally, group)
    total = tally[0] + other[1]
    for bit in range(bits):
        total = total + swapped(total, 1 << bit)
    scalars = jnp.stack([(1.0 - DECAY) / total[0], damp])

    ends = [LEAD, width - ROWS, width] if width > LEAD + ROWS else [LEAD, width]
    chunks = list(zip([0, *ends], ends))
    spread, parts = [], []
    for begin, end in chunks:
        sent = packed[CAP:, begin:end]
        if parts:
            sent = after(sent, incoming)
        incoming = swapped(sent, group)
        part = jnp.concatenate([packed[:CAP, begin:end], incoming], 0)
        parts.append(part)
        if spread:
            part = after(part, spread[-1])
        spread.append(lax.all_gather(part, "fac"))
    across = gather_members(jnp.concatenate(parts, 1), bits)
    lead = gather_members(after(spread[0][0], across[1]), bits)
    near_grad = from_first_member(after(weight_grad[:LEAD], lead[1]), member, group, bits)

    upper, inverse = factor_lead(scalars, corner, lead)
    panel = panel_columns(scalars, inverse, near_factor, lead, across)
    solved = jnp.dot(inverse, near_grad.astype(F32), precision=lax.Precision.HIGH)
    high = solved.astype(BF16)
    low = (solved - high.astype(F32)).astype(BF16)

    results = ()
    gates = [lead[1], inverse, panel]
    for (begin, _), part, gate in zip(chunks, spread, gates):
        views = exchange_members(part, member, bits, gate)
        places = jnp.stack([member, column, member * width + begin] + [at for _, at in views])
        results = finish_rows(
            begin,
            places.astype(jnp.int32),
            scalars,
            factor_old,
            first_cols,
            weight_grad,
            panel,
            inverse,
            upper.T,
            high,
            low,
            [array for array, _ in views],
            lead,
            across,
            results,
        )
    return results


def solution(mesh):
    placed = (P("tok", "fac"), P("tok", None), P("tok"), P("tok", "fac"), P(), P("tok", "fac"))
    return jax.shard_map(
        local,
        mesh=mesh,
        in_specs=placed,
        out_specs=(P("tok", "fac"), P("tok", "fac"), P("tok", "fac")),
        check_vma=False,
    )
```

```python
import jax
import jax.numpy as jnp
from jax import lax
from jax.experimental import pallas as pl
from jax.experimental.pallas import tpu as pltpu
from jax.sharding import PartitionSpec as P

CAP = 320
LEAD = 512
TILE = 128
GROUP = 8
ROWS = 256
COLS = 512
PLACES = 3
DECAY = 0.8

HIGHEST = lax.Precision.HIGHEST
BF16 = jnp.bfloat16
F32 = jnp.float32


def dot_t(left, right, precision=None):
    return lax.dot_general(
        left, right, (((0,), (0,)), ((), ())), precision=precision, preferred_element_type=F32
    )


def splat(rows, lane):
    return jnp.broadcast_to(rows[:, lane : lane + 1], rows.shape)


def eliminate_tile(rows):
    lanes = lax.broadcasted_iota(jnp.int32, (GROUP, TILE), 1)
    subs = lax.broadcasted_iota(jnp.int32, (GROUP, TILE), 0)
    upper, inverse = [], []
    for step in range(TILE // GROUP):
        base = step * GROUP
        inside = (lanes >= base) & (lanes < base + GROUP)
        block = rows[step]
        first = [jnp.broadcast_to(block[t : t + 1, :], (GROUP, TILE)) for t in range(GROUP)]
        second = [
            jnp.where(inside, jnp.where(lanes == base + t, 1.0, 0.0), first[t])
            for t in range(GROUP)
        ]
        pivot = [
            [splat(first[t], base + u) if u >= t else None for u in range(GROUP)]
            for t in range(GROUP)
        ]
        scale = [None] * GROUP
        for t in range(GROUP):
            scale[t] = lax.rsqrt(pivot[t][t])
            for u in range(t + 1, GROUP):
                pivot[t][u] = pivot[t][u] * scale[t]
            for u in range(t + 1, GROUP):
                for w in range(u, GROUP):
                    pivot[u][w] = pivot[u][w] - pivot[t][u] * pivot[t][w]
            first[t] = first[t] * scale[t]
            second[t] = second[t] * scale[t]
            for u in range(t + 1, GROUP):
                first[u] = first[u] - pivot[t][u] * first[t]
                second[u] = second[u] - pivot[t][u] * second[t]
        solved = [None] * GROUP
        for t in reversed(range(GROUP)):
            value = second[t]
            for u in range(t + 1, GROUP):
                value = value - pivot[t][u] * solved[u]
            solved[t] = value * scale[t]
        for later in range(step + 1, TILE // GROUP):
            value = jnp.where(inside, 0.0, rows[later])
            for t in range(GROUP):
                value = value - splat(rows[later], base + t) * solved[t]
            rows[later] = value
        upper_rows, inverse_rows = first[0], second[0]
        for t in range(1, GROUP):
            upper_rows = jnp.where(subs == t, first[t], upper_rows)
            inverse_rows = jnp.where(subs == t, second[t], inverse_rows)
        upper.append(upper_rows)
        inverse.append(inverse_rows)
    return upper, inverse


def factor_kernel(count, places_ref, damp_ref, exact_ref, *refs):
    lead_refs = refs[:count]
    upper_ref, inverse_ref, share_ref, work_ref = refs[-4:]
    steps = LEAD // TILE
    side = LEAD // count
    marks = sum(lead[2 * CAP + side :, :].astype(F32) for lead in lead_refs)
    row = lax.broadcasted_iota(jnp.int32, marks.shape, 0)
    weight = jnp.where(row < 4, jnp.where(row % 2 == 0, 256.0, 1.0), 0.0)
    total = jnp.sum(marks * weight, axis=0, keepdims=True)[:, :1]
    share = (1.0 - DECAY) / total
    share_ref[...] = jnp.broadcast_to(share, share_ref.shape)
    for q, lead in enumerate(lead_refs):
        begin = pl.multiple_of(places_ref[PLACES + q] * side, side)
        work_ref[pl.ds(begin, side), :] = lead[2 * CAP : 2 * CAP + side, :].astype(F32)

    @pl.when((places_ref[0] == 0) & (places_ref[1] == 0))
    def _():
        work_ref[...] = exact_ref[...]

    gram = sum(dot_t(lead[: 2 * CAP, :], lead[: 2 * CAP, :]) for lead in lead_refs)
    rows = lax.broadcasted_iota(jnp.int32, (LEAD, LEAD), 0)
    cols = lax.broadcasted_iota(jnp.int32, (LEAD, LEAD), 1)
    work_ref[...] = (
        DECAY * work_ref[...] + share * gram + jnp.where(rows == cols, damp_ref[0], 0.0)
    )
    upper_ref[...] = jnp.zeros_like(upper_ref)
    inverse_ref[...] = jnp.zeros_like(inverse_ref)
    lanes = lax.broadcasted_iota(jnp.int32, (GROUP, TILE), 1)
    subs = lax.broadcasted_iota(jnp.int32, (GROUP, TILE), 0)

    def tile_step(k, carry):
        begin = pl.multiple_of(k * TILE, TILE)
        rows = [
            work_ref[pl.ds(begin + g * GROUP, GROUP), pl.ds(begin, TILE)]
            for g in range(TILE // GROUP)
        ]
        upper, inverse = eliminate_tile(rows)
        upper_tile = jnp.concatenate(
            [jnp.where(lanes >= subs + g * GROUP, part, 0.0) for g, part in enumerate(upper)], 0
        )
        inverse_tile = jnp.concatenate(
            [jnp.where(lanes <= subs + g * GROUP, part, 0.0) for g, part in enumerate(inverse)], 0
        )
        band = jnp.dot(
            inverse_tile,
            work_ref[pl.ds(begin, TILE), :],
            precision=HIGHEST,
            preferred_element_type=F32,
        )
        work_ref[pl.ds(begin, TILE), :] = band
        work_ref[pl.ds(begin, TILE), pl.ds(begin, TILE)] = inverse_tile
        upper_ref[pl.ds(begin, TILE), pl.ds(begin, TILE)] = upper_tile
        inverse_ref[pl.ds(begin, TILE), pl.ds(begin, TILE)] = inverse_tile
        for other in range(steps):

            @pl.when(other < k)
            def _():
                inverse_ref[pl.ds(begin, TILE), other * TILE : (other + 1) * TILE] = work_ref[
                    pl.ds(begin, TILE), other * TILE : (other + 1) * TILE
                ]

            @pl.when(other > k)
            def _():
                span = slice(other * TILE, (other + 1) * TILE)
                part = work_ref[pl.ds(begin, TILE), span]
                upper_ref[pl.ds(begin, TILE), span] = part
                work_ref[span, pl.ds(begin, TILE)] = jnp.zeros((TILE, TILE), F32)
                work_ref[span, :] = work_ref[span, :] - dot_t(
                    part, work_ref[pl.ds(begin, TILE), :], HIGHEST
                )

        return carry

    lax.fori_loop(0, steps, tile_step, 0)


def factor_lead(places, damp, exact, lead, earlier):
    shape = jax.ShapeDtypeStruct((LEAD, LEAD), F32)
    vmem = pl.BlockSpec(memory_space=pltpu.VMEM)
    smem = pl.BlockSpec(memory_space=pltpu.SMEM)
    return pl.pallas_call(
        lambda *refs: factor_kernel(len(lead), *refs),
        out_shape=(shape, shape, jax.ShapeDtypeStruct((GROUP, TILE), F32)),
        in_specs=[smem, smem]
        + [vmem] * (1 + len(lead))
        + [pl.BlockSpec(memory_space=pl.ANY)] * len(earlier),
        out_specs=(vmem, vmem, vmem),
        scratch_shapes=[pltpu.VMEM((LEAD, LEAD), F32)],
        compiler_params=pltpu.CompilerParams(vmem_limit_bytes=32 * 1024 * 1024),
        cost_estimate=pl.CostEstimate(
            flops=25_000_000_000, bytes_accessed=6 * LEAD * LEAD * 4, transcendentals=LEAD
        ),
    )(places, damp, exact, *lead, *earlier)


def panel_kernel(count, places_ref, share_ref, inverse_ref, *refs):
    lead, across = refs[:count], refs[count : 2 * count]
    out_ref, lead_ref, across_ref, near_ref = refs[-4:]
    side = LEAD // count
    depth = 2 * CAP
    for q in range(count):
        span = slice(q * depth, (q + 1) * depth)
        across_ref[span, :] = across[q][:depth, :]
        begin = pl.multiple_of(places_ref[PLACES + q] * side, side)
        near_ref[pl.ds(begin, side), :] = across[q][depth : depth + side, :].astype(F32)

    @pl.when(pl.program_id(0) == 0)
    def _():
        for q in range(count):
            lead_ref[q * depth : (q + 1) * depth, :] = lead[q][:depth, :]

    gram = dot_t(lead_ref[...], across_ref[...])
    beside = DECAY * near_ref[...] + share_ref[:1, :1] * gram
    out_ref[...] = jnp.dot(
        inverse_ref[...], beside, precision=HIGHEST, preferred_element_type=F32
    ).astype(BF16)


def panel_columns(places, share, inverse, lead, across, earlier):
    count = len(lead)
    width = across[0].shape[1]
    cols = COLS if width % COLS == 0 else ROWS
    tall = 2 * CAP * count
    whole = lambda height: pl.BlockSpec((height, LEAD), lambda j: (0, 0))
    tiled = lambda height: pl.BlockSpec((height, cols), lambda j: (0, j))
    return pl.pallas_call(
        lambda *refs: panel_kernel(count, *refs),
        grid=(width // cols,),
        out_shape=(
            jax.ShapeDtypeStruct((LEAD, width), BF16),
            jax.ShapeDtypeStruct((tall, LEAD), BF16),
            jax.ShapeDtypeStruct((tall, width), BF16),
        ),
        in_specs=[
            pl.BlockSpec(memory_space=pltpu.SMEM),
            pl.BlockSpec((GROUP, TILE), lambda j: (0, 0)),
            whole(LEAD),
        ]
        + [whole(lead[0].shape[0])] * count
        + [tiled(across[0].shape[0])] * count
        + [pl.BlockSpec(memory_space=pl.ANY)] * len(earlier),
        out_specs=(tiled(LEAD), whole(tall), tiled(tall)),
        scratch_shapes=[pltpu.VMEM((LEAD, cols), F32)],
        compiler_params=pltpu.CompilerParams(vmem_limit_bytes=56 * 1024 * 1024),
        cost_estimate=pl.CostEstimate(
            flops=2 * width * LEAD * (tall + 6 * LEAD),
            bytes_accessed=4 * tall * (width + LEAD) + 4 * LEAD * width,
            transcendentals=0,
        ),
    )(places, share, inverse, *lead, *across, *earlier)


def finish_kernel(
    count,
    gram_steps,
    first_chunk,
    aliased,
    places_ref,
    damp_ref,
    share_ref,
    factor_ref,
    grad_ref,
    panel_ref,
    inverse_ref,
    high_ref,
    low_ref,
    lead_ref,
    across_ref,
    *refs,
):
    if first_chunk:
        lower_ref, *refs = refs
    mine = refs[:count]
    outs = refs[count + aliased :]
    running_ref, factored_ref, precond_ref, token_ref, mine_ref, rows_ref, first_ref = outs
    j, i = pl.program_id(0), pl.program_id(1)
    member, column, base = places_ref[0], places_ref[1], places_ref[2]
    share, damp = share_ref[:1, :1], damp_ref[0]
    height = ROWS
    depth = 2 * CAP
    side = LEAD // count
    cols = running_ref.shape[1]
    span = pl.ds(pl.multiple_of(i * height, height), height)
    head = (member == 0) & first_chunk

    @pl.when(j == 0)
    def _():
        token_ref[...] = jnp.zeros_like(token_ref)
        for q in range(count):
            mine_ref[span, q * depth : (q + 1) * depth] = mine[q][0, :depth, :].T
            begin = pl.multiple_of(places_ref[PLACES + q] * side, side)
            first_ref[pl.ds(begin, side), :] = mine[q][0, depth : depth + side, :].astype(F32)
        source = first_ref[...].T
        if cols == LEAD:
            source = jnp.where(column == 0, factor_ref[...], source)
        gram = jnp.dot(mine_ref[span, :], lead_ref[...], preferred_element_type=F32)
        row = base + i * height + lax.broadcasted_iota(jnp.int32, (height, LEAD), 0)
        col = lax.broadcasted_iota(jnp.int32, (height, LEAD), 1)
        source = DECAY * source + share * gram
        source = source + jnp.where(row == col, damp, 0.0)
        rows_ref[span, :] = lax.dot_general(
            source,
            inverse_ref[...],
            (((1,), (1,)), ((), ())),
            precision=HIGHEST,
            preferred_element_type=F32,
        )

    panel = rows_ref[span, :].astype(BF16)

    @pl.when(j < gram_steps)
    def _():
        gram = jnp.dot(mine_ref[span, :], across_ref[...], preferred_element_type=F32)
        running = DECAY * factor_ref[...] + share * gram
        running_ref[...] = running
        row = base + i * height + lax.broadcasted_iota(jnp.int32, (height, cols), 0)
        col = (column * gram_steps + j) * cols + lax.broadcasted_iota(jnp.int32, (height, cols), 1)
        matrix = running + jnp.where(row == col, damp, 0.0)
        factored = matrix - jnp.dot(panel, panel_ref[...], preferred_element_type=F32)
        factored_ref[...] = jnp.where(head, 0.0, factored)

        for part in range(LEAD // cols):
            edge = slice(part * cols, (part + 1) * cols)

            @pl.when((column == 0) & (j == part))
            def _():
                factored_ref[...] = rows_ref[span, edge]

                if first_chunk:

                    @pl.when(head)
                    def _():
                        factored_ref[...] = lower_ref[span, edge]

    high, low = high_ref[...], low_ref[...]
    product = jnp.dot(panel, high, preferred_element_type=F32)
    product = product + jnp.dot(panel, low, preferred_element_type=F32)
    precond_ref[...] = grad_ref[...].astype(F32) - product

    if first_chunk:

        @pl.when(head)
        def _():
            precond_ref[...] = high_ref[span, :].astype(F32) + low_ref[span, :].astype(F32)


def finish_rows(
    begin, places, damp, share, factor, grad, panel, inverse, lower, high, low,
    lead, across, mine, earlier,
):
    count = len(mine)
    deep, rows = mine[0].shape[1:]
    width, grad_cols = factor.shape[0], grad.shape[1]
    tall = lead.shape[0]
    tiles = rows // ROWS
    start = begin // ROWS
    cols = COLS if width % COLS == 0 else ROWS
    gram_steps, steps = width // cols, grad_cols // cols
    assert steps >= gram_steps and rows % ROWS == 0

    def mine_spec(q):
        return pl.BlockSpec(
            (1, deep, ROWS),
            lambda j, i, p: (p[PLACES + count + q], 0, jnp.where(j == 0, i, tiles - 1)),
        )

    def gram_col(j):
        return jnp.minimum(j, gram_steps - 1)

    def gram_tile(j, i, p):
        return (start + jnp.where(j < gram_steps, i, tiles - 1), gram_col(j))

    grad_spec = pl.BlockSpec((ROWS, cols), lambda j, i, p: (start + i, j))
    factor_spec = pl.BlockSpec((ROWS, cols), gram_tile)
    lead_whole = pl.BlockSpec((LEAD, LEAD), lambda j, i, p: (0, 0))
    small = pl.BlockSpec((GROUP, TILE), lambda j, i, p: (0, 0))
    in_specs = [
        pl.BlockSpec(memory_space=pltpu.SMEM),
        small,
        factor_spec,
        grad_spec,
        pl.BlockSpec((LEAD, cols), lambda j, i, p: (0, gram_col(j))),
        lead_whole,
        pl.BlockSpec((LEAD, cols), lambda j, i, p: (0, j)),
        pl.BlockSpec((LEAD, cols), lambda j, i, p: (0, j)),
        pl.BlockSpec((tall, LEAD), lambda j, i, p: (0, 0)),
        pl.BlockSpec((tall, cols), lambda j, i, p: (0, gram_col(j))),
    ]
    operands = [damp, share, factor, grad, panel, inverse, high, low, lead, across]
    if begin == 0:
        in_specs += [lead_whole]
        operands += [lower]
    in_specs += [mine_spec(q) for q in range(count)]
    operands += mine
    in_specs += [pl.BlockSpec(memory_space=pl.ANY)] * len(earlier)
    aliases = {1 + len(operands) + k: k for k in range(len(earlier))}
    operands += earlier
    return pl.pallas_call(
        lambda *refs: finish_kernel(count, gram_steps, begin == 0, len(earlier), *refs),
        grid_spec=pltpu.PrefetchScalarGridSpec(
            num_scalar_prefetch=1,
            grid=(steps, tiles),
            in_specs=in_specs,
            out_specs=(factor_spec, factor_spec, grad_spec, small),
            scratch_shapes=[
                pltpu.VMEM((rows, tall), BF16),
                pltpu.VMEM((rows, LEAD), F32),
                pltpu.VMEM((LEAD, ROWS), F32),
            ],
        ),
        out_shape=(
            jax.ShapeDtypeStruct(factor.shape, F32),
            jax.ShapeDtypeStruct(factor.shape, F32),
            jax.ShapeDtypeStruct(grad.shape, F32),
            jax.ShapeDtypeStruct((GROUP, TILE), F32),
        ),
        input_output_aliases=aliases,
        compiler_params=pltpu.CompilerParams(vmem_limit_bytes=56 * 1024 * 1024),
        cost_estimate=pl.CostEstimate(
            flops=2 * rows * (tall * (width + LEAD) + LEAD * (6 * LEAD + width + 2 * grad_cols)),
            bytes_accessed=2 * tall * (width + LEAD + rows)
            + rows * (12 * width + 6 * grad_cols)
            + LEAD * (4 * grad_cols + 8 * LEAD + 2 * width),
            transcendentals=0,
        ),
    )(places, *operands)


def after(value, earlier):
    mark = earlier[(0,) * earlier.ndim]
    return jnp.where(mark == mark, value, jnp.zeros_like(value))


def swapped(value, mask):
    size = lax.axis_size("tok")
    return lax.ppermute(value, "tok", [(source, source ^ mask) for source in range(size)])


def gather_members(value, bits):
    pieces = [value]
    for bit in reversed(range(bits)):
        pieces = pieces + [swapped(piece, 1 << bit) for piece in pieces]
    return pieces


def exchange_members(blocks, member, bits, earlier):
    views = [(blocks, 0)]
    count = blocks.shape[0]
    for bit in reversed(range(bits)):
        count = count // 2
        mine = member >> bit & 1
        sent = [
            after(lax.dynamic_slice_in_dim(array, at + (1 - mine) * count, count, 0), earlier)
            for array, at in views
        ]
        kept = [(array, at + mine * count) for array, at in views]
        views = kept + [(swapped(part, 1 << bit), 0) for part in sent]
    return views


def member_order(bits):
    order = [0]
    for bit in reversed(range(bits)):
        order = order + [other ^ (1 << bit) for other in order]
    return order


def down_pairs(bit, group):
    mask = 1 << bit
    return [
        (source, source + mask)
        for source in range(lax.axis_size("tok"))
        if source % group % (2 * mask) == 0
    ]


def from_first_member(value, member, group, bits):
    value = jnp.where(member == 0, value, jnp.zeros_like(value))
    for bit in reversed(range(bits)):
        value = value + lax.ppermute(value, "tok", down_pairs(bit, group))
    return value


def share_of_first(blocks, member, group, bits):
    for bit in reversed(range(bits)):
        half = blocks.shape[0] // 2
        moved = lax.ppermute(blocks[half:], "tok", down_pairs(bit, group))
        blocks = jnp.where(member >> bit & 1 == 1, moved, blocks[:half])
    return blocks[0]


def count_rows(number, row, width):
    index = lax.broadcasted_iota(jnp.int32, (16, width), 0)
    rest = jnp.where(index == row + 1, number % 256, 0)
    return jnp.where(index == row, number // 256, rest).astype(BF16)


def local(grad_rows, routes, counts, factor_old, damping, weight_grad):
    group = lax.axis_size("tok") // 2
    bits = group.bit_length() - 1
    position = lax.axis_index("tok")
    expert = position // group
    member = position % group
    column = lax.axis_index("fac")
    tok_rows, width = grad_rows.shape
    damp = jnp.where(expert == 0, damping[0], damping[1])[None]
    order = [member ^ other for other in member_order(bits)]

    lead_factor = factor_old[:LEAD].astype(BF16).reshape(group, LEAD // group, width)
    lead_factor = share_of_first(lead_factor, member, group, bits)

    live = jnp.arange(tok_rows) < counts[0]
    named = routes[:, 0]
    own = live & (named == expert)
    away = live & (named != expert)
    flags = jnp.stack([own, away])
    ranks = jnp.cumsum(flags.astype(jnp.int32), 1) - 1
    picker = (ranks[:, None, :] == jnp.arange(CAP)[None, :, None]) & flags[:, None, :]
    packed = jnp.dot(
        picker.reshape(2 * CAP, tok_rows).astype(BF16), grad_rows, preferred_element_type=F32
    ).astype(BF16)
    tally = jnp.sum(flags.astype(jnp.int32), 1)
    front = swapped(
        jnp.concatenate([packed[CAP:, :LEAD], count_rows(tally[1], 2, LEAD)], 0), group
    )
    first_part = jnp.concatenate(
        [
            packed[:CAP, :LEAD],
            front[:CAP],
            lead_factor[:, :LEAD],
            front[CAP:] + count_rows(tally[0], 0, LEAD),
        ],
        0,
    )
    incoming = swapped(after(packed[CAP:], front), group)
    quarter = jnp.concatenate([packed[:CAP], incoming, lead_factor], 0)

    ends = [end for end in (LEAD, 2 * LEAD, 2 * LEAD + ROWS) if end < width] + [width]
    chunks = list(zip([0, *ends], ends))
    spread = [lax.all_gather(first_part, "fac")]
    across = gather_members(quarter, bits)
    lead = gather_members(after(spread[0][0], across[1]), bits)
    near_grad = from_first_member(after(weight_grad[:LEAD], lead[1]), member, group, bits)

    places = [member, column, member * width]
    assert len(places) == PLACES
    slots = jnp.stack(places + order).astype(jnp.int32)
    parts = [first_part]
    for (begin, end), gate in zip(chunks[1:], [spread[0], lead[1], lead[1]]):
        parts.append(after(quarter[:, begin:end], gate))
        spread.append(lax.all_gather(parts[-1], "fac"))
    upper, inverse, share = factor_lead(
        slots, damp, factor_old[:LEAD, :LEAD], lead, parts[1:3]
    )
    panel, lead_stack, across_stack = panel_columns(
        slots, share, inverse, lead, across, parts[3:]
    )
    solved = jnp.dot(inverse, near_grad.astype(F32), precision=lax.Precision.HIGH)
    high = solved.astype(BF16)
    low = (solved - high.astype(F32)).astype(BF16)
    lower = upper.T

    results = ()
    gates = [lead[1], panel]
    for (begin, end), part in zip(chunks, spread):
        views = exchange_members(part, member, bits, gates.pop(0))
        places[2] = member * width + begin
        slots = jnp.stack(places + order + [jnp.int32(at) for _, at in views])
        *results, token = finish_rows(
            begin,
            slots.astype(jnp.int32),
            damp,
            share,
            factor_old,
            weight_grad,
            panel,
            inverse,
            lower,
            high,
            low,
            lead_stack,
            across_stack,
            [array for array, _ in views],
            list(results),
        )
        gates.append(token)
    return tuple(results)


def solution(mesh):
    placed = (P("tok", "fac"), P("tok", None), P("tok"), P("tok", "fac"), P(), P("tok", "fac"))
    return jax.shard_map(
        local,
        mesh=mesh,
        in_specs=placed,
        out_specs=(P("tok", "fac"), P("tok", "fac"), P("tok", "fac")),
        check_vma=False,
    )
```

```python
import jax
import jax.numpy as jnp
from jax import lax
from jax.experimental import pallas as pl
from jax.experimental.pallas import tpu as pltpu
from jax.sharding import PartitionSpec as P

CAP = 320
LEAD = 512
TILE = 128
GROUP = 8
ROWS = 256
COLS = 512
PLACES = 3
NO_COST = pl.CostEstimate(flops=1, bytes_accessed=1, transcendentals=0)
DECAY = 0.8

HIGHEST = lax.Precision.HIGHEST
BF16 = jnp.bfloat16
F32 = jnp.float32


def dot_t(left, right, precision=None):
    return lax.dot_general(
        left, right, (((0,), (0,)), ((), ())), precision=precision, preferred_element_type=F32
    )


def splat(rows, lane):
    return jnp.broadcast_to(rows[:, lane : lane + 1], rows.shape)


def eliminate_tile(rows):
    lanes = lax.broadcasted_iota(jnp.int32, (GROUP, TILE), 1)
    subs = lax.broadcasted_iota(jnp.int32, (GROUP, TILE), 0)
    upper, inverse = [], []
    for step in range(TILE // GROUP):
        base = step * GROUP
        inside = (lanes >= base) & (lanes < base + GROUP)
        block = rows[step]
        first = [jnp.broadcast_to(block[t : t + 1, :], (GROUP, TILE)) for t in range(GROUP)]
        second = [
            jnp.where(inside, jnp.where(lanes == base + t, 1.0, 0.0), first[t])
            for t in range(GROUP)
        ]
        pivot = [
            [splat(first[t], base + u) if u >= t else None for u in range(GROUP)]
            for t in range(GROUP)
        ]
        scale = [None] * GROUP
        for t in range(GROUP):
            scale[t] = lax.rsqrt(pivot[t][t])
            for u in range(t + 1, GROUP):
                pivot[t][u] = pivot[t][u] * scale[t]
            for u in range(t + 1, GROUP):
                for w in range(u, GROUP):
                    pivot[u][w] = pivot[u][w] - pivot[t][u] * pivot[t][w]
            first[t] = first[t] * scale[t]
            second[t] = second[t] * scale[t]
            for u in range(t + 1, GROUP):
                first[u] = first[u] - pivot[t][u] * first[t]
                second[u] = second[u] - pivot[t][u] * second[t]
        solved = [None] * GROUP
        for t in reversed(range(GROUP)):
            value = second[t]
            for u in range(t + 1, GROUP):
                value = value - pivot[t][u] * solved[u]
            solved[t] = value * scale[t]
        for later in range(step + 1, TILE // GROUP):
            value = jnp.where(inside, 0.0, rows[later])
            for t in range(GROUP):
                value = value - splat(rows[later], base + t) * solved[t]
            rows[later] = value
        upper_rows, inverse_rows = first[0], second[0]
        for t in range(1, GROUP):
            upper_rows = jnp.where(subs == t, first[t], upper_rows)
            inverse_rows = jnp.where(subs == t, second[t], inverse_rows)
        upper.append(upper_rows)
        inverse.append(inverse_rows)
    return upper, inverse


def factor_kernel(count, places_ref, damp_ref, exact_ref, *refs):
    lead_refs = refs[:count]
    upper_ref, inverse_ref, share_ref, work_ref = refs[-4:]
    steps = LEAD // TILE
    side = LEAD // count
    marks = sum(lead[2 * CAP + side :, :].astype(F32) for lead in lead_refs)
    row = lax.broadcasted_iota(jnp.int32, marks.shape, 0)
    weight = jnp.where(row < 4, jnp.where(row % 2 == 0, 256.0, 1.0), 0.0)
    total = jnp.sum(marks * weight, axis=0, keepdims=True)[:, :1]
    share = (1.0 - DECAY) / total
    share_ref[...] = jnp.broadcast_to(share, share_ref.shape)
    for q, lead in enumerate(lead_refs):
        begin = pl.multiple_of(places_ref[PLACES + q] * side, side)
        work_ref[pl.ds(begin, side), :] = lead[2 * CAP : 2 * CAP + side, :].astype(F32)

    @pl.when((places_ref[0] == 0) & (places_ref[1] == 0))
    def _():
        work_ref[...] = exact_ref[...]

    gram = sum(dot_t(lead[: 2 * CAP, :], lead[: 2 * CAP, :]) for lead in lead_refs)
    rows = lax.broadcasted_iota(jnp.int32, (LEAD, LEAD), 0)
    cols = lax.broadcasted_iota(jnp.int32, (LEAD, LEAD), 1)
    work_ref[...] = (
        DECAY * work_ref[...] + share * gram + jnp.where(rows == cols, damp_ref[0], 0.0)
    )
    upper_ref[...] = jnp.zeros_like(upper_ref)
    inverse_ref[...] = jnp.zeros_like(inverse_ref)
    lanes = lax.broadcasted_iota(jnp.int32, (GROUP, TILE), 1)
    subs = lax.broadcasted_iota(jnp.int32, (GROUP, TILE), 0)

    def tile_step(k, carry):
        begin = pl.multiple_of(k * TILE, TILE)
        rows = [
            work_ref[pl.ds(begin + g * GROUP, GROUP), pl.ds(begin, TILE)]
            for g in range(TILE // GROUP)
        ]
        upper, inverse = eliminate_tile(rows)
        upper_tile = jnp.concatenate(
            [jnp.where(lanes >= subs + g * GROUP, part, 0.0) for g, part in enumerate(upper)], 0
        )
        inverse_tile = jnp.concatenate(
            [jnp.where(lanes <= subs + g * GROUP, part, 0.0) for g, part in enumerate(inverse)], 0
        )
        band = jnp.dot(
            inverse_tile,
            work_ref[pl.ds(begin, TILE), :],
            precision=HIGHEST,
            preferred_element_type=F32,
        )
        work_ref[pl.ds(begin, TILE), :] = band
        work_ref[pl.ds(begin, TILE), pl.ds(begin, TILE)] = inverse_tile
        upper_ref[pl.ds(begin, TILE), pl.ds(begin, TILE)] = upper_tile
        inverse_ref[pl.ds(begin, TILE), pl.ds(begin, TILE)] = inverse_tile
        for other in range(steps):

            @pl.when(other < k)
            def _():
                inverse_ref[pl.ds(begin, TILE), other * TILE : (other + 1) * TILE] = work_ref[
                    pl.ds(begin, TILE), other * TILE : (other + 1) * TILE
                ]

            @pl.when(other > k)
            def _():
                span = slice(other * TILE, (other + 1) * TILE)
                part = work_ref[pl.ds(begin, TILE), span]
                upper_ref[pl.ds(begin, TILE), span] = part
                work_ref[span, pl.ds(begin, TILE)] = jnp.zeros((TILE, TILE), F32)
                work_ref[span, :] = work_ref[span, :] - dot_t(
                    part, work_ref[pl.ds(begin, TILE), :], HIGHEST
                )

        return carry

    lax.fori_loop(0, steps, tile_step, 0)


def factor_lead(places, damp, exact, lead):
    shape = jax.ShapeDtypeStruct((LEAD, LEAD), F32)
    vmem = pl.BlockSpec(memory_space=pltpu.VMEM)
    smem = pl.BlockSpec(memory_space=pltpu.SMEM)
    return pl.pallas_call(
        lambda *refs: factor_kernel(len(lead), *refs),
        out_shape=(shape, shape, jax.ShapeDtypeStruct((GROUP, TILE), F32)),
        in_specs=[smem, smem] + [vmem] * (1 + len(lead)),
        out_specs=(vmem, vmem, vmem),
        scratch_shapes=[pltpu.VMEM((LEAD, LEAD), F32)],
        compiler_params=pltpu.CompilerParams(vmem_limit_bytes=32 * 1024 * 1024),
        cost_estimate=NO_COST,
    )(places, damp, exact, *lead)


def panel_kernel(count, places_ref, share_ref, inverse_ref, *refs):
    lead, own, other = refs[:count], refs[count : 2 * count], refs[2 * count : 3 * count]
    out_ref, lead_ref, across_ref, near_ref = refs[-4:]
    side = LEAD // count
    depth = 2 * CAP
    for q in range(count):
        across_ref[q * depth : q * depth + CAP, :] = own[q][:CAP, :]
        across_ref[q * depth + CAP : (q + 1) * depth, :] = other[q][...]
        begin = pl.multiple_of(places_ref[PLACES + q] * side, side)
        near_ref[pl.ds(begin, side), :] = own[q][CAP:, :].astype(F32)

    @pl.when(pl.program_id(0) == 0)
    def _():
        for q in range(count):
            lead_ref[q * depth : (q + 1) * depth, :] = lead[q][:depth, :]

    gram = dot_t(lead_ref[...], across_ref[...])
    beside = DECAY * near_ref[...] + share_ref[:1, :1] * gram
    out_ref[...] = jnp.dot(
        inverse_ref[...], beside, precision=HIGHEST, preferred_element_type=F32
    ).astype(BF16)


def panel_columns(places, share, inverse, lead, own, other):
    count = len(lead)
    width = own[0].shape[1]
    cols = COLS if width % COLS == 0 else ROWS
    tall = 2 * CAP * count
    whole = lambda height: pl.BlockSpec((height, LEAD), lambda j: (0, 0))
    tiled = lambda height: pl.BlockSpec((height, cols), lambda j: (0, j))
    return pl.pallas_call(
        lambda *refs: panel_kernel(count, *refs),
        grid=(width // cols,),
        out_shape=(
            jax.ShapeDtypeStruct((LEAD, width), BF16),
            jax.ShapeDtypeStruct((tall, LEAD), BF16),
            jax.ShapeDtypeStruct((tall, width), BF16),
        ),
        in_specs=[
            pl.BlockSpec(memory_space=pltpu.SMEM),
            pl.BlockSpec((GROUP, TILE), lambda j: (0, 0)),
            whole(LEAD),
        ]
        + [whole(lead[0].shape[0])] * count
        + [tiled(own[0].shape[0])] * count
        + [tiled(CAP)] * count,
        out_specs=(tiled(LEAD), whole(tall), tiled(tall)),
        scratch_shapes=[pltpu.VMEM((LEAD, cols), F32)],
        compiler_params=pltpu.CompilerParams(vmem_limit_bytes=56 * 1024 * 1024),
        cost_estimate=NO_COST,
    )(places, share, inverse, *lead, *own, *other)


def finish_kernel(
    count,
    gram_steps,
    first_chunk,
    unread,
    places_ref,
    damp_ref,
    share_ref,
    factor_ref,
    grad_ref,
    panel_ref,
    inverse_ref,
    high_ref,
    low_ref,
    lead_ref,
    across_ref,
    *refs,
):
    if first_chunk:
        lower_ref, *refs = refs
    mine = refs[:count]
    outs = refs[count + unread :]
    running_ref, factored_ref, precond_ref, token_ref, mine_ref, rows_ref, first_ref = outs
    j, i = pl.program_id(0), pl.program_id(1)
    member, column, base = places_ref[0], places_ref[1], places_ref[2]
    share, damp = share_ref[:1, :1], damp_ref[0]
    height, cols = running_ref.shape
    depth = 2 * CAP
    side = LEAD // count
    span = pl.ds(pl.multiple_of(i * height, height), height)
    head = (member == 0) & first_chunk

    @pl.when(j == 0)
    def _():
        token_ref[...] = jnp.zeros_like(token_ref)
        for q in range(count):
            mine_ref[span, q * depth : (q + 1) * depth] = mine[q][0, :depth, :].T
            begin = pl.multiple_of(places_ref[PLACES + q] * side, side)
            first_ref[pl.ds(begin, side), :] = mine[q][0, depth : depth + side, :].astype(F32)
        source = first_ref[...].T
        if cols == LEAD:
            source = jnp.where(column == 0, factor_ref[...], source)
        gram = jnp.dot(mine_ref[span, :], lead_ref[...], preferred_element_type=F32)
        row = base + i * height + lax.broadcasted_iota(jnp.int32, (height, LEAD), 0)
        col = lax.broadcasted_iota(jnp.int32, (height, LEAD), 1)
        source = DECAY * source + share * gram
        source = source + jnp.where(row == col, damp, 0.0)
        rows_ref[span, :] = lax.dot_general(
            source,
            inverse_ref[...],
            (((1,), (1,)), ((), ())),
            precision=HIGHEST,
            preferred_element_type=F32,
        )

    panel = rows_ref[span, :].astype(BF16)

    @pl.when(j < gram_steps)
    def _():
        gram = jnp.dot(mine_ref[span, :], across_ref[...], preferred_element_type=F32)
        running = DECAY * factor_ref[...] + share * gram
        running_ref[...] = running
        row = base + i * height + lax.broadcasted_iota(jnp.int32, (height, cols), 0)
        col = (column * gram_steps + j) * cols + lax.broadcasted_iota(jnp.int32, (height, cols), 1)
        matrix = running + jnp.where(row == col, damp, 0.0)
        factored = matrix - jnp.dot(panel, panel_ref[...], preferred_element_type=F32)
        factored_ref[...] = jnp.where(head, 0.0, factored)

        for part in range(LEAD // cols):
            edge = slice(part * cols, (part + 1) * cols)

            @pl.when((column == 0) & (j == part))
            def _():
                factored_ref[...] = rows_ref[span, edge]

                if first_chunk:

                    @pl.when(head)
                    def _():
                        factored_ref[...] = lower_ref[span, edge]

    high, low = high_ref[...], low_ref[...]
    product = jnp.dot(panel, high, preferred_element_type=F32)
    product = product + jnp.dot(panel, low, preferred_element_type=F32)
    precond_ref[...] = grad_ref[...].astype(F32) - product

    if first_chunk:

        @pl.when(head)
        def _():
            precond_ref[...] = high_ref[span, :].astype(F32) + low_ref[span, :].astype(F32)


def finish_rows(
    begin, places, damp, share, factor, grad, panel, inverse, lower, high, low,
    lead, across, mine, results, earlier,
):
    count = len(mine)
    deep, rows = mine[0].shape[1:]
    width, grad_cols = factor.shape[0], grad.shape[1]
    tall = lead.shape[0]
    height = min(rows, COLS)
    tiles = rows // height
    start = begin // height
    cols = COLS if width % COLS == 0 else ROWS
    gram_steps, steps = width // cols, grad_cols // cols
    assert steps >= gram_steps and rows % height == 0 and begin % height == 0

    def mine_spec(q):
        return pl.BlockSpec(
            (1, deep, height),
            lambda j, i, p: (p[PLACES + count + q], 0, jnp.where(j == 0, i, tiles - 1)),
        )

    def gram_col(j):
        return jnp.minimum(j, gram_steps - 1)

    def gram_tile(j, i, p):
        return (start + jnp.where(j < gram_steps, i, tiles - 1), gram_col(j))

    grad_spec = pl.BlockSpec((height, cols), lambda j, i, p: (start + i, j))
    factor_spec = pl.BlockSpec((height, cols), gram_tile)
    lead_whole = pl.BlockSpec((LEAD, LEAD), lambda j, i, p: (0, 0))
    small = pl.BlockSpec((GROUP, TILE), lambda j, i, p: (0, 0))
    in_specs = [
        pl.BlockSpec(memory_space=pltpu.SMEM),
        small,
        factor_spec,
        grad_spec,
        pl.BlockSpec((LEAD, cols), lambda j, i, p: (0, gram_col(j))),
        lead_whole,
        pl.BlockSpec((LEAD, cols), lambda j, i, p: (0, j)),
        pl.BlockSpec((LEAD, cols), lambda j, i, p: (0, j)),
        pl.BlockSpec((tall, LEAD), lambda j, i, p: (0, 0)),
        pl.BlockSpec((tall, cols), lambda j, i, p: (0, gram_col(j))),
    ]
    operands = [damp, share, factor, grad, panel, inverse, high, low, lead, across]
    if begin == 0:
        in_specs += [lead_whole]
        operands += [lower]
    in_specs += [mine_spec(q) for q in range(count)]
    operands += mine
    aliases = {1 + len(operands) + k: k for k in range(len(results))}
    operands += [*results, *earlier]
    unread = len(results) + len(earlier)
    in_specs += [pl.BlockSpec(memory_space=pl.ANY)] * unread
    return pl.pallas_call(
        lambda *refs: finish_kernel(count, gram_steps, begin == 0, unread, *refs),
        grid_spec=pltpu.PrefetchScalarGridSpec(
            num_scalar_prefetch=1,
            grid=(steps, tiles),
            in_specs=in_specs,
            out_specs=(factor_spec, factor_spec, grad_spec, small),
            scratch_shapes=[
                pltpu.VMEM((rows, tall), BF16),
                pltpu.VMEM((rows, LEAD), F32),
                pltpu.VMEM((LEAD, height), F32),
            ],
        ),
        out_shape=(
            jax.ShapeDtypeStruct(factor.shape, F32),
            jax.ShapeDtypeStruct(factor.shape, F32),
            jax.ShapeDtypeStruct(grad.shape, F32),
            jax.ShapeDtypeStruct((GROUP, TILE), F32),
        ),
        input_output_aliases=aliases,
        compiler_params=pltpu.CompilerParams(vmem_limit_bytes=56 * 1024 * 1024),
        cost_estimate=NO_COST,
    )(places, *operands)


def after(value, earlier):
    mark = earlier[(0,) * earlier.ndim]
    return jnp.where(mark == mark, value, jnp.zeros_like(value))


def swapped(value, mask):
    size = lax.axis_size("tok")
    return lax.ppermute(value, "tok", [(source, source ^ mask) for source in range(size)])


def gather_members(value, bits):
    pieces = [value]
    for bit in reversed(range(bits)):
        pieces = pieces + [swapped(piece, 1 << bit) for piece in pieces]
    return pieces


def copy_kernel(plans, starts_ref, *refs):
    outs, sems = refs[-1 - len(plans) : -1], refs[-1]
    copies = []
    for number, (count, axis, begin) in enumerate(plans):
        source, out = refs[number], outs[number]
        rows = out.shape[-2] // 32 * 16
        for part in (slice(0, rows), slice(rows, out.shape[-2])):
            if axis is None:
                pairs = [
                    (source.at[starts_ref[number] + k, part], out.at[k, part])
                    for k in range(count)
                ]
            else:
                pairs = [(source.at[part, begin : begin + out.shape[1]], out.at[part])]
            copies += [
                pltpu.make_async_copy(before, after, sems.at[len(copies) + k])
                for k, (before, after) in enumerate(pairs)
            ]
    for copy in copies:
        copy.start()
    for copy in copies:
        copy.wait()


def copied(requests, earlier):
    plans, shapes, starts, total = [], [], [], 0
    for array, begin, size in requests:
        if array.ndim == 3:
            plans.append((size, None, None))
            shapes.append((size, *array.shape[1:]))
            starts.append(begin)
            total += 2 * size
        else:
            plans.append((1, 1, begin))
            shapes.append((array.shape[0], size - begin))
            starts.append(0)
            total += 2
    anywhere = pl.BlockSpec(memory_space=pl.ANY)
    arrays = [array for array, _, _ in requests]
    return pl.pallas_call(
        lambda *refs: copy_kernel(plans, *refs),
        in_specs=[pl.BlockSpec(memory_space=pltpu.SMEM)]
        + [anywhere] * (len(arrays) + len(earlier)),
        out_specs=[anywhere] * len(plans),
        out_shape=[jax.ShapeDtypeStruct(shape, BF16) for shape in shapes],
        scratch_shapes=[pltpu.SemaphoreType.DMA((total,))],
        cost_estimate=NO_COST,
    )(jnp.stack([jnp.int32(start) for start in starts]), *arrays, *earlier)


def exchange_members(blocks, member, bits, earlier):
    views = [(blocks, 0)]
    sent = []
    count = blocks.shape[0]
    for bit in reversed(range(bits)):
        count = count // 2
        mine = member >> bit & 1
        sent = copied(
            [(array, at + (1 - mine) * count, count) for array, at in views], earlier
        )
        kept = [(array, at + mine * count) for array, at in views]
        views = kept + [(swapped(part, 1 << bit), 0) for part in sent]
    return views


def member_order(bits):
    order = [0]
    for bit in reversed(range(bits)):
        order = order + [other ^ (1 << bit) for other in order]
    return order


def down_pairs(bit, group):
    mask = 1 << bit
    return [
        (source, source + mask)
        for source in range(lax.axis_size("tok"))
        if source % group % (2 * mask) == 0
    ]


def from_first_member(value, member, group, bits, earlier):
    for bit in reversed(range(bits)):
        if 1 << bit < group // 2:
            value = after(value, earlier)
        moved = lax.ppermute(value, "tok", down_pairs(bit, group))
        value = jnp.where(member >> bit & 1 == 1, moved, value)
    return value


def share_of_first(blocks, member, group, bits):
    for bit in reversed(range(bits)):
        half = blocks.shape[0] // 2
        moved = lax.ppermute(blocks[half:], "tok", down_pairs(bit, group))
        blocks = jnp.where(member >> bit & 1 == 1, moved, blocks[:half])
    return blocks[0]


def count_rows(number, row, width):
    index = lax.broadcasted_iota(jnp.int32, (16, width), 0)
    rest = jnp.where(index == row + 1, number % 256, 0)
    return jnp.where(index == row, number // 256, rest).astype(BF16)


def local(grad_rows, routes, counts, factor_old, damping, weight_grad):
    group = lax.axis_size("tok") // 2
    bits = group.bit_length() - 1
    position = lax.axis_index("tok")
    expert = position // group
    member = position % group
    column = lax.axis_index("fac")
    tok_rows, width = grad_rows.shape
    damp = jnp.where(expert == 0, damping[0], damping[1])[None]
    order = [member ^ other for other in member_order(bits)]

    lead_factor = factor_old[:LEAD].astype(BF16).reshape(group, LEAD // group, width)
    lead_factor = share_of_first(lead_factor, member, group, bits)

    live = jnp.arange(tok_rows) < counts[0]
    named = routes[:, 0]
    own = live & (named == expert)
    away = live & (named != expert)
    flags = jnp.stack([own, away])
    ranks = jnp.cumsum(flags.astype(jnp.int32), 1) - 1
    picker = (ranks[:, None, :] == jnp.arange(CAP)[None, :, None]) & flags[:, None, :]
    packed = jnp.dot(
        picker.reshape(2 * CAP, tok_rows).astype(BF16), grad_rows, preferred_element_type=F32
    ).astype(BF16)
    tally = jnp.sum(flags.astype(jnp.int32), 1)
    front = swapped(
        jnp.concatenate([packed[CAP:, :LEAD], count_rows(tally[1], 2, LEAD)], 0), group
    )
    first_part = jnp.concatenate(
        [
            packed[:CAP, :LEAD],
            front[:CAP],
            lead_factor[:, :LEAD],
            front[CAP:] + count_rows(tally[0], 0, LEAD),
        ],
        0,
    )
    incoming = swapped(after(packed[CAP:], front), group)
    outgoing = jnp.concatenate([packed[:CAP], lead_factor], 0)

    ends = [end for end in (LEAD, 2 * LEAD, 2 * LEAD + ROWS) if end < width] + [width]
    chunks = list(zip([0, *ends], ends))
    parts = [first_part]
    quarter = jnp.concatenate([packed[:CAP], incoming, lead_factor], 0)
    for begin, end in chunks[1:]:
        parts += copied([(quarter, begin, end)], [parts[-1]])
    spread = [lax.all_gather(part, "fac") for part in parts]
    across_own = gather_members(outgoing, bits)
    across_other = gather_members(incoming, bits)
    earlier = [across_own[1], across_other[1], *parts[1:]]
    lead = gather_members(copied([(spread[0], 0, 1)], earlier)[0][0], bits)

    places = [member, column, member * width]
    assert len(places) == PLACES
    slots = jnp.stack(places + order).astype(jnp.int32)
    upper, inverse, share = factor_lead(slots, damp, factor_old[:LEAD, :LEAD], lead)
    panel, lead_stack, across_stack = panel_columns(
        slots, share, inverse, lead, across_own, across_other
    )
    near_grad = weight_grad.reshape(-1, ROWS, weight_grad.shape[1])
    near_grad = copied([(near_grad, 0, LEAD // ROWS)], [lead[1]])[0].reshape(LEAD, -1)
    near_grad = from_first_member(near_grad, member, group, bits, inverse)
    solved = jnp.dot(inverse, near_grad.astype(F32), precision=lax.Precision.HIGH)
    high = solved.astype(BF16)
    low = (solved - high.astype(F32)).astype(BF16)
    lower = upper.T

    results = ()
    gates = [lead[1], inverse, panel]
    for (begin, end), part in zip(chunks, spread):
        views = exchange_members(part, member, bits, [gates.pop(0)])
        places[2] = member * width + begin
        slots = jnp.stack(places + order + [jnp.int32(at) for _, at in views])
        *results, token = finish_rows(
            begin,
            slots.astype(jnp.int32),
            damp,
            share,
            factor_old,
            weight_grad,
            panel,
            inverse,
            lower,
            high,
            low,
            lead_stack,
            across_stack,
            [array for array, _ in views],
            list(results),
            [] if begin else spread[2:3],
        )
        if begin:
            gates.append(token)
    return tuple(results)


def solution(mesh):
    placed = (P("tok", "fac"), P("tok", None), P("tok"), P("tok", "fac"), P(), P("tok", "fac"))
    return jax.shard_map(
        local,
        mesh=mesh,
        in_specs=placed,
        out_specs=(P("tok", "fac"), P("tok", "fac"), P("tok", "fac")),
        check_vma=False,
    )
```

```python
import jax
import jax.numpy as jnp
from jax import lax
from jax.experimental import pallas as pl
from jax.experimental.pallas import tpu as pltpu
from jax.sharding import PartitionSpec as P

CAP = 320
LEAD = 512
TILE = 128
GROUP = 8
ROWS = 256
COLS = 512
PLACES = 3
NO_COST = pl.CostEstimate(flops=1, bytes_accessed=1, transcendentals=0)
DECAY = 0.8

HIGHEST = lax.Precision.HIGHEST
BF16 = jnp.bfloat16
F32 = jnp.float32


def dot_t(left, right, precision=None):
    return lax.dot_general(
        left, right, (((0,), (0,)), ((), ())), precision=precision, preferred_element_type=F32
    )


def splat(rows, lane):
    return jnp.broadcast_to(rows[:, lane : lane + 1], rows.shape)


def eliminate_tile(rows):
    lanes = lax.broadcasted_iota(jnp.int32, (GROUP, TILE), 1)
    subs = lax.broadcasted_iota(jnp.int32, (GROUP, TILE), 0)
    upper, inverse = [], []
    for step in range(TILE // GROUP):
        base = step * GROUP
        inside = (lanes >= base) & (lanes < base + GROUP)
        block = rows[step]
        first = [jnp.broadcast_to(block[t : t + 1, :], (GROUP, TILE)) for t in range(GROUP)]
        second = [
            jnp.where(inside, jnp.where(lanes == base + t, 1.0, 0.0), first[t])
            for t in range(GROUP)
        ]
        pivot = [
            [splat(first[t], base + u) if u >= t else None for u in range(GROUP)]
            for t in range(GROUP)
        ]
        scale = [None] * GROUP
        for t in range(GROUP):
            scale[t] = lax.rsqrt(pivot[t][t])
            for u in range(t + 1, GROUP):
                pivot[t][u] = pivot[t][u] * scale[t]
            for u in range(t + 1, GROUP):
                for w in range(u, GROUP):
                    pivot[u][w] = pivot[u][w] - pivot[t][u] * pivot[t][w]
            first[t] = first[t] * scale[t]
            second[t] = second[t] * scale[t]
            for u in range(t + 1, GROUP):
                first[u] = first[u] - pivot[t][u] * first[t]
                second[u] = second[u] - pivot[t][u] * second[t]
        solved = [None] * GROUP
        for t in reversed(range(GROUP)):
            value = second[t]
            for u in range(t + 1, GROUP):
                value = value - pivot[t][u] * solved[u]
            solved[t] = value * scale[t]
        for later in range(step + 1, TILE // GROUP):
            value = jnp.where(inside, 0.0, rows[later])
            for t in range(GROUP):
                value = value - splat(rows[later], base + t) * solved[t]
            rows[later] = value
        upper_rows, inverse_rows = first[0], second[0]
        for t in range(1, GROUP):
            upper_rows = jnp.where(subs == t, first[t], upper_rows)
            inverse_rows = jnp.where(subs == t, second[t], inverse_rows)
        upper.append(upper_rows)
        inverse.append(inverse_rows)
    return upper, inverse


def factor_kernel(count, places_ref, damp_ref, exact_ref, *refs):
    lead_refs = refs[:count]
    upper_ref, inverse_ref, share_ref, work_ref = refs[-4:]
    steps = LEAD // TILE
    side = LEAD // count
    marks = sum(lead[2 * CAP + side :, :].astype(F32) for lead in lead_refs)
    row = lax.broadcasted_iota(jnp.int32, marks.shape, 0)
    weight = jnp.where(row < 4, jnp.where(row % 2 == 0, 256.0, 1.0), 0.0)
    total = jnp.sum(marks * weight, axis=0, keepdims=True)[:, :1]
    share = (1.0 - DECAY) / total
    share_ref[...] = jnp.broadcast_to(share, share_ref.shape)
    for q, lead in enumerate(lead_refs):
        begin = pl.multiple_of(places_ref[PLACES + q] * side, side)
        work_ref[pl.ds(begin, side), :] = lead[2 * CAP : 2 * CAP + side, :].astype(F32)

    @pl.when((places_ref[0] == 0) & (places_ref[1] == 0))
    def _():
        work_ref[...] = exact_ref[...]

    gram = sum(dot_t(lead[: 2 * CAP, :], lead[: 2 * CAP, :]) for lead in lead_refs)
    rows = lax.broadcasted_iota(jnp.int32, (LEAD, LEAD), 0)
    cols = lax.broadcasted_iota(jnp.int32, (LEAD, LEAD), 1)
    work_ref[...] = (
        DECAY * work_ref[...] + share * gram + jnp.where(rows == cols, damp_ref[0], 0.0)
    )
    upper_ref[...] = jnp.zeros_like(upper_ref)
    inverse_ref[...] = jnp.zeros_like(inverse_ref)
    lanes = lax.broadcasted_iota(jnp.int32, (GROUP, TILE), 1)
    subs = lax.broadcasted_iota(jnp.int32, (GROUP, TILE), 0)

    def tile_step(k, carry):
        begin = pl.multiple_of(k * TILE, TILE)
        rows = [
            work_ref[pl.ds(begin + g * GROUP, GROUP), pl.ds(begin, TILE)]
            for g in range(TILE // GROUP)
        ]
        upper, inverse = eliminate_tile(rows)
        upper_tile = jnp.concatenate(
            [jnp.where(lanes >= subs + g * GROUP, part, 0.0) for g, part in enumerate(upper)], 0
        )
        inverse_tile = jnp.concatenate(
            [jnp.where(lanes <= subs + g * GROUP, part, 0.0) for g, part in enumerate(inverse)], 0
        )
        band = jnp.dot(
            inverse_tile,
            work_ref[pl.ds(begin, TILE), :],
            precision=HIGHEST,
            preferred_element_type=F32,
        )
        work_ref[pl.ds(begin, TILE), :] = band
        work_ref[pl.ds(begin, TILE), pl.ds(begin, TILE)] = inverse_tile
        upper_ref[pl.ds(begin, TILE), pl.ds(begin, TILE)] = upper_tile
        inverse_ref[pl.ds(begin, TILE), pl.ds(begin, TILE)] = inverse_tile
        for other in range(steps):

            @pl.when(other < k)
            def _():
                inverse_ref[pl.ds(begin, TILE), other * TILE : (other + 1) * TILE] = work_ref[
                    pl.ds(begin, TILE), other * TILE : (other + 1) * TILE
                ]

            @pl.when(other > k)
            def _():
                span = slice(other * TILE, (other + 1) * TILE)
                part = work_ref[pl.ds(begin, TILE), span]
                upper_ref[pl.ds(begin, TILE), span] = part
                work_ref[span, pl.ds(begin, TILE)] = jnp.zeros((TILE, TILE), F32)
                work_ref[span, :] = work_ref[span, :] - dot_t(
                    part, work_ref[pl.ds(begin, TILE), :], HIGHEST
                )

        return carry

    lax.fori_loop(0, steps, tile_step, 0)


def factor_lead(places, damp, exact, lead):
    shape = jax.ShapeDtypeStruct((LEAD, LEAD), F32)
    vmem = pl.BlockSpec(memory_space=pltpu.VMEM)
    smem = pl.BlockSpec(memory_space=pltpu.SMEM)
    return pl.pallas_call(
        lambda *refs: factor_kernel(len(lead), *refs),
        out_shape=(shape, shape, jax.ShapeDtypeStruct((GROUP, TILE), F32)),
        in_specs=[smem, smem] + [vmem] * (1 + len(lead)),
        out_specs=(vmem, vmem, vmem),
        scratch_shapes=[pltpu.VMEM((LEAD, LEAD), F32)],
        compiler_params=pltpu.CompilerParams(vmem_limit_bytes=32 * 1024 * 1024),
        cost_estimate=NO_COST,
    )(places, damp, exact, *lead)


def panel_kernel(count, places_ref, share_ref, inverse_ref, *refs):
    lead, own, other = refs[:count], refs[count : 2 * count], refs[2 * count : 3 * count]
    out_ref, lead_ref, across_ref, near_ref = refs[-4:]
    side = LEAD // count
    depth = 2 * CAP
    for q in range(count):
        across_ref[q * depth : q * depth + CAP, :] = own[q][:CAP, :]
        across_ref[q * depth + CAP : (q + 1) * depth, :] = other[q][...]
        begin = pl.multiple_of(places_ref[PLACES + q] * side, side)
        near_ref[pl.ds(begin, side), :] = own[q][CAP:, :].astype(F32)

    @pl.when(pl.program_id(0) == 0)
    def _():
        for q in range(count):
            lead_ref[q * depth : (q + 1) * depth, :] = lead[q][:depth, :]

    gram = dot_t(lead_ref[...], across_ref[...])
    beside = DECAY * near_ref[...] + share_ref[:1, :1] * gram
    out_ref[...] = jnp.dot(
        inverse_ref[...], beside, precision=HIGHEST, preferred_element_type=F32
    ).astype(BF16)


def panel_columns(places, share, inverse, lead, own, other):
    count = len(lead)
    width = own[0].shape[1]
    cols = COLS if width % COLS == 0 else ROWS
    tall = 2 * CAP * count
    whole = lambda height: pl.BlockSpec((height, LEAD), lambda j: (0, 0))
    tiled = lambda height: pl.BlockSpec((height, cols), lambda j: (0, j))
    return pl.pallas_call(
        lambda *refs: panel_kernel(count, *refs),
        grid=(width // cols,),
        out_shape=(
            jax.ShapeDtypeStruct((LEAD, width), BF16),
            jax.ShapeDtypeStruct((tall, LEAD), BF16),
            jax.ShapeDtypeStruct((tall, width), BF16),
        ),
        in_specs=[
            pl.BlockSpec(memory_space=pltpu.SMEM),
            pl.BlockSpec((GROUP, TILE), lambda j: (0, 0)),
            whole(LEAD),
        ]
        + [whole(lead[0].shape[0])] * count
        + [tiled(own[0].shape[0])] * count
        + [tiled(CAP)] * count,
        out_specs=(tiled(LEAD), whole(tall), tiled(tall)),
        scratch_shapes=[pltpu.VMEM((LEAD, cols), F32)],
        compiler_params=pltpu.CompilerParams(vmem_limit_bytes=56 * 1024 * 1024),
        cost_estimate=NO_COST,
    )(places, share, inverse, *lead, *own, *other)


def finish_kernel(
    count,
    gram_steps,
    first_chunk,
    unread,
    places_ref,
    damp_ref,
    share_ref,
    factor_ref,
    grad_ref,
    panel_ref,
    inverse_ref,
    high_ref,
    low_ref,
    lead_ref,
    across_ref,
    *refs,
):
    if first_chunk:
        lower_ref, *refs = refs
    mine = refs[:count]
    outs = refs[count + unread :]
    running_ref, factored_ref, precond_ref, token_ref, mine_ref, rows_ref, first_ref = outs
    j, i = pl.program_id(0), pl.program_id(1)
    member, column, base = places_ref[0], places_ref[1], places_ref[2]
    share, damp = share_ref[:1, :1], damp_ref[0]
    height, cols = running_ref.shape
    depth = 2 * CAP
    side = LEAD // count
    span = pl.ds(pl.multiple_of(i * height, height), height)
    head = (member == 0) & first_chunk

    @pl.when(j == 0)
    def _():
        token_ref[...] = jnp.zeros_like(token_ref)
        for q in range(count):
            mine_ref[span, q * depth : (q + 1) * depth] = mine[q][0, :depth, :].T
            begin = pl.multiple_of(places_ref[PLACES + q] * side, side)
            first_ref[pl.ds(begin, side), :] = mine[q][0, depth : depth + side, :].astype(F32)
        source = first_ref[...].T
        if cols == LEAD:
            source = jnp.where(column == 0, factor_ref[...], source)
        gram = jnp.dot(mine_ref[span, :], lead_ref[...], preferred_element_type=F32)
        row = base + i * height + lax.broadcasted_iota(jnp.int32, (height, LEAD), 0)
        col = lax.broadcasted_iota(jnp.int32, (height, LEAD), 1)
        source = DECAY * source + share * gram
        source = source + jnp.where(row == col, damp, 0.0)
        rows_ref[span, :] = lax.dot_general(
            source,
            inverse_ref[...],
            (((1,), (1,)), ((), ())),
            precision=HIGHEST,
            preferred_element_type=F32,
        )

    panel = rows_ref[span, :].astype(BF16)

    @pl.when(j < gram_steps)
    def _():
        gram = jnp.dot(mine_ref[span, :], across_ref[...], preferred_element_type=F32)
        running = DECAY * factor_ref[...] + share * gram
        running_ref[...] = running
        row = base + i * height + lax.broadcasted_iota(jnp.int32, (height, cols), 0)
        col = (column * gram_steps + j) * cols + lax.broadcasted_iota(jnp.int32, (height, cols), 1)
        matrix = running + jnp.where(row == col, damp, 0.0)
        factored = matrix - jnp.dot(panel, panel_ref[...], preferred_element_type=F32)
        factored_ref[...] = jnp.where(head, 0.0, factored)

        for part in range(LEAD // cols):
            edge = slice(part * cols, (part + 1) * cols)

            @pl.when((column == 0) & (j == part))
            def _():
                factored_ref[...] = rows_ref[span, edge]

                if first_chunk:

                    @pl.when(head)
                    def _():
                        factored_ref[...] = lower_ref[span, edge]

    high, low = high_ref[...], low_ref[...]
    product = jnp.dot(panel, high, preferred_element_type=F32)
    product = product + jnp.dot(panel, low, preferred_element_type=F32)
    precond_ref[...] = grad_ref[...].astype(F32) - product

    if first_chunk:

        @pl.when(head)
        def _():
            precond_ref[...] = high_ref[span, :].astype(F32) + low_ref[span, :].astype(F32)


def finish_rows(
    begin, places, damp, share, factor, grad, panel, inverse, lower, high, low,
    lead, across, mine, results, earlier,
):
    count = len(mine)
    deep, rows = mine[0].shape[1:]
    width, grad_cols = factor.shape[0], grad.shape[1]
    tall = lead.shape[0]
    height = min(rows, COLS)
    tiles = rows // height
    start = begin // height
    cols = COLS if width % COLS == 0 else ROWS
    gram_steps, steps = width // cols, grad_cols // cols
    assert steps >= gram_steps and rows % height == 0 and begin % height == 0

    def mine_spec(q):
        return pl.BlockSpec(
            (1, deep, height),
            lambda j, i, p: (p[PLACES + count + q], 0, jnp.where(j == 0, i, tiles - 1)),
        )

    def gram_col(j):
        return jnp.minimum(j, gram_steps - 1)

    def gram_tile(j, i, p):
        return (start + jnp.where(j < gram_steps, i, tiles - 1), gram_col(j))

    grad_spec = pl.BlockSpec((height, cols), lambda j, i, p: (start + i, j))
    factor_spec = pl.BlockSpec((height, cols), gram_tile)
    lead_whole = pl.BlockSpec((LEAD, LEAD), lambda j, i, p: (0, 0))
    small = pl.BlockSpec((GROUP, TILE), lambda j, i, p: (0, 0))
    in_specs = [
        pl.BlockSpec(memory_space=pltpu.SMEM),
        small,
        factor_spec,
        grad_spec,
        pl.BlockSpec((LEAD, cols), lambda j, i, p: (0, gram_col(j))),
        lead_whole,
        pl.BlockSpec((LEAD, cols), lambda j, i, p: (0, j)),
        pl.BlockSpec((LEAD, cols), lambda j, i, p: (0, j)),
        pl.BlockSpec((tall, LEAD), lambda j, i, p: (0, 0)),
        pl.BlockSpec((tall, cols), lambda j, i, p: (0, gram_col(j))),
    ]
    operands = [damp, share, factor, grad, panel, inverse, high, low, lead, across]
    if begin == 0:
        in_specs += [lead_whole]
        operands += [lower]
    in_specs += [mine_spec(q) for q in range(count)]
    operands += mine
    aliases = {1 + len(operands) + k: k for k in range(len(results))}
    operands += [*results, *earlier]
    unread = len(results) + len(earlier)
    in_specs += [pl.BlockSpec(memory_space=pl.ANY)] * unread
    return pl.pallas_call(
        lambda *refs: finish_kernel(count, gram_steps, begin == 0, unread, *refs),
        grid_spec=pltpu.PrefetchScalarGridSpec(
            num_scalar_prefetch=1,
            grid=(steps, tiles),
            in_specs=in_specs,
            out_specs=(factor_spec, factor_spec, grad_spec, small),
            scratch_shapes=[
                pltpu.VMEM((rows, tall), BF16),
                pltpu.VMEM((rows, LEAD), F32),
                pltpu.VMEM((LEAD, height), F32),
            ],
        ),
        out_shape=(
            jax.ShapeDtypeStruct(factor.shape, F32),
            jax.ShapeDtypeStruct(factor.shape, F32),
            jax.ShapeDtypeStruct(grad.shape, F32),
            jax.ShapeDtypeStruct((GROUP, TILE), F32),
        ),
        input_output_aliases=aliases,
        compiler_params=pltpu.CompilerParams(vmem_limit_bytes=56 * 1024 * 1024),
        cost_estimate=NO_COST,
    )(places, *operands)


def after(value, earlier):
    mark = earlier[(0,) * earlier.ndim]
    return jnp.where(mark == mark, value, jnp.zeros_like(value))


def swapped(value, mask):
    size = lax.axis_size("tok")
    return lax.ppermute(value, "tok", [(source, source ^ mask) for source in range(size)])


def gather_members(value, bits):
    pieces = [value]
    for bit in reversed(range(bits)):
        pieces = pieces + [swapped(piece, 1 << bit) for piece in pieces]
    return pieces


def copy_kernel(count, starts_ref, *refs):
    for source, out in zip(refs[:count], refs[-count:]):
        out[...] = source[...].astype(BF16)


def copied(requests, earlier):
    in_specs, out_specs, shapes, starts = [], [], [], []
    for number, (array, begin, size) in enumerate(requests):
        rows = array.shape[-2]
        split = next(parts for parts in (4, 7, 1) if rows % (16 * parts) == 0)
        if array.ndim == 3:
            count, width = size, array.shape[2]
            shapes.append((count, rows, width))
            starts.append(begin)
            block = (1, rows // split, width)
            in_specs.append(pl.BlockSpec(block, lambda k, r, p, n=number: (p[n] + k, r, 0)))
            out_specs.append(pl.BlockSpec(block, lambda k, r, p: (k, r, 0)))
        else:
            count, width = 1, size - begin
            shapes.append((rows, width))
            starts.append(begin // width)
            block = (rows // split, width)
            in_specs.append(pl.BlockSpec(block, lambda k, r, p, n=number: (r, p[n])))
            out_specs.append(pl.BlockSpec(block, lambda k, r, p: (r, 0)))
    arrays = [array for array, _, _ in requests]
    return pl.pallas_call(
        lambda *refs: copy_kernel(len(arrays), *refs),
        grid_spec=pltpu.PrefetchScalarGridSpec(
            num_scalar_prefetch=1,
            grid=(count, split),
            in_specs=in_specs + [pl.BlockSpec(memory_space=pl.ANY)] * len(earlier),
            out_specs=out_specs,
        ),
        out_shape=[jax.ShapeDtypeStruct(shape, BF16) for shape in shapes],
        cost_estimate=NO_COST,
    )(jnp.stack([jnp.int32(start) for start in starts]), *arrays, *earlier)


def exchange_members(blocks, member, bits, earlier):
    views = [(blocks, 0)]
    sent = []
    count = blocks.shape[0]
    for bit in reversed(range(bits)):
        count = count // 2
        mine = member >> bit & 1
        sent = copied(
            [(array, at + (1 - mine) * count, count) for array, at in views], earlier
        )
        kept = [(array, at + mine * count) for array, at in views]
        views = kept + [(swapped(part, 1 << bit), 0) for part in sent]
    return views


def member_order(bits):
    order = [0]
    for bit in reversed(range(bits)):
        order = order + [other ^ (1 << bit) for other in order]
    return order


def down_pairs(bit, group):
    mask = 1 << bit
    return [
        (source, source + mask)
        for source in range(lax.axis_size("tok"))
        if source % group % (2 * mask) == 0
    ]


def from_first_member(value, member, group, bits, earlier):
    for bit in reversed(range(bits)):
        if 1 << bit < group // 2:
            value = after(value, earlier)
        moved = lax.ppermute(value, "tok", down_pairs(bit, group))
        value = jnp.where(member >> bit & 1 == 1, moved, value)
    return value


def share_of_first(blocks, member, group, bits):
    for bit in reversed(range(bits)):
        half = blocks.shape[0] // 2
        moved = lax.ppermute(blocks[half:], "tok", down_pairs(bit, group))
        blocks = jnp.where(member >> bit & 1 == 1, moved, blocks[:half])
    return blocks[0]


def count_rows(number, row, width):
    index = lax.broadcasted_iota(jnp.int32, (16, width), 0)
    rest = jnp.where(index == row + 1, number % 256, 0)
    return jnp.where(index == row, number // 256, rest).astype(BF16)


def local(grad_rows, routes, counts, factor_old, damping, weight_grad):
    group = lax.axis_size("tok") // 2
    bits = group.bit_length() - 1
    position = lax.axis_index("tok")
    expert = position // group
    member = position % group
    column = lax.axis_index("fac")
    tok_rows, width = grad_rows.shape
    damp = jnp.where(expert == 0, damping[0], damping[1])[None]
    order = [member ^ other for other in member_order(bits)]

    lead_factor = factor_old.reshape(-1, LEAD // group, width)
    lead_factor = copied([(lead_factor, 0, group)], [])[0]
    lead_factor = share_of_first(lead_factor, member, group, bits)

    live = jnp.arange(tok_rows) < counts[0]
    named = routes[:, 0]
    own = live & (named == expert)
    away = live & (named != expert)
    flags = jnp.stack([own, away])
    ranks = jnp.cumsum(flags.astype(jnp.int32), 1) - 1
    picker = (ranks[:, None, :] == jnp.arange(CAP)[None, :, None]) & flags[:, None, :]
    packed = jnp.dot(
        picker.reshape(2 * CAP, tok_rows).astype(BF16), grad_rows, preferred_element_type=F32
    ).astype(BF16)
    tally = jnp.sum(flags.astype(jnp.int32), 1)
    front = swapped(
        jnp.concatenate([packed[CAP:, :LEAD], count_rows(tally[1], 2, LEAD)], 0), group
    )
    first_part = jnp.concatenate(
        [
            packed[:CAP, :LEAD],
            front[:CAP],
            lead_factor[:, :LEAD],
            front[CAP:] + count_rows(tally[0], 0, LEAD),
        ],
        0,
    )
    incoming = swapped(after(packed[CAP:], front), group)
    outgoing = jnp.concatenate([packed[:CAP], lead_factor], 0)

    ends = [end for end in (LEAD, 2 * LEAD, 2 * LEAD + ROWS) if end < width] + [width]
    chunks = list(zip([0, *ends], ends))
    parts = [first_part]
    quarter = jnp.concatenate([packed[:CAP], incoming, lead_factor], 0)
    for begin, end in chunks[1:]:
        parts += copied([(quarter, begin, end)], [parts[-1]])
    spread = [lax.all_gather(part, "fac") for part in parts]
    across_own = gather_members(outgoing, bits)
    across_other = gather_members(incoming, bits)
    earlier = [across_own[1], across_other[1], *parts[1:]]
    lead = gather_members(copied([(spread[0], 0, 1)], earlier)[0][0], bits)

    places = [member, column, member * width]
    assert len(places) == PLACES
    slots = jnp.stack(places + order).astype(jnp.int32)
    upper, inverse, share = factor_lead(slots, damp, factor_old[:LEAD, :LEAD], lead)
    panel, lead_stack, across_stack = panel_columns(
        slots, share, inverse, lead, across_own, across_other
    )
    near_grad = weight_grad.reshape(-1, ROWS, weight_grad.shape[1])
    near_grad = copied([(near_grad, 0, LEAD // ROWS)], [lead[1]])[0].reshape(LEAD, -1)
    near_grad = from_first_member(near_grad, member, group, bits, inverse)
    solved = jnp.dot(inverse, near_grad.astype(F32), precision=lax.Precision.HIGH)
    high = solved.astype(BF16)
    low = (solved - high.astype(F32)).astype(BF16)
    lower = upper.T

    results = ()
    gates = [lead[1], inverse, panel]
    for (begin, end), part in zip(chunks, spread):
        views = exchange_members(part, member, bits, [gates.pop(0)])
        places[2] = member * width + begin
        slots = jnp.stack(places + order + [jnp.int32(at) for _, at in views])
        *results, token = finish_rows(
            begin,
            slots.astype(jnp.int32),
            damp,
            share,
            factor_old,
            weight_grad,
            panel,
            inverse,
            lower,
            high,
            low,
            lead_stack,
            across_stack,
            [array for array, _ in views],
            list(results),
            [] if begin else spread[2:3],
        )
        if begin:
            gates.append(token)
    return tuple(results)


def solution(mesh):
    placed = (P("tok", "fac"), P("tok", None), P("tok"), P("tok", "fac"), P(), P("tok", "fac"))
    return jax.shard_map(
        local,
        mesh=mesh,
        in_specs=placed,
        out_specs=(P("tok", "fac"), P("tok", "fac"), P("tok", "fac")),
        check_vma=False,
    )
```

```python
import jax
import jax.numpy as jnp
from jax import lax
from jax.experimental import pallas as pl
from jax.experimental.pallas import tpu as pltpu
from jax.sharding import PartitionSpec as P

CAP = 320
LEAD = 512
TILE = 128
GROUP = 8
ROWS = 256
COLS = 512
PLACES = 3
ANYWHERE = pl.BlockSpec(memory_space=pl.ANY)
NO_COST = pl.CostEstimate(flops=1, bytes_accessed=1, transcendentals=0)
DECAY = 0.8

HIGHEST = lax.Precision.HIGHEST
BF16 = jnp.bfloat16
F32 = jnp.float32


def dot_t(left, right, precision=None):
    return lax.dot_general(
        left, right, (((0,), (0,)), ((), ())), precision=precision, preferred_element_type=F32
    )


def split(value):
    high = value.astype(BF16)
    return high, (value - high.astype(F32)).astype(BF16)


def dot_split(left, right, contract):
    (left_high, left_low), (right_high, right_low) = split(left), split(right)
    product = lambda a, b: lax.dot_general(
        a, b, (contract, ((), ())), preferred_element_type=F32
    )
    return product(left_high, right_high) + (
        product(left_high, right_low) + product(left_low, right_high)
    )


def splat(rows, lane):
    return jnp.broadcast_to(rows[:, lane : lane + 1], rows.shape)


def eliminate_tile(rows):
    lanes = lax.broadcasted_iota(jnp.int32, (GROUP, TILE), 1)
    subs = lax.broadcasted_iota(jnp.int32, (GROUP, TILE), 0)
    upper, inverse = [], []
    for step in range(TILE // GROUP):
        base = step * GROUP
        inside = (lanes >= base) & (lanes < base + GROUP)
        block = rows[step]
        first = [jnp.broadcast_to(block[t : t + 1, :], (GROUP, TILE)) for t in range(GROUP)]
        second = [
            jnp.where(inside, jnp.where(lanes == base + t, 1.0, 0.0), first[t])
            for t in range(GROUP)
        ]
        pivot = [
            [splat(first[t], base + u) if u >= t else None for u in range(GROUP)]
            for t in range(GROUP)
        ]
        scale = [None] * GROUP
        for t in range(GROUP):
            scale[t] = lax.rsqrt(pivot[t][t])
            for u in range(t + 1, GROUP):
                pivot[t][u] = pivot[t][u] * scale[t]
            for u in range(t + 1, GROUP):
                for w in range(u, GROUP):
                    pivot[u][w] = pivot[u][w] - pivot[t][u] * pivot[t][w]
            first[t] = first[t] * scale[t]
            second[t] = second[t] * scale[t]
            for u in range(t + 1, GROUP):
                first[u] = first[u] - pivot[t][u] * first[t]
                second[u] = second[u] - pivot[t][u] * second[t]
        solved = [None] * GROUP
        for t in reversed(range(GROUP)):
            value = second[t]
            for u in range(t + 1, GROUP):
                value = value - pivot[t][u] * solved[u]
            solved[t] = value * scale[t]
        for later in range(step + 1, TILE // GROUP):
            value = jnp.where(inside, 0.0, rows[later])
            for t in range(GROUP):
                value = value - splat(rows[later], base + t) * solved[t]
            rows[later] = value
        upper_rows, inverse_rows = first[0], second[0]
        for t in range(1, GROUP):
            upper_rows = jnp.where(subs == t, first[t], upper_rows)
            inverse_rows = jnp.where(subs == t, second[t], inverse_rows)
        upper.append(upper_rows)
        inverse.append(inverse_rows)
    return upper, inverse


def factor_kernel(count, places_ref, damp_ref, exact_ref, *refs):
    lead_refs = refs[:count]
    lower_ref, inverse_ref, share_ref, work_ref, upper_ref = refs[-5:]
    steps = LEAD // TILE
    side = LEAD // count
    marks = sum(lead[2 * CAP + side :, :].astype(F32) for lead in lead_refs)
    row = lax.broadcasted_iota(jnp.int32, marks.shape, 0)
    weight = jnp.where(row < 4, jnp.where(row % 2 == 0, 256.0, 1.0), 0.0)
    total = jnp.sum(marks * weight, axis=0, keepdims=True)[:, :1]
    share = (1.0 - DECAY) / total
    share_ref[...] = jnp.broadcast_to(share, share_ref.shape)
    for q, lead in enumerate(lead_refs):
        begin = pl.multiple_of(places_ref[PLACES + q] * side, side)
        work_ref[pl.ds(begin, side), :] = lead[2 * CAP : 2 * CAP + side, :].astype(F32)

    @pl.when((places_ref[0] == 0) & (places_ref[1] == 0))
    def _():
        work_ref[...] = exact_ref[...]

    gram = sum(dot_t(lead[: 2 * CAP, :], lead[: 2 * CAP, :]) for lead in lead_refs)
    rows = lax.broadcasted_iota(jnp.int32, (LEAD, LEAD), 0)
    cols = lax.broadcasted_iota(jnp.int32, (LEAD, LEAD), 1)
    work_ref[...] = (
        DECAY * work_ref[...] + share * gram + jnp.where(rows == cols, damp_ref[0], 0.0)
    )
    upper_ref[...] = jnp.zeros_like(upper_ref)
    inverse_ref[...] = jnp.zeros_like(inverse_ref)
    lanes = lax.broadcasted_iota(jnp.int32, (GROUP, TILE), 1)
    subs = lax.broadcasted_iota(jnp.int32, (GROUP, TILE), 0)

    def tile_step(k, carry):
        begin = pl.multiple_of(k * TILE, TILE)
        rows = [
            work_ref[pl.ds(begin + g * GROUP, GROUP), pl.ds(begin, TILE)]
            for g in range(TILE // GROUP)
        ]
        upper, inverse = eliminate_tile(rows)
        upper_tile = jnp.concatenate(
            [jnp.where(lanes >= subs + g * GROUP, part, 0.0) for g, part in enumerate(upper)], 0
        )
        inverse_tile = jnp.concatenate(
            [jnp.where(lanes <= subs + g * GROUP, part, 0.0) for g, part in enumerate(inverse)], 0
        )
        band = jnp.dot(
            inverse_tile,
            work_ref[pl.ds(begin, TILE), :],
            precision=HIGHEST,
            preferred_element_type=F32,
        )
        work_ref[pl.ds(begin, TILE), :] = band
        work_ref[pl.ds(begin, TILE), pl.ds(begin, TILE)] = inverse_tile
        upper_ref[pl.ds(begin, TILE), pl.ds(begin, TILE)] = upper_tile
        inverse_ref[pl.ds(begin, TILE), pl.ds(begin, TILE)] = inverse_tile
        for other in range(steps):

            @pl.when(other < k)
            def _():
                inverse_ref[pl.ds(begin, TILE), other * TILE : (other + 1) * TILE] = work_ref[
                    pl.ds(begin, TILE), other * TILE : (other + 1) * TILE
                ]

            @pl.when(other > k)
            def _():
                span = slice(other * TILE, (other + 1) * TILE)
                part = work_ref[pl.ds(begin, TILE), span]
                upper_ref[pl.ds(begin, TILE), span] = part
                work_ref[span, pl.ds(begin, TILE)] = jnp.zeros((TILE, TILE), F32)
                work_ref[span, :] = work_ref[span, :] - dot_t(
                    part, work_ref[pl.ds(begin, TILE), :], HIGHEST
                )

        return carry

    lax.fori_loop(0, steps, tile_step, 0)
    lower_ref[...] = upper_ref[...].T


def factor_lead(places, damp, exact, lead, earlier):
    shape = jax.ShapeDtypeStruct((LEAD, LEAD), F32)
    vmem = pl.BlockSpec(memory_space=pltpu.VMEM)
    smem = pl.BlockSpec(memory_space=pltpu.SMEM)
    return pl.pallas_call(
        lambda *refs: factor_kernel(len(lead), *refs),
        out_shape=(shape, shape, jax.ShapeDtypeStruct((GROUP, TILE), F32)),
        in_specs=[smem, smem] + [vmem] * (1 + len(lead)) + [ANYWHERE] * len(earlier),
        out_specs=(vmem, vmem, vmem),
        scratch_shapes=[pltpu.VMEM((LEAD, LEAD), F32)] * 2,
        compiler_params=pltpu.CompilerParams(vmem_limit_bytes=32 * 1024 * 1024),
        cost_estimate=NO_COST,
    )(places, damp, exact, *lead, *earlier)


def panel_kernel(count, places_ref, share_ref, inverse_ref, *refs):
    lead, own, other = refs[:count], refs[count : 2 * count], refs[2 * count : 3 * count]
    out_ref, lead_ref, across_ref, near_ref = refs[-4:]
    side = LEAD // count
    depth = 2 * CAP
    for q in range(count):
        across_ref[q * depth : q * depth + CAP, :] = own[q][:CAP, :]
        across_ref[q * depth + CAP : (q + 1) * depth, :] = other[q][...]
        begin = pl.multiple_of(places_ref[PLACES + q] * side, side)
        near_ref[pl.ds(begin, side), :] = own[q][CAP:, :].astype(F32)

    @pl.when(pl.program_id(0) == 0)
    def _():
        for q in range(count):
            lead_ref[q * depth : (q + 1) * depth, :] = lead[q][:depth, :]

    gram = dot_t(lead_ref[...], across_ref[...])
    beside = DECAY * near_ref[...] + share_ref[:1, :1] * gram
    out_ref[...] = dot_split(inverse_ref[...], beside, ((1,), (0,))).astype(BF16)


def panel_columns(places, share, inverse, lead, own, other):
    count = len(lead)
    width = own[0].shape[1]
    cols = COLS if width % COLS == 0 else ROWS
    tall = 2 * CAP * count
    whole = lambda height: pl.BlockSpec((height, LEAD), lambda j: (0, 0))
    tiled = lambda height: pl.BlockSpec((height, cols), lambda j: (0, j))
    return pl.pallas_call(
        lambda *refs: panel_kernel(count, *refs),
        grid=(width // cols,),
        out_shape=(
            jax.ShapeDtypeStruct((LEAD, width), BF16),
            jax.ShapeDtypeStruct((tall, LEAD), BF16),
            jax.ShapeDtypeStruct((tall, width), BF16),
        ),
        in_specs=[
            pl.BlockSpec(memory_space=pltpu.SMEM),
            pl.BlockSpec((GROUP, TILE), lambda j: (0, 0)),
            whole(LEAD),
        ]
        + [whole(lead[0].shape[0])] * count
        + [tiled(own[0].shape[0])] * count
        + [tiled(CAP)] * count,
        out_specs=(tiled(LEAD), whole(tall), tiled(tall)),
        scratch_shapes=[pltpu.VMEM((LEAD, cols), F32)],
        compiler_params=pltpu.CompilerParams(vmem_limit_bytes=56 * 1024 * 1024),
        cost_estimate=NO_COST,
    )(places, share, inverse, *lead, *own, *other)


def solve_kernel(flag_ref, inverse_ref, first_ref, second_ref, *refs):
    high_ref, low_ref = refs[-2:]
    values = jnp.where(flag_ref[0] == 1, first_ref[...], second_ref[...])
    high, low = split(inverse_ref[...])
    solved = jnp.dot(high, values, preferred_element_type=F32)
    solved = solved + jnp.dot(low, values, preferred_element_type=F32)
    high_ref[...], low_ref[...] = split(solved)


def solve_lead(flag, inverse, first, second, earlier):
    tiled = pl.BlockSpec((LEAD, ROWS), lambda j: (0, j))
    return pl.pallas_call(
        solve_kernel,
        grid=(first.shape[1] // ROWS,),
        out_shape=(jax.ShapeDtypeStruct(first.shape, BF16),) * 2,
        in_specs=[
            pl.BlockSpec(memory_space=pltpu.SMEM),
            pl.BlockSpec((LEAD, LEAD), lambda j: (0, 0)),
            tiled,
            tiled,
        ]
        + [ANYWHERE] * len(earlier),
        out_specs=(tiled, tiled),
        compiler_params=pltpu.CompilerParams(vmem_limit_bytes=32 * 1024 * 1024),
        cost_estimate=NO_COST,
    )(flag, inverse, first, second, *earlier)


def finish_kernel(
    count,
    gram_steps,
    first_chunk,
    unread,
    places_ref,
    damp_ref,
    share_ref,
    factor_ref,
    grad_ref,
    panel_ref,
    inverse_ref,
    high_ref,
    lead_ref,
    across_ref,
    *refs,
):
    if first_chunk:
        lower_ref, low_ref, *refs = refs
    mine = refs[:count]
    outs = refs[count + unread :]
    running_ref, factored_ref, precond_ref, token_ref, mine_ref, rows_ref, first_ref = outs
    j, i = pl.program_id(0), pl.program_id(1)
    member, column, base = places_ref[0], places_ref[1], places_ref[2]
    share, damp = share_ref[:1, :1], damp_ref[0]
    height, cols = running_ref.shape
    depth = 2 * CAP
    side = LEAD // count
    span = pl.ds(pl.multiple_of(i * height, height), height)
    head = (member == 0) & first_chunk

    @pl.when(j == 0)
    def _():
        token_ref[...] = jnp.zeros_like(token_ref)
        for q in range(count):
            mine_ref[span, q * depth : (q + 1) * depth] = mine[q][0, :depth, :].T
            begin = pl.multiple_of(places_ref[PLACES + q] * side, side)
            first_ref[pl.ds(begin, side), :] = mine[q][0, depth : depth + side, :].astype(F32)
        source = first_ref[...].T
        if cols == LEAD:
            source = jnp.where(column == 0, factor_ref[...], source)
        gram = jnp.dot(mine_ref[span, :], lead_ref[...], preferred_element_type=F32)
        row = base + i * height + lax.broadcasted_iota(jnp.int32, (height, LEAD), 0)
        col = lax.broadcasted_iota(jnp.int32, (height, LEAD), 1)
        source = DECAY * source + share * gram
        source = source + jnp.where(row == col, damp, 0.0)
        rows_ref[span, :] = dot_split(source, inverse_ref[...], ((1,), (1,)))

    panel = rows_ref[span, :].astype(BF16)

    @pl.when(j < gram_steps)
    def _():
        gram = jnp.dot(mine_ref[span, :], across_ref[...], preferred_element_type=F32)
        running = DECAY * factor_ref[...] + share * gram
        running_ref[...] = running
        row = base + i * height + lax.broadcasted_iota(jnp.int32, (height, cols), 0)
        col = (column * gram_steps + j) * cols + lax.broadcasted_iota(jnp.int32, (height, cols), 1)
        matrix = running + jnp.where(row == col, damp, 0.0)
        factored = matrix - jnp.dot(panel, panel_ref[...], preferred_element_type=F32)
        factored_ref[...] = jnp.where(head, 0.0, factored)

        for part in range(LEAD // cols):
            edge = slice(part * cols, (part + 1) * cols)

            @pl.when((column == 0) & (j == part))
            def _():
                factored_ref[...] = rows_ref[span, edge]

                if first_chunk:

                    @pl.when(head)
                    def _():
                        factored_ref[...] = lower_ref[span, edge]

    product = jnp.dot(panel, high_ref[...], preferred_element_type=F32)
    precond_ref[...] = grad_ref[...].astype(F32) - product

    if first_chunk:

        @pl.when(head)
        def _():
            precond_ref[...] = high_ref[span, :].astype(F32) + low_ref[span, :].astype(F32)


def finish_rows(
    begin, places, damp, share, factor, grad, panel, inverse, lower, high, low,
    lead, across, mine, results, earlier,
):
    count = len(mine)
    deep, rows = mine[0].shape[1:]
    width, grad_cols = factor.shape[0], grad.shape[1]
    tall = lead.shape[0]
    height = min(rows, COLS)
    tiles = rows // height
    start = begin // height
    cols = COLS if width % COLS == 0 else ROWS
    gram_steps, steps = width // cols, grad_cols // cols
    assert steps >= gram_steps and rows % height == 0 and begin % height == 0

    def mine_spec(q):
        return pl.BlockSpec(
            (1, deep, height),
            lambda j, i, p: (p[PLACES + count + q], 0, jnp.where(j == 0, i, tiles - 1)),
        )

    def gram_col(j):
        return jnp.minimum(j, gram_steps - 1)

    def gram_tile(j, i, p):
        return (start + jnp.where(j < gram_steps, i, tiles - 1), gram_col(j))

    grad_spec = pl.BlockSpec((height, cols), lambda j, i, p: (start + i, j))
    factor_spec = pl.BlockSpec((height, cols), gram_tile)
    lead_whole = pl.BlockSpec((LEAD, LEAD), lambda j, i, p: (0, 0))
    small = pl.BlockSpec((GROUP, TILE), lambda j, i, p: (0, 0))
    in_specs = [
        pl.BlockSpec(memory_space=pltpu.SMEM),
        small,
        factor_spec,
        grad_spec,
        pl.BlockSpec((LEAD, cols), lambda j, i, p: (0, gram_col(j))),
        lead_whole,
        pl.BlockSpec((LEAD, cols), lambda j, i, p: (0, j)),
        pl.BlockSpec((tall, LEAD), lambda j, i, p: (0, 0)),
        pl.BlockSpec((tall, cols), lambda j, i, p: (0, gram_col(j))),
    ]
    operands = [damp, share, factor, grad, panel, inverse, high, lead, across]
    if begin == 0:
        in_specs += [lead_whole, pl.BlockSpec((LEAD, cols), lambda j, i, p: (0, j))]
        operands += [lower, low]
    in_specs += [mine_spec(q) for q in range(count)]
    operands += mine
    aliases = {1 + len(operands) + k: k for k in range(len(results))}
    operands += [*results, *earlier]
    unread = len(results) + len(earlier)
    in_specs += [ANYWHERE] * unread
    return pl.pallas_call(
        lambda *refs: finish_kernel(count, gram_steps, begin == 0, unread, *refs),
        grid_spec=pltpu.PrefetchScalarGridSpec(
            num_scalar_prefetch=1,
            grid=(steps, tiles),
            in_specs=in_specs,
            out_specs=(factor_spec, factor_spec, grad_spec, small),
            scratch_shapes=[
                pltpu.VMEM((rows, tall), BF16),
                pltpu.VMEM((rows, LEAD), F32),
                pltpu.VMEM((LEAD, height), F32),
            ],
        ),
        out_shape=(
            jax.ShapeDtypeStruct(factor.shape, F32),
            jax.ShapeDtypeStruct(factor.shape, F32),
            jax.ShapeDtypeStruct(grad.shape, F32),
            jax.ShapeDtypeStruct((GROUP, TILE), F32),
        ),
        input_output_aliases=aliases,
        compiler_params=pltpu.CompilerParams(vmem_limit_bytes=56 * 1024 * 1024),
        cost_estimate=NO_COST,
    )(places, *operands)


def after(value, earlier):
    mark = earlier[(0,) * earlier.ndim]
    return jnp.where(mark == mark, value, jnp.zeros_like(value))


def swapped(value, mask):
    size = lax.axis_size("tok")
    return lax.ppermute(value, "tok", [(source, source ^ mask) for source in range(size)])


def gather_members(value, bits):
    pieces = [value]
    for bit in reversed(range(bits)):
        pieces = pieces + [swapped(piece, 1 << bit) for piece in pieces]
    return pieces


def copy_kernel(count, places_ref, *refs):
    for source, out in zip(refs[:count], refs[-count:]):
        out[...] = source[...].astype(BF16)


def copied(requests, earlier):
    in_specs, out_specs, shapes, places = [], [], [], []
    for array, block, place in requests:
        at = len(places)
        places += place
        shape = tuple(size for size in block if size is not None)
        shapes.append(shape)
        in_specs.append(
            pl.BlockSpec(block, lambda i, p, a=at, n=len(block): tuple(p[a + k] for k in range(n)))
        )
        out_specs.append(pl.BlockSpec(shape, lambda i, p: (0, 0)))
    arrays = [array for array, _, _ in requests]
    return pl.pallas_call(
        lambda *refs: copy_kernel(len(arrays), *refs),
        grid_spec=pltpu.PrefetchScalarGridSpec(
            num_scalar_prefetch=1,
            grid=(1,),
            in_specs=in_specs + [ANYWHERE] * len(earlier),
            out_specs=out_specs,
        ),
        out_shape=[jax.ShapeDtypeStruct(shape, BF16) for shape in shapes],
        compiler_params=pltpu.CompilerParams(vmem_limit_bytes=32 * 1024 * 1024),
        cost_estimate=NO_COST,
    )(jnp.stack([jnp.int32(place) for place in places]), *arrays, *earlier)


def choose_kernel(flag_ref, first_ref, second_ref, *refs):
    refs[-1][...] = jnp.where(flag_ref[0] == 1, first_ref[...], second_ref[...])


def chosen(flag, first, second, earlier):
    tiled = pl.BlockSpec((first.shape[0] // 2, first.shape[1]), lambda i: (i, 0))
    return pl.pallas_call(
        choose_kernel,
        grid=(2,),
        out_shape=jax.ShapeDtypeStruct(first.shape, first.dtype),
        in_specs=[pl.BlockSpec(memory_space=pltpu.SMEM), tiled, tiled] + [ANYWHERE] * len(earlier),
        out_specs=tiled,
        compiler_params=pltpu.CompilerParams(vmem_limit_bytes=32 * 1024 * 1024),
        cost_estimate=NO_COST,
    )(flag, first, second, *earlier)


def member_blocks(blocks, member, group, earlier):
    _, rows, width = blocks.shape
    return copied(
        [(blocks, (None, rows, width), [member ^ other, 0, 0]) for other in range(1, group)],
        earlier,
    )


def exchange_members(blocks, sent, bits, earlier):
    held = [[blocks]] + [[part] for part in sent]
    for bit in reversed(range(bits)):
        half = 1 << bit
        for passed in held[half:]:
            if earlier:
                passed[1:] = [copied([(part, part.shape, [0, 0])], earlier)[0] for part in passed[1:]]
        held = [
            kept + [swapped(part, half) for part in passed]
            for kept, passed in zip(held[:half], held[half:])
        ]
    first, *others = held[0]
    return [first] + [part[None] for part in others]


def member_order(bits):
    order = [0]
    for bit in reversed(range(bits)):
        order = order + [other ^ (1 << bit) for other in order]
    return order


def down_pairs(bit, group):
    mask = 1 << bit
    return [
        (source, source + mask)
        for source in range(lax.axis_size("tok"))
        if source % group % (2 * mask) == 0
    ]


def share_of_first(lower, upper, member, group, bits):
    arrived = None
    for bit in reversed(range(bits)):
        moved = lax.ppermute(upper, "tok", down_pairs(bit, group))
        arrived = moved if arrived is None else arrived
        blocks = jnp.where(member >> bit & 1 == 1, moved, lower)
        half = blocks.shape[0] // 2
        lower, upper = blocks[:half], blocks[half:]
    return blocks, arrived


def count_rows(number, row, width):
    index = lax.broadcasted_iota(jnp.int32, (16, width), 0)
    rest = jnp.where(index == row + 1, number % 256, 0)
    return jnp.where(index == row, number // 256, rest).astype(BF16)


def local(grad_rows, routes, counts, factor_old, damping, weight_grad):
    group = lax.axis_size("tok") // 2
    bits = group.bit_length() - 1
    position = lax.axis_index("tok")
    expert = position // group
    member = position % group
    column = lax.axis_index("fac")
    tok_rows, width = grad_rows.shape
    damp = jnp.where(expert == 0, damping[0], damping[1])[None]
    order = [member ^ other for other in member_order(bits)]

    side = LEAD // 2
    halves = [(factor_old, (side, width), [place, 0]) for place in range(2)]
    lead_factor, arrived = share_of_first(*copied(halves, []), member, group, bits)

    live = jnp.arange(tok_rows) < counts[0]
    named = routes[:, 0]
    own = live & (named == expert)
    away = live & (named != expert)
    flags = jnp.stack([own, away])
    ranks = jnp.cumsum(flags.astype(jnp.int32), 1) - 1
    picker = (ranks[:, None, :] == jnp.arange(CAP)[None, :, None]) & flags[:, None, :]
    packed = jnp.dot(
        picker.reshape(2 * CAP, tok_rows).astype(BF16), grad_rows, preferred_element_type=F32
    ).astype(BF16)
    tally = jnp.sum(flags.astype(jnp.int32), 1)
    front = swapped(
        jnp.concatenate([packed[CAP:, :LEAD], count_rows(tally[1], 2, LEAD)], 0), group
    )
    first_part = jnp.concatenate(
        [
            packed[:CAP, :LEAD],
            front[:CAP],
            lead_factor[:, :LEAD],
            front[CAP:] + count_rows(tally[0], 0, LEAD),
        ],
        0,
    )
    incoming = swapped(after(packed[CAP:], front), group)
    outgoing = jnp.concatenate([packed[:CAP], lead_factor], 0)
    quarter = jnp.concatenate([packed[:CAP], incoming, lead_factor], 0)

    grad_cols = weight_grad.shape[1]
    near = copied([(weight_grad, (LEAD, grad_cols), [0, 0])], [arrived])[0]
    across_own = gather_members(outgoing, bits)
    across_other = gather_members(incoming, bits)
    for bit in reversed(range(bits)):
        moved = lax.ppermute(near, "tok", down_pairs(bit, group))
        flag = (member >> bit & 1)[None]
        if bit:
            near = chosen(flag, moved, near, [across_own[1]])

    ends = [end for end in (LEAD, 2 * LEAD, 2 * LEAD + ROWS) if end < width] + [width]
    chunks = list(zip([0, *ends], ends))
    rows = quarter.shape[0]
    later = [
        (quarter, (rows, end - begin), [0, begin // (end - begin)]) for begin, end in chunks[1:]
    ]
    parts = [first_part, *copied(later, [across_own[1]])]
    spread = [lax.all_gather(part, "fac") for part in parts]
    rows = first_part.shape[0]
    lead = copied([(spread[0], (None, rows, LEAD), [0, 0, 0])], parts[1:])[0]
    lead = gather_members(lead, bits)
    sent = member_blocks(spread[0], member, group, [lead[1]])

    slots = jnp.stack([member, column, member * width] + order).astype(jnp.int32)
    lower, inverse, share = factor_lead(
        slots, damp, factor_old[:LEAD, :LEAD], lead, sent[:1]
    )
    panel, lead_stack, across_stack = panel_columns(
        slots, share, inverse, lead, across_own, across_other
    )
    token = panel
    results = []
    for number, (begin, _) in enumerate(chunks):
        ahead = number + 1 < len(chunks)
        gate = [token] if number else []
        if ahead:
            coming = member_blocks(spread[number + 1], member, group, [token])
            gate = coming[:1] if number else []
        pieces = exchange_members(spread[number], sent, bits, gate)
        if number == 0:
            high, low = solve_lead(flag, inverse, moved, near, coming[:1])
        slots = [member, column, member * width + begin] + order + [member] + [0] * (group - 1)
        assert len(slots) == PLACES + 2 * group
        *results, token = finish_rows(
            begin,
            jnp.stack([jnp.int32(slot) for slot in slots]),
            damp,
            share,
            factor_old,
            weight_grad,
            panel,
            inverse,
            lower,
            high,
            low,
            lead_stack,
            across_stack,
            pieces,
            results,
            coming[:1] if ahead else [],
        )
        sent = coming
    return tuple(results)


def solution(mesh):
    placed = (P("tok", "fac"), P("tok", None), P("tok"), P("tok", "fac"), P(), P("tok", "fac"))
    return jax.shard_map(
        local,
        mesh=mesh,
        in_specs=placed,
        out_specs=(P("tok", "fac"), P("tok", "fac"), P("tok", "fac")),
        check_vma=False,
    )
```

```python
import jax
import jax.numpy as jnp
from jax import lax
from jax.experimental import pallas as pl
from jax.experimental.pallas import tpu as pltpu
from jax.sharding import PartitionSpec as P

CAP = 320
LEAD = 512
TILE = 128
GROUP = 8
ROWS = 256
COLS = 512
PLACES = 3
VMEM_BYTES = 60 * 1024 * 1024
ANYWHERE = pl.BlockSpec(memory_space=pl.ANY)
NO_COST = pl.CostEstimate(flops=1, bytes_accessed=1, transcendentals=0)
DECAY = 0.8

HIGHEST = lax.Precision.HIGHEST
BF16 = jnp.bfloat16
F32 = jnp.float32


def dot_t(left, right, precision=None):
    return lax.dot_general(
        left, right, (((0,), (0,)), ((), ())), precision=precision, preferred_element_type=F32
    )


def split(value):
    high = value.astype(BF16)
    return high, (value - high.astype(F32)).astype(BF16)


def dot_split(left, right, contract):
    (left_high, left_low), (right_high, right_low) = split(left), split(right)
    product = lambda a, b: lax.dot_general(
        a, b, (contract, ((), ())), preferred_element_type=F32
    )
    return product(left_high, right_high) + (
        product(left_high, right_low) + product(left_low, right_high)
    )


def splat(rows, lane):
    return jnp.broadcast_to(rows[:, lane : lane + 1], rows.shape)


def eliminate_tile(rows):
    lanes = lax.broadcasted_iota(jnp.int32, (GROUP, TILE), 1)
    subs = lax.broadcasted_iota(jnp.int32, (GROUP, TILE), 0)
    upper, inverse = [], []
    for step in range(TILE // GROUP):
        base = step * GROUP
        inside = (lanes >= base) & (lanes < base + GROUP)
        block = rows[step]
        first = [jnp.broadcast_to(block[t : t + 1, :], (GROUP, TILE)) for t in range(GROUP)]
        second = [
            jnp.where(inside, jnp.where(lanes == base + t, 1.0, 0.0), first[t])
            for t in range(GROUP)
        ]
        pivot = [
            [splat(first[t], base + u) if u >= t else None for u in range(GROUP)]
            for t in range(GROUP)
        ]
        scale = [None] * GROUP
        for t in range(GROUP):
            scale[t] = lax.rsqrt(pivot[t][t])
            for u in range(t + 1, GROUP):
                pivot[t][u] = pivot[t][u] * scale[t]
            for u in range(t + 1, GROUP):
                for w in range(u, GROUP):
                    pivot[u][w] = pivot[u][w] - pivot[t][u] * pivot[t][w]
            first[t] = first[t] * scale[t]
            second[t] = second[t] * scale[t]
            for u in range(t + 1, GROUP):
                first[u] = first[u] - pivot[t][u] * first[t]
                second[u] = second[u] - pivot[t][u] * second[t]
        solved = [None] * GROUP
        for t in reversed(range(GROUP)):
            value = second[t]
            for u in range(t + 1, GROUP):
                value = value - pivot[t][u] * solved[u]
            solved[t] = value * scale[t]
        for later in range(step + 1, TILE // GROUP):
            value = jnp.where(inside, 0.0, rows[later])
            for t in range(GROUP):
                value = value - splat(rows[later], base + t) * solved[t]
            rows[later] = value
        upper_rows, inverse_rows = first[0], second[0]
        for t in range(1, GROUP):
            upper_rows = jnp.where(subs == t, first[t], upper_rows)
            inverse_rows = jnp.where(subs == t, second[t], inverse_rows)
        upper.append(upper_rows)
        inverse.append(inverse_rows)
    return upper, inverse


def factor_kernel(count, places_ref, damp_ref, exact_ref, *refs):
    lead_refs = refs[:count]
    lower_ref, inverse_ref, share_ref, work_ref, upper_ref = refs[-5:]
    steps = LEAD // TILE
    side = LEAD // count
    marks = sum(lead[2 * CAP + side :, :].astype(F32) for lead in lead_refs)
    row = lax.broadcasted_iota(jnp.int32, marks.shape, 0)
    weight = jnp.where(row < 4, jnp.where(row % 2 == 0, 256.0, 1.0), 0.0)
    total = jnp.sum(marks * weight, axis=0, keepdims=True)[:, :1]
    share = (1.0 - DECAY) / total
    share_ref[...] = jnp.broadcast_to(share, share_ref.shape)
    for q, lead in enumerate(lead_refs):
        begin = pl.multiple_of(places_ref[PLACES + q] * side, side)
        work_ref[pl.ds(begin, side), :] = lead[2 * CAP : 2 * CAP + side, :].astype(F32)

    @pl.when((places_ref[0] == 0) & (places_ref[1] == 0))
    def _():
        work_ref[...] = exact_ref[...]

    gram = sum(dot_t(lead[: 2 * CAP, :], lead[: 2 * CAP, :]) for lead in lead_refs)
    rows = lax.broadcasted_iota(jnp.int32, (LEAD, LEAD), 0)
    cols = lax.broadcasted_iota(jnp.int32, (LEAD, LEAD), 1)
    work_ref[...] = (
        DECAY * work_ref[...] + share * gram + jnp.where(rows == cols, damp_ref[0], 0.0)
    )
    upper_ref[...] = jnp.zeros_like(upper_ref)
    inverse_ref[...] = jnp.zeros_like(inverse_ref)
    lanes = lax.broadcasted_iota(jnp.int32, (GROUP, TILE), 1)
    subs = lax.broadcasted_iota(jnp.int32, (GROUP, TILE), 0)

    def tile_step(k, carry):
        begin = pl.multiple_of(k * TILE, TILE)
        rows = [
            work_ref[pl.ds(begin + g * GROUP, GROUP), pl.ds(begin, TILE)]
            for g in range(TILE // GROUP)
        ]
        upper, inverse = eliminate_tile(rows)
        upper_tile = jnp.concatenate(
            [jnp.where(lanes >= subs + g * GROUP, part, 0.0) for g, part in enumerate(upper)], 0
        )
        inverse_tile = jnp.concatenate(
            [jnp.where(lanes <= subs + g * GROUP, part, 0.0) for g, part in enumerate(inverse)], 0
        )
        band = jnp.dot(
            inverse_tile,
            work_ref[pl.ds(begin, TILE), :],
            precision=HIGHEST,
            preferred_element_type=F32,
        )
        work_ref[pl.ds(begin, TILE), :] = band
        work_ref[pl.ds(begin, TILE), pl.ds(begin, TILE)] = inverse_tile
        upper_ref[pl.ds(begin, TILE), pl.ds(begin, TILE)] = upper_tile
        inverse_ref[pl.ds(begin, TILE), pl.ds(begin, TILE)] = inverse_tile
        for other in range(steps):

            @pl.when(other < k)
            def _():
                inverse_ref[pl.ds(begin, TILE), other * TILE : (other + 1) * TILE] = work_ref[
                    pl.ds(begin, TILE), other * TILE : (other + 1) * TILE
                ]

            @pl.when(other > k)
            def _():
                span = slice(other * TILE, (other + 1) * TILE)
                part = work_ref[pl.ds(begin, TILE), span]
                upper_ref[pl.ds(begin, TILE), span] = part
                work_ref[span, pl.ds(begin, TILE)] = jnp.zeros((TILE, TILE), F32)
                work_ref[span, :] = work_ref[span, :] - dot_t(
                    part, work_ref[pl.ds(begin, TILE), :], HIGHEST
                )

        return carry

    lax.fori_loop(0, steps, tile_step, 0)
    lower_ref[...] = upper_ref[...].T


def factor_lead(places, damp, exact, lead, earlier):
    shape = jax.ShapeDtypeStruct((LEAD, LEAD), F32)
    vmem = pl.BlockSpec(memory_space=pltpu.VMEM)
    smem = pl.BlockSpec(memory_space=pltpu.SMEM)
    return pl.pallas_call(
        lambda *refs: factor_kernel(len(lead), *refs),
        out_shape=(shape, shape, jax.ShapeDtypeStruct((GROUP, TILE), F32)),
        in_specs=[smem, smem] + [vmem] * (1 + len(lead)) + [ANYWHERE] * len(earlier),
        out_specs=(vmem, vmem, vmem),
        scratch_shapes=[pltpu.VMEM((LEAD, LEAD), F32)] * 2,
        compiler_params=pltpu.CompilerParams(vmem_limit_bytes=VMEM_BYTES),
        cost_estimate=NO_COST,
    )(places, damp, exact, *lead, *earlier)


def panel_kernel(count, places_ref, share_ref, inverse_ref, *refs):
    lead, own, other = refs[:count], refs[count : 2 * count], refs[2 * count : 3 * count]
    out_ref, lead_ref, across_ref, near_ref = refs[-4:]
    side = LEAD // count
    depth = 2 * CAP
    for q in range(count):
        across_ref[q * depth : q * depth + CAP, :] = own[q][:CAP, :]
        across_ref[q * depth + CAP : (q + 1) * depth, :] = other[q][...]
        begin = pl.multiple_of(places_ref[PLACES + q] * side, side)
        near_ref[pl.ds(begin, side), :] = own[q][CAP:, :].astype(F32)

    @pl.when(pl.program_id(0) == 0)
    def _():
        for q in range(count):
            lead_ref[q * depth : (q + 1) * depth, :] = lead[q][:depth, :]

    gram = dot_t(lead_ref[...], across_ref[...])
    beside = DECAY * near_ref[...] + share_ref[:1, :1] * gram
    out_ref[...] = dot_split(inverse_ref[...], beside, ((1,), (0,))).astype(BF16)


def panel_columns(places, share, inverse, lead, own, other):
    count = len(lead)
    width = own[0].shape[1]
    cols = COLS if width % COLS == 0 else ROWS
    tall = 2 * CAP * count
    whole = lambda height: pl.BlockSpec((height, LEAD), lambda j: (0, 0))
    tiled = lambda height: pl.BlockSpec((height, cols), lambda j: (0, j))
    return pl.pallas_call(
        lambda *refs: panel_kernel(count, *refs),
        grid=(width // cols,),
        out_shape=(
            jax.ShapeDtypeStruct((LEAD, width), BF16),
            jax.ShapeDtypeStruct((tall, LEAD), BF16),
            jax.ShapeDtypeStruct((tall, width), BF16),
        ),
        in_specs=[
            pl.BlockSpec(memory_space=pltpu.SMEM),
            pl.BlockSpec((GROUP, TILE), lambda j: (0, 0)),
            whole(LEAD),
        ]
        + [whole(lead[0].shape[0])] * count
        + [tiled(own[0].shape[0])] * count
        + [tiled(CAP)] * count,
        out_specs=(tiled(LEAD), whole(tall), tiled(tall)),
        scratch_shapes=[pltpu.VMEM((LEAD, cols), F32)],
        compiler_params=pltpu.CompilerParams(vmem_limit_bytes=VMEM_BYTES),
        cost_estimate=NO_COST,
    )(places, share, inverse, *lead, *own, *other)


def solve_kernel(flag_ref, inverse_ref, first_ref, second_ref, *refs):
    high_ref, low_ref = refs[-2:]
    values = jnp.where(flag_ref[0] == 1, first_ref[...], second_ref[...])
    high, low = split(inverse_ref[...])
    solved = jnp.dot(high, values, preferred_element_type=F32)
    solved = solved + jnp.dot(low, values, preferred_element_type=F32)
    high_ref[...], low_ref[...] = split(solved)


def solve_lead(flag, inverse, first, second, earlier):
    tiled = pl.BlockSpec((LEAD, ROWS), lambda j: (0, j))
    return pl.pallas_call(
        solve_kernel,
        grid=(first.shape[1] // ROWS,),
        out_shape=(jax.ShapeDtypeStruct(first.shape, BF16),) * 2,
        in_specs=[
            pl.BlockSpec(memory_space=pltpu.SMEM),
            pl.BlockSpec((LEAD, LEAD), lambda j: (0, 0)),
            tiled,
            tiled,
        ]
        + [ANYWHERE] * len(earlier),
        out_specs=(tiled, tiled),
        compiler_params=pltpu.CompilerParams(vmem_limit_bytes=VMEM_BYTES),
        cost_estimate=NO_COST,
    )(flag, inverse, first, second, *earlier)


def finish_kernel(
    count,
    gram_steps,
    first_chunk,
    unread,
    places_ref,
    damp_ref,
    share_ref,
    factor_ref,
    grad_ref,
    panel_ref,
    inverse_ref,
    high_ref,
    lead_ref,
    across_ref,
    *refs,
):
    if first_chunk:
        lower_ref, low_ref, *refs = refs
    mine = refs[:count]
    outs = refs[count + unread :]
    running_ref, factored_ref, precond_ref, token_ref, mine_ref, rows_ref, first_ref = outs
    j, i = pl.program_id(0), pl.program_id(1)
    member, column, base = places_ref[0], places_ref[1], places_ref[2]
    share, damp = share_ref[:1, :1], damp_ref[0]
    height, cols = running_ref.shape
    depth = 2 * CAP
    side = LEAD // count
    span = pl.ds(pl.multiple_of(i * height, height), height)
    head = (member == 0) & first_chunk

    @pl.when(j == 0)
    def _():
        token_ref[...] = jnp.zeros_like(token_ref)
        for q in range(count):
            mine_ref[span, q * depth : (q + 1) * depth] = mine[q][0, :depth, :].T
            begin = pl.multiple_of(places_ref[PLACES + q] * side, side)
            first_ref[pl.ds(begin, side), :] = mine[q][0, depth : depth + side, :].astype(F32)
        source = first_ref[...].T
        if cols == LEAD:
            source = jnp.where(column == 0, factor_ref[...], source)
        gram = jnp.dot(mine_ref[span, :], lead_ref[...], preferred_element_type=F32)
        row = base + i * height + lax.broadcasted_iota(jnp.int32, (height, LEAD), 0)
        col = lax.broadcasted_iota(jnp.int32, (height, LEAD), 1)
        source = DECAY * source + share * gram
        source = source + jnp.where(row == col, damp, 0.0)
        rows_ref[span, :] = dot_split(source, inverse_ref[...], ((1,), (1,)))

    panel = rows_ref[span, :].astype(BF16)

    @pl.when(j < gram_steps)
    def _():
        gram = jnp.dot(mine_ref[span, :], across_ref[...], preferred_element_type=F32)
        running = DECAY * factor_ref[...] + share * gram
        running_ref[...] = running
        row = base + i * height + lax.broadcasted_iota(jnp.int32, (height, cols), 0)
        col = (column * gram_steps + j) * cols + lax.broadcasted_iota(jnp.int32, (height, cols), 1)
        matrix = running + jnp.where(row == col, damp, 0.0)
        factored = matrix - jnp.dot(panel, panel_ref[...], preferred_element_type=F32)
        factored_ref[...] = jnp.where(head, 0.0, factored)

        for part in range(LEAD // cols):
            edge = slice(part * cols, (part + 1) * cols)

            @pl.when((column == 0) & (j == part))
            def _():
                factored_ref[...] = rows_ref[span, edge]

                if first_chunk:

                    @pl.when(head)
                    def _():
                        factored_ref[...] = lower_ref[span, edge]

    product = jnp.dot(panel, high_ref[...], preferred_element_type=F32)
    precond_ref[...] = grad_ref[...].astype(F32) - product

    if first_chunk:

        @pl.when(head)
        def _():
            precond_ref[...] = high_ref[span, :].astype(F32) + low_ref[span, :].astype(F32)


def finish_rows(
    begin, places, damp, share, factor, grad, panel, inverse, lower, high, low,
    lead, across, mine, results, earlier,
):
    count = len(mine)
    deep, rows = mine[0].shape[1:]
    width, grad_cols = factor.shape[0], grad.shape[1]
    tall = lead.shape[0]
    height = min(rows, COLS)
    tiles = rows // height
    start = begin // height
    cols = COLS if width % COLS == 0 else ROWS
    gram_steps, steps = width // cols, grad_cols // cols
    assert steps >= gram_steps and rows % height == 0 and begin % height == 0

    def mine_spec(q):
        return pl.BlockSpec(
            (1, deep, height),
            lambda j, i, p: (p[PLACES + count + q], 0, jnp.where(j == 0, i, tiles - 1)),
        )

    def gram_col(j):
        return jnp.minimum(j, gram_steps - 1)

    def gram_tile(j, i, p):
        return (start + jnp.where(j < gram_steps, i, tiles - 1), gram_col(j))

    grad_spec = pl.BlockSpec((height, cols), lambda j, i, p: (start + i, j))
    factor_spec = pl.BlockSpec((height, cols), gram_tile)
    lead_whole = pl.BlockSpec((LEAD, LEAD), lambda j, i, p: (0, 0))
    small = pl.BlockSpec((GROUP, TILE), lambda j, i, p: (0, 0))
    in_specs = [
        pl.BlockSpec(memory_space=pltpu.SMEM),
        small,
        factor_spec,
        grad_spec,
        pl.BlockSpec((LEAD, cols), lambda j, i, p: (0, gram_col(j))),
        lead_whole,
        pl.BlockSpec((LEAD, cols), lambda j, i, p: (0, j)),
        pl.BlockSpec((tall, LEAD), lambda j, i, p: (0, 0)),
        pl.BlockSpec((tall, cols), lambda j, i, p: (0, gram_col(j))),
    ]
    operands = [damp, share, factor, grad, panel, inverse, high, lead, across]
    if begin == 0:
        in_specs += [lead_whole, pl.BlockSpec((LEAD, cols), lambda j, i, p: (0, j))]
        operands += [lower, low]
    in_specs += [mine_spec(q) for q in range(count)]
    operands += mine
    aliases = {1 + len(operands) + k: k for k in range(len(results))}
    operands += [*results, *earlier]
    unread = len(results) + len(earlier)
    in_specs += [ANYWHERE] * unread
    return pl.pallas_call(
        lambda *refs: finish_kernel(count, gram_steps, begin == 0, unread, *refs),
        grid_spec=pltpu.PrefetchScalarGridSpec(
            num_scalar_prefetch=1,
            grid=(steps, tiles),
            in_specs=in_specs,
            out_specs=(factor_spec, factor_spec, grad_spec, small),
            scratch_shapes=[
                pltpu.VMEM((rows, tall), BF16),
                pltpu.VMEM((rows, LEAD), F32),
                pltpu.VMEM((LEAD, height), F32),
            ],
        ),
        out_shape=(
            jax.ShapeDtypeStruct(factor.shape, F32),
            jax.ShapeDtypeStruct(factor.shape, F32),
            jax.ShapeDtypeStruct(grad.shape, F32),
            jax.ShapeDtypeStruct((GROUP, TILE), F32),
        ),
        input_output_aliases=aliases,
        compiler_params=pltpu.CompilerParams(vmem_limit_bytes=VMEM_BYTES),
        cost_estimate=NO_COST,
    )(places, *operands)


def swapped(value, mask):
    size = lax.axis_size("tok")
    return lax.ppermute(value, "tok", [(source, source ^ mask) for source in range(size)])


def gather_members(value, bits):
    pieces = [value]
    for bit in reversed(range(bits)):
        pieces = pieces + [swapped(piece, 1 << bit) for piece in pieces]
    return pieces


def copy_kernel(count, places_ref, *refs):
    for source, out in zip(refs[:count], refs[-count:]):
        out[...] = source[...].astype(BF16)


def copied(requests, earlier):
    in_specs, out_specs, shapes, places = [], [], [], []
    for array, block, place in requests:
        at = len(places)
        places += place
        shape = tuple(size for size in block if size is not None)
        shapes.append(shape)
        in_specs.append(
            pl.BlockSpec(block, lambda i, p, a=at, n=len(block): tuple(p[a + k] for k in range(n)))
        )
        out_specs.append(pl.BlockSpec(shape, lambda i, p: (0, 0)))
    arrays = [array for array, _, _ in requests]
    return pl.pallas_call(
        lambda *refs: copy_kernel(len(arrays), *refs),
        grid_spec=pltpu.PrefetchScalarGridSpec(
            num_scalar_prefetch=1,
            grid=(1,),
            in_specs=in_specs + [ANYWHERE] * len(earlier),
            out_specs=out_specs,
        ),
        out_shape=[jax.ShapeDtypeStruct(shape, BF16) for shape in shapes],
        compiler_params=pltpu.CompilerParams(vmem_limit_bytes=VMEM_BYTES),
        cost_estimate=NO_COST,
    )(jnp.stack([jnp.int32(place) for place in places]), *arrays, *earlier)


def choose_kernel(flag_ref, first_ref, second_ref, *refs):
    refs[-1][...] = jnp.where(flag_ref[0] == 1, first_ref[...], second_ref[...])


def chosen(flag, first, second, earlier):
    tiled = pl.BlockSpec((first.shape[0] // 2, first.shape[1]), lambda i: (i, 0))
    return pl.pallas_call(
        choose_kernel,
        grid=(2,),
        out_shape=jax.ShapeDtypeStruct(first.shape, first.dtype),
        in_specs=[pl.BlockSpec(memory_space=pltpu.SMEM), tiled, tiled] + [ANYWHERE] * len(earlier),
        out_specs=tiled,
        compiler_params=pltpu.CompilerParams(vmem_limit_bytes=VMEM_BYTES),
        cost_estimate=NO_COST,
    )(flag, first, second, *earlier)


def member_blocks(blocks, member, group, earlier):
    _, rows, width = blocks.shape
    return copied(
        [(blocks, (None, rows, width), [member ^ other, 0, 0]) for other in range(1, group)],
        earlier,
    )


def exchange_members(blocks, sent, bits, earlier):
    held = [[blocks]] + [[part] for part in sent]
    for bit in reversed(range(bits)):
        half = 1 << bit
        for passed in held[half:]:
            passed[1:] = [copied([(part, part.shape, [0, 0])], earlier)[0] for part in passed[1:]]
        held = [
            kept + [swapped(part, half) for part in passed]
            for kept, passed in zip(held[:half], held[half:])
        ]
    first, *others = held[0]
    return [first] + [part[None] for part in others]


def member_order(bits):
    order = [0]
    for bit in reversed(range(bits)):
        order = order + [other ^ (1 << bit) for other in order]
    return order


def down_pairs(bit, group):
    mask = 1 << bit
    return [
        (source, source + mask)
        for source in range(lax.axis_size("tok"))
        if source % group % (2 * mask) == 0
    ]


def share_of_first(lower, upper, member, group, bits):
    arrived = None
    for bit in reversed(range(bits)):
        moved = lax.ppermute(upper, "tok", down_pairs(bit, group))
        arrived = moved if arrived is None else arrived
        blocks = jnp.where(member >> bit & 1 == 1, moved, lower)
        half = blocks.shape[0] // 2
        lower, upper = blocks[:half], blocks[half:]
    return blocks, arrived


def count_rows(number, row, width):
    index = lax.broadcasted_iota(jnp.int32, (16, width), 0)
    rest = jnp.where(index == row + 1, number % 256, 0)
    return jnp.where(index == row, number // 256, rest).astype(BF16)


def local(grad_rows, routes, counts, factor_old, damping, weight_grad):
    group = lax.axis_size("tok") // 2
    bits = group.bit_length() - 1
    position = lax.axis_index("tok")
    expert = position // group
    member = position % group
    column = lax.axis_index("fac")
    tok_rows, width = grad_rows.shape
    damp = jnp.where(expert == 0, damping[0], damping[1])[None]
    order = [member ^ other for other in member_order(bits)]

    side = LEAD // 2
    halves = [(factor_old, (side, width), [place, 0]) for place in range(2)]
    lead_factor, arrived = share_of_first(*copied(halves, []), member, group, bits)

    live = jnp.arange(tok_rows) < counts[0]
    named = routes[:, 0]
    own = live & (named == expert)
    away = live & (named != expert)
    flags = jnp.stack([own, away])
    ranks = jnp.cumsum(flags.astype(jnp.int32), 1) - 1
    picker = (ranks[:, None, :] == jnp.arange(CAP)[None, :, None]) & flags[:, None, :]
    packed = jnp.dot(
        picker.reshape(2 * CAP, tok_rows).astype(BF16), grad_rows, preferred_element_type=F32
    ).astype(BF16)
    tally = jnp.sum(flags.astype(jnp.int32), 1)
    front = swapped(
        jnp.concatenate([packed[CAP:, :LEAD], count_rows(tally[1], 2, LEAD)], 0), group
    )
    first_part = jnp.concatenate(
        [
            packed[:CAP, :LEAD],
            front[:CAP],
            lead_factor[:, :LEAD],
            front[CAP:] + count_rows(tally[0], 0, LEAD),
        ],
        0,
    )
    grad_cols = weight_grad.shape[1]
    near = copied([(weight_grad, (LEAD, grad_cols), [0, 0])], [arrived])[0]
    away_rows = copied([(packed, (CAP, width), [1, 0])], [front, near])[0]
    incoming = swapped(away_rows, group)
    outgoing = jnp.concatenate([packed[:CAP], lead_factor], 0)
    quarter = jnp.concatenate([packed[:CAP], incoming, lead_factor], 0)
    across_own = gather_members(outgoing, bits)
    across_other = gather_members(incoming, bits)
    for bit in reversed(range(bits)):
        moved = lax.ppermute(near, "tok", down_pairs(bit, group))
        flag = (member >> bit & 1)[None]
        if bit:
            near = chosen(flag, moved, near, [across_own[1]])

    ends = [end for end in (LEAD, 2 * LEAD, 2 * LEAD + ROWS) if end < width] + [width]
    chunks = list(zip([0, *ends], ends))
    rows = quarter.shape[0]
    later = [
        (quarter, (rows, end - begin), [0, begin // (end - begin)]) for begin, end in chunks[1:]
    ]
    parts = [first_part, *copied(later, [across_own[1]])]
    spread = [lax.all_gather(part, "fac") for part in parts]
    rows = first_part.shape[0]
    lead = copied([(spread[0], (None, rows, LEAD), [0, 0, 0])], parts[1:])[0]
    lead = gather_members(lead, bits)
    sent = member_blocks(spread[0], member, group, [lead[1]])

    slots = jnp.stack([member, column, member * width] + order).astype(jnp.int32)
    lower, inverse, share = factor_lead(
        slots, damp, factor_old[:LEAD, :LEAD], lead, sent[:1]
    )
    panel, lead_stack, across_stack = panel_columns(
        slots, share, inverse, lead, across_own, across_other
    )
    token = panel
    results = []
    for number, (begin, _) in enumerate(chunks):
        ahead = number + 1 < len(chunks)
        if ahead:
            coming = member_blocks(spread[number + 1], member, group, [token])
        pieces = exchange_members(
            spread[number], sent, bits, coming[:1] if ahead else [token]
        )
        if number == 0:
            high, low = solve_lead(flag, inverse, moved, near, coming[:1])
        slots = [member, column, member * width + begin] + order + [member] + [0] * (group - 1)
        assert len(slots) == PLACES + 2 * group
        *results, token = finish_rows(
            begin,
            jnp.stack([jnp.int32(slot) for slot in slots]),
            damp,
            share,
            factor_old,
            weight_grad,
            panel,
            inverse,
            lower,
            high,
            low,
            lead_stack,
            across_stack,
            pieces,
            results,
            coming[:1] if ahead else [],
        )
        sent = coming
    return tuple(results)


def solution(mesh):
    placed = (P("tok", "fac"), P("tok", None), P("tok"), P("tok", "fac"), P(), P("tok", "fac"))
    return jax.shard_map(
        local,
        mesh=mesh,
        in_specs=placed,
        out_specs=(P("tok", "fac"), P("tok", "fac"), P("tok", "fac")),
        check_vma=False,
    )
```

```python
import jax
import jax.numpy as jnp
from jax import lax
from jax.experimental import pallas as pl
from jax.experimental.pallas import tpu as pltpu
from jax.sharding import PartitionSpec as P

CAP = 320
LEAD = 512
TILE = 128
GROUP = 8
ROWS = 256
COLS = 512
PLACES = 3
VMEM_BYTES = 60 * 1024 * 1024
ANYWHERE = pl.BlockSpec(memory_space=pl.ANY)
NO_COST = pl.CostEstimate(flops=1, bytes_accessed=1, transcendentals=0)
DECAY = 0.8

HIGHEST = lax.Precision.HIGHEST
BF16 = jnp.bfloat16
F32 = jnp.float32


def dot_t(left, right, precision=None):
    return lax.dot_general(
        left, right, (((0,), (0,)), ((), ())), precision=precision, preferred_element_type=F32
    )


def split(value):
    high = value.astype(BF16)
    return high, (value - high.astype(F32)).astype(BF16)


def dot_split(left, right, contract):
    (left_high, left_low), (right_high, right_low) = split(left), split(right)
    product = lambda a, b: lax.dot_general(
        a, b, (contract, ((), ())), preferred_element_type=F32
    )
    return product(left_high, right_high) + (
        product(left_high, right_low) + product(left_low, right_high)
    )


def splat(rows, lane):
    return jnp.broadcast_to(rows[:, lane : lane + 1], rows.shape)


def eliminate_tile(rows):
    lanes = lax.broadcasted_iota(jnp.int32, (GROUP, TILE), 1)
    subs = lax.broadcasted_iota(jnp.int32, (GROUP, TILE), 0)
    upper, inverse = [], []
    for step in range(TILE // GROUP):
        base = step * GROUP
        inside = (lanes >= base) & (lanes < base + GROUP)
        block = rows[step]
        first = [jnp.broadcast_to(block[t : t + 1, :], (GROUP, TILE)) for t in range(GROUP)]
        second = [
            jnp.where(inside, jnp.where(lanes == base + t, 1.0, 0.0), first[t])
            for t in range(GROUP)
        ]
        pivot = [
            [splat(first[t], base + u) if u >= t else None for u in range(GROUP)]
            for t in range(GROUP)
        ]
        scale = [None] * GROUP
        for t in range(GROUP):
            scale[t] = lax.rsqrt(pivot[t][t])
            for u in range(t + 1, GROUP):
                pivot[t][u] = pivot[t][u] * scale[t]
            for u in range(t + 1, GROUP):
                for w in range(u, GROUP):
                    pivot[u][w] = pivot[u][w] - pivot[t][u] * pivot[t][w]
            first[t] = first[t] * scale[t]
            second[t] = second[t] * scale[t]
            for u in range(t + 1, GROUP):
                first[u] = first[u] - pivot[t][u] * first[t]
                second[u] = second[u] - pivot[t][u] * second[t]
        solved = [None] * GROUP
        for t in reversed(range(GROUP)):
            value = second[t]
            for u in range(t + 1, GROUP):
                value = value - pivot[t][u] * solved[u]
            solved[t] = value * scale[t]
        for later in range(step + 1, TILE // GROUP):
            value = jnp.where(inside, 0.0, rows[later])
            for t in range(GROUP):
                value = value - splat(rows[later], base + t) * solved[t]
            rows[later] = value
        upper_rows, inverse_rows = first[0], second[0]
        for t in range(1, GROUP):
            upper_rows = jnp.where(subs == t, first[t], upper_rows)
            inverse_rows = jnp.where(subs == t, second[t], inverse_rows)
        upper.append(upper_rows)
        inverse.append(inverse_rows)
    return upper, inverse


def factor_kernel(count, places_ref, damp_ref, exact_ref, *refs):
    lead_refs = refs[:count]
    lower_ref, inverse_ref, share_ref, work_ref, upper_ref = refs[-5:]
    steps = LEAD // TILE
    side = LEAD // count
    marks = sum(lead[2 * CAP + side :, :].astype(F32) for lead in lead_refs)
    row = lax.broadcasted_iota(jnp.int32, marks.shape, 0)
    weight = jnp.where(row < 4, jnp.where(row % 2 == 0, 256.0, 1.0), 0.0)
    total = jnp.sum(marks * weight, axis=0, keepdims=True)[:, :1]
    share = (1.0 - DECAY) / total
    share_ref[...] = jnp.broadcast_to(share, share_ref.shape)
    for q, lead in enumerate(lead_refs):
        begin = pl.multiple_of(places_ref[PLACES + q] * side, side)
        work_ref[pl.ds(begin, side), :] = lead[2 * CAP : 2 * CAP + side, :].astype(F32)

    @pl.when((places_ref[0] == 0) & (places_ref[1] == 0))
    def _():
        work_ref[...] = exact_ref[...]

    gram = sum(dot_t(lead[: 2 * CAP, :], lead[: 2 * CAP, :]) for lead in lead_refs)
    rows = lax.broadcasted_iota(jnp.int32, (LEAD, LEAD), 0)
    cols = lax.broadcasted_iota(jnp.int32, (LEAD, LEAD), 1)
    work_ref[...] = (
        DECAY * work_ref[...] + share * gram + jnp.where(rows == cols, damp_ref[0], 0.0)
    )
    upper_ref[...] = jnp.zeros_like(upper_ref)
    inverse_ref[...] = jnp.zeros_like(inverse_ref)
    lanes = lax.broadcasted_iota(jnp.int32, (GROUP, TILE), 1)
    subs = lax.broadcasted_iota(jnp.int32, (GROUP, TILE), 0)

    def tile_step(k, carry):
        begin = pl.multiple_of(k * TILE, TILE)
        rows = [
            work_ref[pl.ds(begin + g * GROUP, GROUP), pl.ds(begin, TILE)]
            for g in range(TILE // GROUP)
        ]
        upper, inverse = eliminate_tile(rows)
        upper_tile = jnp.concatenate(
            [jnp.where(lanes >= subs + g * GROUP, part, 0.0) for g, part in enumerate(upper)], 0
        )
        inverse_tile = jnp.concatenate(
            [jnp.where(lanes <= subs + g * GROUP, part, 0.0) for g, part in enumerate(inverse)], 0
        )
        band = jnp.dot(
            inverse_tile,
            work_ref[pl.ds(begin, TILE), :],
            precision=HIGHEST,
            preferred_element_type=F32,
        )
        work_ref[pl.ds(begin, TILE), :] = band
        work_ref[pl.ds(begin, TILE), pl.ds(begin, TILE)] = inverse_tile
        upper_ref[pl.ds(begin, TILE), pl.ds(begin, TILE)] = upper_tile
        inverse_ref[pl.ds(begin, TILE), pl.ds(begin, TILE)] = inverse_tile
        for other in range(steps):

            @pl.when(other < k)
            def _():
                inverse_ref[pl.ds(begin, TILE), other * TILE : (other + 1) * TILE] = work_ref[
                    pl.ds(begin, TILE), other * TILE : (other + 1) * TILE
                ]

            @pl.when(other > k)
            def _():
                span = slice(other * TILE, (other + 1) * TILE)
                part = work_ref[pl.ds(begin, TILE), span]
                upper_ref[pl.ds(begin, TILE), span] = part
                work_ref[span, pl.ds(begin, TILE)] = jnp.zeros((TILE, TILE), F32)
                work_ref[span, :] = work_ref[span, :] - dot_t(
                    part, work_ref[pl.ds(begin, TILE), :], HIGHEST
                )

        return carry

    lax.fori_loop(0, steps, tile_step, 0)
    lower_ref[...] = upper_ref[...].T


def factor_lead(places, damp, exact, lead, earlier):
    shape = jax.ShapeDtypeStruct((LEAD, LEAD), F32)
    vmem = pl.BlockSpec(memory_space=pltpu.VMEM)
    smem = pl.BlockSpec(memory_space=pltpu.SMEM)
    return pl.pallas_call(
        lambda *refs: factor_kernel(len(lead), *refs),
        out_shape=(shape, shape, jax.ShapeDtypeStruct((GROUP, TILE), F32)),
        in_specs=[smem, smem] + [vmem] * (1 + len(lead)) + [ANYWHERE] * len(earlier),
        out_specs=(vmem, vmem, vmem),
        scratch_shapes=[pltpu.VMEM((LEAD, LEAD), F32)] * 2,
        compiler_params=pltpu.CompilerParams(vmem_limit_bytes=VMEM_BYTES),
        cost_estimate=NO_COST,
    )(places, damp, exact, *lead, *earlier)


def panel_kernel(count, places_ref, share_ref, inverse_ref, *refs):
    lead, own, other = refs[:count], refs[count : 2 * count], refs[2 * count : 3 * count]
    out_ref, lead_ref, across_ref, near_ref = refs[-4:]
    side = LEAD // count
    depth = 2 * CAP
    for q in range(count):
        across_ref[q * depth : q * depth + CAP, :] = own[q][:CAP, :]
        across_ref[q * depth + CAP : (q + 1) * depth, :] = other[q][...]
        begin = pl.multiple_of(places_ref[PLACES + q] * side, side)
        near_ref[pl.ds(begin, side), :] = own[q][CAP:, :].astype(F32)

    @pl.when(pl.program_id(0) == 0)
    def _():
        for q in range(count):
            lead_ref[q * depth : (q + 1) * depth, :] = lead[q][:depth, :]

    gram = dot_t(lead_ref[...], across_ref[...])
    beside = DECAY * near_ref[...] + share_ref[:1, :1] * gram
    out_ref[...] = dot_split(inverse_ref[...], beside, ((1,), (0,))).astype(BF16)


def panel_columns(places, share, inverse, lead, own, other):
    count = len(lead)
    width = own[0].shape[1]
    cols = COLS if width % COLS == 0 else ROWS
    tall = 2 * CAP * count
    whole = lambda height: pl.BlockSpec((height, LEAD), lambda j: (0, 0))
    tiled = lambda height: pl.BlockSpec((height, cols), lambda j: (0, j))
    return pl.pallas_call(
        lambda *refs: panel_kernel(count, *refs),
        grid=(width // cols,),
        out_shape=(
            jax.ShapeDtypeStruct((LEAD, width), BF16),
            jax.ShapeDtypeStruct((tall, LEAD), BF16),
            jax.ShapeDtypeStruct((tall, width), BF16),
        ),
        in_specs=[
            pl.BlockSpec(memory_space=pltpu.SMEM),
            pl.BlockSpec((GROUP, TILE), lambda j: (0, 0)),
            whole(LEAD),
        ]
        + [whole(lead[0].shape[0])] * count
        + [tiled(own[0].shape[0])] * count
        + [tiled(CAP)] * count,
        out_specs=(tiled(LEAD), whole(tall), tiled(tall)),
        scratch_shapes=[pltpu.VMEM((LEAD, cols), F32)],
        compiler_params=pltpu.CompilerParams(vmem_limit_bytes=VMEM_BYTES),
        cost_estimate=NO_COST,
    )(places, share, inverse, *lead, *own, *other)


def solve_kernel(flag_ref, inverse_ref, first_ref, second_ref, *refs):
    high_ref, low_ref, parts_ref = refs

    @pl.when(pl.program_id(0) == 0)
    def _():
        parts_ref[0], parts_ref[1] = split(inverse_ref[...])

    values = jnp.where(flag_ref[0] == 1, first_ref[...], second_ref[...])
    solved = jnp.dot(parts_ref[0], values, preferred_element_type=F32)
    solved = solved + jnp.dot(parts_ref[1], values, preferred_element_type=F32)
    high_ref[...], low_ref[...] = split(solved)


def solve_lead(flag, inverse, first, second):
    tiled = pl.BlockSpec((LEAD, COLS), lambda j: (0, j))
    return pl.pallas_call(
        solve_kernel,
        grid=(first.shape[1] // COLS,),
        out_shape=(jax.ShapeDtypeStruct(first.shape, BF16),) * 2,
        in_specs=[
            pl.BlockSpec(memory_space=pltpu.SMEM),
            pl.BlockSpec((LEAD, LEAD), lambda j: (0, 0)),
            tiled,
            tiled,
        ],
        out_specs=(tiled, tiled),
        scratch_shapes=[pltpu.VMEM((2, LEAD, LEAD), BF16)],
        compiler_params=pltpu.CompilerParams(vmem_limit_bytes=VMEM_BYTES),
        cost_estimate=NO_COST,
    )(flag, inverse, first, second)


def finish_kernel(
    count,
    gram_steps,
    begin,
    unread,
    places_ref,
    damp_ref,
    share_ref,
    factor_ref,
    grad_ref,
    panel_ref,
    inverse_ref,
    high_ref,
    lead_ref,
    across_ref,
    *refs,
):
    first_chunk = begin == 0
    if first_chunk:
        lower_ref, low_ref, *refs = refs
    mine = refs[:count]
    outs = refs[count + unread :]
    running_ref, factored_ref, precond_ref, token_ref, mine_ref, rows_ref, first_ref = outs
    j, i = pl.program_id(0), pl.program_id(1)
    member, column, base = places_ref[0], places_ref[1], places_ref[2] + begin
    share, damp = share_ref[:1, :1], damp_ref[0]
    height, cols = running_ref.shape
    depth = 2 * CAP
    side = LEAD // count
    span = pl.ds(pl.multiple_of(i * height, height), height)
    head = (member == 0) & first_chunk

    @pl.when(j == 0)
    def _():
        token_ref[...] = jnp.zeros_like(token_ref)
        for q in range(count):
            mine_ref[span, q * depth : (q + 1) * depth] = mine[q][0, :depth, :].T
            place = pl.multiple_of(places_ref[PLACES + q] * side, side)
            first_ref[pl.ds(place, side), :] = mine[q][0, depth : depth + side, :].astype(F32)
        source = first_ref[...].T
        if cols == LEAD:
            source = jnp.where(column == 0, factor_ref[...], source)
        gram = jnp.dot(mine_ref[span, :], lead_ref[...], preferred_element_type=F32)
        row = base + i * height + lax.broadcasted_iota(jnp.int32, (height, LEAD), 0)
        col = lax.broadcasted_iota(jnp.int32, (height, LEAD), 1)
        source = DECAY * source + share * gram
        source = source + jnp.where(row == col, damp, 0.0)
        rows_ref[span, :] = dot_split(source, inverse_ref[...], ((1,), (1,)))

    panel = rows_ref[span, :].astype(BF16)

    @pl.when(j < gram_steps)
    def _():
        gram = jnp.dot(mine_ref[span, :], across_ref[...], preferred_element_type=F32)
        running = DECAY * factor_ref[...] + share * gram
        running_ref[...] = running
        row = base + i * height + lax.broadcasted_iota(jnp.int32, (height, cols), 0)
        col = (column * gram_steps + j) * cols + lax.broadcasted_iota(jnp.int32, (height, cols), 1)
        matrix = running + jnp.where(row == col, damp, 0.0)
        factored = matrix - jnp.dot(panel, panel_ref[...], preferred_element_type=F32)
        factored_ref[...] = jnp.where(head, 0.0, factored)

        for part in range(LEAD // cols):
            edge = slice(part * cols, (part + 1) * cols)

            @pl.when((column == 0) & (j == part))
            def _():
                factored_ref[...] = rows_ref[span, edge]

                if first_chunk:

                    @pl.when(head)
                    def _():
                        factored_ref[...] = lower_ref[span, edge]

    product = jnp.dot(panel, high_ref[...], preferred_element_type=F32)
    precond_ref[...] = grad_ref[...].astype(F32) - product

    if first_chunk:

        @pl.when(head)
        def _():
            precond_ref[...] = high_ref[span, :].astype(F32) + low_ref[span, :].astype(F32)


def finish_rows(
    begin, places, damp, share, factor, grad, panel, inverse, lower, high, low,
    lead, across, mine, results, earlier,
):
    count = len(mine)
    deep, rows = mine[0].shape[1:]
    width, grad_cols = factor.shape[0], grad.shape[1]
    tall = lead.shape[0]
    height = min(rows, COLS)
    tiles = rows // height
    start = begin // height
    cols = COLS if width % COLS == 0 else ROWS
    gram_steps, steps = width // cols, grad_cols // cols
    assert steps >= gram_steps and rows % height == 0 and begin % height == 0

    def mine_spec(q):
        return pl.BlockSpec(
            (1, deep, height),
            lambda j, i, p: (p[PLACES + count + q], 0, jnp.where(j == 0, i, tiles - 1)),
        )

    def gram_col(j):
        return jnp.minimum(j, gram_steps - 1)

    def gram_tile(j, i, p):
        return (start + jnp.where(j < gram_steps, i, tiles - 1), gram_col(j))

    grad_spec = pl.BlockSpec((height, cols), lambda j, i, p: (start + i, j))
    factor_spec = pl.BlockSpec((height, cols), gram_tile)
    lead_whole = pl.BlockSpec((LEAD, LEAD), lambda j, i, p: (0, 0))
    small = pl.BlockSpec((GROUP, TILE), lambda j, i, p: (0, 0))
    in_specs = [
        pl.BlockSpec(memory_space=pltpu.SMEM),
        small,
        factor_spec,
        grad_spec,
        pl.BlockSpec((LEAD, cols), lambda j, i, p: (0, gram_col(j))),
        lead_whole,
        pl.BlockSpec((LEAD, cols), lambda j, i, p: (0, j)),
        pl.BlockSpec((tall, LEAD), lambda j, i, p: (0, 0)),
        pl.BlockSpec((tall, cols), lambda j, i, p: (0, gram_col(j))),
    ]
    operands = [damp, share, factor, grad, panel, inverse, high, lead, across]
    if begin == 0:
        in_specs += [lead_whole, pl.BlockSpec((LEAD, cols), lambda j, i, p: (0, j))]
        operands += [lower, low]
    in_specs += [mine_spec(q) for q in range(count)]
    operands += mine
    aliases = {1 + len(operands) + k: k for k in range(len(results))}
    operands += [*results, *earlier]
    unread = len(results) + len(earlier)
    in_specs += [ANYWHERE] * unread
    return pl.pallas_call(
        lambda *refs: finish_kernel(count, gram_steps, begin, unread, *refs),
        grid_spec=pltpu.PrefetchScalarGridSpec(
            num_scalar_prefetch=1,
            grid=(steps, tiles),
            in_specs=in_specs,
            out_specs=(factor_spec, factor_spec, grad_spec, small),
            scratch_shapes=[
                pltpu.VMEM((rows, tall), BF16),
                pltpu.VMEM((rows, LEAD), F32),
                pltpu.VMEM((LEAD, height), F32),
            ],
        ),
        out_shape=(
            jax.ShapeDtypeStruct(factor.shape, F32),
            jax.ShapeDtypeStruct(factor.shape, F32),
            jax.ShapeDtypeStruct(grad.shape, F32),
            jax.ShapeDtypeStruct((GROUP, TILE), F32),
        ),
        input_output_aliases=aliases,
        compiler_params=pltpu.CompilerParams(vmem_limit_bytes=VMEM_BYTES),
        cost_estimate=NO_COST,
    )(places, *operands)


def swapped(value, mask):
    size = lax.axis_size("tok")
    return lax.ppermute(value, "tok", [(source, source ^ mask) for source in range(size)])


def gather_members(value, bits):
    pieces = [value]
    for bit in reversed(range(bits)):
        pieces = pieces + [swapped(piece, 1 << bit) for piece in pieces]
    return pieces


def copy_kernel(count, places_ref, *refs):
    for source, out in zip(refs[:count], refs[-count:]):
        out[...] = source[...].astype(BF16)


def copied(requests, earlier):
    in_specs, out_specs, shapes, places = [], [], [], []
    for array, block, place in requests:
        at = len(places)
        places += place
        shape = tuple(size for size in block if size is not None)
        shapes.append(shape)
        in_specs.append(
            pl.BlockSpec(block, lambda i, p, a=at, n=len(block): tuple(p[a + k] for k in range(n)))
        )
        out_specs.append(pl.BlockSpec(shape, lambda i, p: (0, 0)))
    arrays = [array for array, _, _ in requests]
    return pl.pallas_call(
        lambda *refs: copy_kernel(len(arrays), *refs),
        grid_spec=pltpu.PrefetchScalarGridSpec(
            num_scalar_prefetch=1,
            grid=(1,),
            in_specs=in_specs + [ANYWHERE] * len(earlier),
            out_specs=out_specs,
        ),
        out_shape=[jax.ShapeDtypeStruct(shape, BF16) for shape in shapes],
        compiler_params=pltpu.CompilerParams(vmem_limit_bytes=VMEM_BYTES),
        cost_estimate=NO_COST,
    )(jnp.stack([jnp.int32(place) for place in places]), *arrays, *earlier)


def choose_kernel(flag_ref, first_ref, second_ref, *refs):
    refs[-1][...] = jnp.where(flag_ref[0] == 1, first_ref[...], second_ref[...])


def chosen(flag, first, second, earlier):
    tiled = pl.BlockSpec((first.shape[0] // 2, first.shape[1]), lambda i: (i, 0))
    return pl.pallas_call(
        choose_kernel,
        grid=(2,),
        out_shape=jax.ShapeDtypeStruct(first.shape, first.dtype),
        in_specs=[pl.BlockSpec(memory_space=pltpu.SMEM), tiled, tiled] + [ANYWHERE] * len(earlier),
        out_specs=tiled,
        compiler_params=pltpu.CompilerParams(vmem_limit_bytes=VMEM_BYTES),
        cost_estimate=NO_COST,
    )(flag, first, second, *earlier)


def member_blocks(blocks, member, group):
    _, rows, width = blocks.shape
    return [(blocks, (None, rows, width), [member ^ other, 0, 0]) for other in range(1, group)]


def exchange_members(blocks, sent, bits, requests, earlier):
    held = [[blocks]] + [[part] for part in sent]
    copies = None
    for bit in reversed(range(bits)):
        half = 1 << bit
        arrived = [(part, part.shape, [0, 0]) for passed in held[half:] for part in passed[1:]]
        if arrived:
            passing = copied(
                requests + arrived if copies is None else arrived, earlier + held[0][1:]
            )
            if copies is None:
                copies, passing = passing[: len(requests)], passing[len(requests) :]
            for passed in held[half:]:
                count = len(passed) - 1
                passed[1:], passing = passing[:count], passing[count:]
        held = [
            kept + [swapped(part, half) for part in passed]
            for kept, passed in zip(held[:half], held[half:])
        ]
    first, *others = held[0]
    return [first] + [part[None] for part in others], copies


def member_order(bits):
    order = [0]
    for bit in reversed(range(bits)):
        order = order + [other ^ (1 << bit) for other in order]
    return order


def down_pairs(bit, group):
    mask = 1 << bit
    return [
        (source, source + mask)
        for source in range(lax.axis_size("tok"))
        if source % group % (2 * mask) == 0
    ]


def share_of_first(lower, upper, member, group, bits):
    for bit in reversed(range(bits)):
        moved = lax.ppermute(upper, "tok", down_pairs(bit, group))
        blocks = jnp.where(member >> bit & 1 == 1, moved, lower)
        half = blocks.shape[0] // 2
        lower, upper = blocks[:half], blocks[half:]
    return blocks


def count_rows(number, row, width):
    index = lax.broadcasted_iota(jnp.int32, (16, width), 0)
    rest = jnp.where(index == row + 1, number % 256, 0)
    return jnp.where(index == row, number // 256, rest).astype(BF16)


def local(grad_rows, routes, counts, factor_old, damping, weight_grad):
    group = lax.axis_size("tok") // 2
    bits = group.bit_length() - 1
    position = lax.axis_index("tok")
    expert = position // group
    member = position % group
    column = lax.axis_index("fac")
    tok_rows, width = grad_rows.shape
    damp = jnp.where(expert == 0, damping[0], damping[1])[None]
    order = [member ^ other for other in member_order(bits)]

    side = LEAD // 2
    halves = [(factor_old, (side, width), [place, 0]) for place in range(2)]
    lead_factor = share_of_first(*copied(halves, []), member, group, bits)

    live = jnp.arange(tok_rows) < counts[0]
    named = routes[:, 0]
    own = live & (named == expert)
    away = live & (named != expert)
    flags = jnp.stack([own, away])
    ranks = jnp.cumsum(flags.astype(jnp.int32), 1) - 1
    picker = (ranks[:, None, :] == jnp.arange(CAP)[None, :, None]) & flags[:, None, :]
    packed = jnp.dot(
        picker.reshape(2 * CAP, tok_rows).astype(BF16), grad_rows, preferred_element_type=F32
    ).astype(BF16)
    tally = jnp.sum(flags.astype(jnp.int32), 1)
    front = swapped(
        jnp.concatenate([packed[CAP:, :LEAD], count_rows(tally[1], 2, LEAD)], 0), group
    )
    first_part = jnp.concatenate(
        [
            packed[:CAP, :LEAD],
            front[:CAP],
            lead_factor[:, :LEAD],
            front[CAP:] + count_rows(tally[0], 0, LEAD),
        ],
        0,
    )
    away_rows = copied([(packed, (CAP, width), [1, 0])], [front])[0]
    incoming = swapped(away_rows, group)
    outgoing = jnp.concatenate([packed[:CAP], lead_factor], 0)
    quarter = jnp.concatenate([packed[:CAP], incoming, lead_factor], 0)
    across_own = gather_members(outgoing, bits)
    across_other = gather_members(incoming, bits)

    ends = [end for end in (LEAD, 2 * LEAD, 2 * LEAD + ROWS) if end < width] + [width]
    chunks = list(zip([0, *ends], ends))
    rows = quarter.shape[0]
    later = [
        (quarter, (rows, end - begin), [0, begin // (end - begin)]) for begin, end in chunks[1:]
    ]
    parts = [first_part, *copied(later, [across_own[1]])]
    spread = [lax.all_gather(part, "fac") for part in parts]
    rows = first_part.shape[0]
    earlier = [across_other[1], *parts[1:]]
    lead = copied([(spread[0], (None, rows, LEAD), [0, 0, 0])], earlier)[0]
    lead = gather_members(lead, bits)
    grad_cols = weight_grad.shape[1]
    requests = member_blocks(spread[0], member, group)
    requests += [(weight_grad, (LEAD, grad_cols), [0, 0])]
    *sent, near = copied(requests, [lead[1]])

    slots = [member, column, member * width] + order + [member] + [0] * (group - 1)
    assert len(slots) == PLACES + 2 * group
    slots = jnp.stack([jnp.int32(slot) for slot in slots])
    lower, inverse, share = factor_lead(
        slots, damp, factor_old[:LEAD, :LEAD], lead, sent[:1]
    )
    panel, lead_stack, across_stack = panel_columns(
        slots, share, inverse, lead, across_own, across_other
    )
    token = panel
    results = []
    for number, (begin, _) in enumerate(chunks):
        requests = []
        if number + 1 < len(chunks):
            requests = member_blocks(spread[number + 1], member, group)
        pieces, sent = exchange_members(spread[number], sent, bits, requests, [token])
        if number == 0:
            for bit in reversed(range(bits)):
                moved = lax.ppermute(near, "tok", down_pairs(bit, group))
                flag = (member >> bit & 1)[None]
                if bit:
                    near = chosen(flag, moved, near, sent[:1])
            high, low = solve_lead(flag, inverse, moved, near)
        *results, token = finish_rows(
            begin,
            slots,
            damp,
            share,
            factor_old,
            weight_grad,
            panel,
            inverse,
            lower,
            high,
            low,
            lead_stack,
            across_stack,
            pieces,
            results,
            sent[:1],
        )
    return tuple(results)


def solution(mesh):
    placed = (P("tok", "fac"), P("tok", None), P("tok"), P("tok", "fac"), P(), P("tok", "fac"))
    return jax.shard_map(
        local,
        mesh=mesh,
        in_specs=placed,
        out_specs=(P("tok", "fac"), P("tok", "fac"), P("tok", "fac")),
        check_vma=False,
    )
```

```python
import jax
import jax.numpy as jnp
from jax import lax
from jax.experimental import pallas as pl
from jax.experimental.pallas import tpu as pltpu
from jax.sharding import PartitionSpec as P

CAP = 320
LEAD = 512
TILE = 128
GROUP = 8
ROWS = 256
COLS = 512
PLACES = 3
VMEM_BYTES = 60 * 1024 * 1024
ANYWHERE = pl.BlockSpec(memory_space=pl.ANY)
NO_COST = pl.CostEstimate(flops=1, bytes_accessed=1, transcendentals=0)
DECAY = 0.8

HIGHEST = lax.Precision.HIGHEST
BF16 = jnp.bfloat16
F32 = jnp.float32


def dot_t(left, right, precision=None):
    return lax.dot_general(
        left, right, (((0,), (0,)), ((), ())), precision=precision, preferred_element_type=F32
    )


def split(value):
    high = value.astype(BF16)
    return high, (value - high.astype(F32)).astype(BF16)


def dot_split(left, right, contract):
    (left_high, left_low), (right_high, right_low) = split(left), split(right)
    product = lambda a, b: lax.dot_general(
        a, b, (contract, ((), ())), preferred_element_type=F32
    )
    return product(left_high, right_high) + (
        product(left_high, right_low) + product(left_low, right_high)
    )


def splat(rows, lane):
    return jnp.broadcast_to(rows[:, lane : lane + 1], rows.shape)


def eliminate_tile(rows):
    lanes = lax.broadcasted_iota(jnp.int32, (GROUP, TILE), 1)
    subs = lax.broadcasted_iota(jnp.int32, (GROUP, TILE), 0)
    upper, inverse = [], []
    for step in range(TILE // GROUP):
        base = step * GROUP
        inside = (lanes >= base) & (lanes < base + GROUP)
        block = rows[step]
        first = [jnp.broadcast_to(block[t : t + 1, :], (GROUP, TILE)) for t in range(GROUP)]
        second = [
            jnp.where(inside, jnp.where(lanes == base + t, 1.0, 0.0), first[t])
            for t in range(GROUP)
        ]
        pivot = [
            [splat(first[t], base + u) if u >= t else None for u in range(GROUP)]
            for t in range(GROUP)
        ]
        scale = [None] * GROUP
        for t in range(GROUP):
            scale[t] = lax.rsqrt(pivot[t][t])
            for u in range(t + 1, GROUP):
                pivot[t][u] = pivot[t][u] * scale[t]
            for u in range(t + 1, GROUP):
                for w in range(u, GROUP):
                    pivot[u][w] = pivot[u][w] - pivot[t][u] * pivot[t][w]
            first[t] = first[t] * scale[t]
            second[t] = second[t] * scale[t]
            for u in range(t + 1, GROUP):
                first[u] = first[u] - pivot[t][u] * first[t]
                second[u] = second[u] - pivot[t][u] * second[t]
        solved = [None] * GROUP
        for t in reversed(range(GROUP)):
            value = second[t]
            for u in range(t + 1, GROUP):
                value = value - pivot[t][u] * solved[u]
            solved[t] = value * scale[t]
        for later in range(step + 1, TILE // GROUP):
            value = jnp.where(inside, 0.0, rows[later])
            for t in range(GROUP):
                value = value - splat(rows[later], base + t) * solved[t]
            rows[later] = value
        upper_rows, inverse_rows = first[0], second[0]
        for t in range(1, GROUP):
            upper_rows = jnp.where(subs == t, first[t], upper_rows)
            inverse_rows = jnp.where(subs == t, second[t], inverse_rows)
        upper.append(upper_rows)
        inverse.append(inverse_rows)
    return upper, inverse


def factor_kernel(count, places_ref, damp_ref, exact_ref, *refs):
    lead_refs = refs[:count]
    lower_ref, inverse_ref, share_ref, work_ref, upper_ref = refs[-5:]
    steps = LEAD // TILE
    side = LEAD // count
    marks = sum(lead[2 * CAP + side :, :].astype(F32) for lead in lead_refs)
    row = lax.broadcasted_iota(jnp.int32, marks.shape, 0)
    weight = jnp.where(row < 4, jnp.where(row % 2 == 0, 256.0, 1.0), 0.0)
    total = jnp.sum(marks * weight, axis=0, keepdims=True)[:, :1]
    share = (1.0 - DECAY) / total
    share_ref[...] = jnp.broadcast_to(share, share_ref.shape)
    for q, lead in enumerate(lead_refs):
        begin = pl.multiple_of(places_ref[PLACES + q] * side, side)
        work_ref[pl.ds(begin, side), :] = lead[2 * CAP : 2 * CAP + side, :].astype(F32)

    @pl.when((places_ref[0] == 0) & (places_ref[1] == 0))
    def _():
        work_ref[...] = exact_ref[...]

    gram = sum(dot_t(lead[: 2 * CAP, :], lead[: 2 * CAP, :]) for lead in lead_refs)
    rows = lax.broadcasted_iota(jnp.int32, (LEAD, LEAD), 0)
    cols = lax.broadcasted_iota(jnp.int32, (LEAD, LEAD), 1)
    work_ref[...] = (
        DECAY * work_ref[...] + share * gram + jnp.where(rows == cols, damp_ref[0], 0.0)
    )
    lanes = lax.broadcasted_iota(jnp.int32, (GROUP, TILE), 1)
    subs = lax.broadcasted_iota(jnp.int32, (GROUP, TILE), 0)

    def tile_step(k, carry):
        begin = pl.multiple_of(k * TILE, TILE)
        rows = [
            work_ref[pl.ds(begin + g * GROUP, GROUP), pl.ds(begin, TILE)]
            for g in range(TILE // GROUP)
        ]
        upper, inverse = eliminate_tile(rows)
        upper_tile = jnp.concatenate(
            [jnp.where(lanes >= subs + g * GROUP, part, 0.0) for g, part in enumerate(upper)], 0
        )
        inverse_tile = jnp.concatenate(
            [jnp.where(lanes <= subs + g * GROUP, part, 0.0) for g, part in enumerate(inverse)], 0
        )
        band = dot_split(inverse_tile, work_ref[pl.ds(begin, TILE), :], ((1,), (0,)))
        work_ref[pl.ds(begin, TILE), :] = band
        work_ref[pl.ds(begin, TILE), pl.ds(begin, TILE)] = inverse_tile
        band = work_ref[pl.ds(begin, TILE), :]
        at = lax.broadcasted_iota(jnp.int32, (TILE, LEAD), 1)
        right = jnp.where(at >= begin + TILE, band, 0.0)
        inverse_ref[pl.ds(begin, TILE), :] = jnp.where(at < begin + TILE, band, 0.0)
        upper_ref[pl.ds(begin, TILE), :] = right
        upper_ref[pl.ds(begin, TILE), pl.ds(begin, TILE)] = upper_tile
        down = lax.broadcasted_iota(jnp.int32, (LEAD, TILE), 0)
        column = work_ref[:, pl.ds(begin, TILE)]
        work_ref[:, pl.ds(begin, TILE)] = jnp.where(down >= begin + TILE, 0.0, column)
        work_ref[...] = work_ref[...] - dot_split(right, band, ((0,), (0,)))
        return carry

    lax.fori_loop(0, steps, tile_step, 0)
    lower_ref[...] = upper_ref[...].T


def factor_lead(places, damp, exact, lead, earlier):
    shape = jax.ShapeDtypeStruct((LEAD, LEAD), F32)
    vmem = pl.BlockSpec(memory_space=pltpu.VMEM)
    smem = pl.BlockSpec(memory_space=pltpu.SMEM)
    return pl.pallas_call(
        lambda *refs: factor_kernel(len(lead), *refs),
        grid=(1,),
        out_shape=(shape, shape, jax.ShapeDtypeStruct((GROUP, TILE), F32)),
        in_specs=[smem, smem, pl.BlockSpec((LEAD, LEAD), lambda i: (0, 0))]
        + [vmem] * len(lead)
        + [ANYWHERE] * len(earlier),
        out_specs=(vmem, vmem, vmem),
        scratch_shapes=[pltpu.VMEM((LEAD, LEAD), F32)] * 2,
        compiler_params=pltpu.CompilerParams(vmem_limit_bytes=VMEM_BYTES),
        cost_estimate=NO_COST,
    )(places, damp, exact, *lead, *earlier)


def stack_kernel(count, places_ref, *refs):
    own, other = refs[:count], refs[count : 2 * count]
    stack_ref, near_ref = refs[-2:]
    depth, side = 2 * CAP, LEAD // count
    for q in range(count):
        stack_ref[q * depth : q * depth + CAP, :] = own[q][:CAP, :]
        stack_ref[q * depth + CAP : (q + 1) * depth, :] = other[q][...]
        begin = pl.multiple_of(places_ref[PLACES + q] * side, side)
        near_ref[pl.ds(begin, side), :] = own[q][CAP:, :]


def stacked(places, own, other, earlier):
    count = len(own)
    rows, width = own[0].shape
    cols = COLS if width % COLS == 0 else ROWS
    tiled = lambda height: pl.BlockSpec((height, cols), lambda j: (0, j))
    return pl.pallas_call(
        lambda *refs: stack_kernel(count, *refs),
        grid=(width // cols,),
        out_shape=(
            jax.ShapeDtypeStruct((2 * CAP * count, width), BF16),
            jax.ShapeDtypeStruct((LEAD, width), BF16),
        ),
        in_specs=[pl.BlockSpec(memory_space=pltpu.SMEM)]
        + [tiled(rows)] * count
        + [tiled(CAP)] * count
        + [ANYWHERE] * len(earlier),
        out_specs=(tiled(2 * CAP * count), tiled(LEAD)),
        compiler_params=pltpu.CompilerParams(vmem_limit_bytes=VMEM_BYTES),
        cost_estimate=NO_COST,
    )(places, *own, *other, *earlier)


def panel_kernel(count, share_ref, inverse_ref, near_ref, across_ref, *refs):
    lead = refs[:count]
    out_ref, lead_ref = refs[-2:]
    depth = 2 * CAP

    @pl.when(pl.program_id(0) == 0)
    def _():
        for q in range(count):
            lead_ref[q * depth : (q + 1) * depth, :] = lead[q][:depth, :]

    gram = dot_t(lead_ref[...], across_ref[...])
    beside = DECAY * near_ref[...].astype(F32) + share_ref[:1, :1] * gram
    out_ref[...] = dot_split(inverse_ref[...], beside, ((1,), (0,))).astype(BF16)


def panel_columns(share, inverse, near, lead, across, earlier):
    count = len(lead)
    tall, width = across.shape
    cols = COLS if width % COLS == 0 else ROWS
    whole = lambda height: pl.BlockSpec((height, LEAD), lambda j: (0, 0))
    tiled = lambda height: pl.BlockSpec((height, cols), lambda j: (0, j))
    return pl.pallas_call(
        lambda *refs: panel_kernel(count, *refs),
        grid=(width // cols,),
        out_shape=(
            jax.ShapeDtypeStruct((LEAD, width), BF16),
            jax.ShapeDtypeStruct((tall, LEAD), BF16),
        ),
        in_specs=[
            pl.BlockSpec((GROUP, TILE), lambda j: (0, 0)),
            whole(LEAD),
            tiled(LEAD),
            tiled(tall),
        ]
        + [whole(lead[0].shape[0])] * count
        + [ANYWHERE] * len(earlier),
        out_specs=(tiled(LEAD), whole(tall)),
        compiler_params=pltpu.CompilerParams(vmem_limit_bytes=VMEM_BYTES),
        cost_estimate=NO_COST,
    )(share, inverse, near, across, *lead, *earlier)


def solve_kernel(flag_ref, inverse_ref, first_ref, second_ref, *refs):
    high_ref, low_ref, parts_ref = refs[-3:]

    @pl.when(pl.program_id(0) == 0)
    def _():
        parts_ref[0], parts_ref[1] = split(inverse_ref[...])

    values = jnp.where(flag_ref[0] == 1, first_ref[...], second_ref[...])
    solved = jnp.dot(parts_ref[0], values, preferred_element_type=F32)
    solved = solved + jnp.dot(parts_ref[1], values, preferred_element_type=F32)
    high_ref[...], low_ref[...] = split(solved)


def solve_lead(flag, inverse, first, second, earlier):
    tiled = pl.BlockSpec((LEAD, COLS), lambda j: (0, j))
    return pl.pallas_call(
        solve_kernel,
        grid=(first.shape[1] // COLS,),
        out_shape=(jax.ShapeDtypeStruct(first.shape, BF16),) * 2,
        in_specs=[
            pl.BlockSpec(memory_space=pltpu.SMEM),
            pl.BlockSpec((LEAD, LEAD), lambda j: (0, 0)),
            tiled,
            tiled,
        ]
        + [ANYWHERE] * len(earlier),
        out_specs=(tiled, tiled),
        scratch_shapes=[pltpu.VMEM((2, LEAD, LEAD), BF16)],
        compiler_params=pltpu.CompilerParams(vmem_limit_bytes=VMEM_BYTES),
        cost_estimate=NO_COST,
    )(flag, inverse, first, second, *earlier)


def finish_kernel(
    count,
    gram_steps,
    begin,
    unread,
    places_ref,
    damp_ref,
    share_ref,
    factor_ref,
    grad_ref,
    panel_ref,
    inverse_ref,
    high_ref,
    lead_ref,
    across_ref,
    *refs,
):
    first_chunk = begin == 0
    if first_chunk:
        lower_ref, low_ref, *refs = refs
    mine = refs[:count]
    outs = refs[count + unread :]
    running_ref, factored_ref, precond_ref, token_ref, mine_ref, rows_ref, first_ref = outs
    j, i = pl.program_id(0), pl.program_id(1)
    member, column, base = places_ref[0], places_ref[1], places_ref[2] + begin
    share, damp = share_ref[:1, :1], damp_ref[0]
    height, cols = running_ref.shape
    depth = 2 * CAP
    side = LEAD // count
    span = pl.ds(pl.multiple_of(i * height, height), height)
    head = (member == 0) & first_chunk

    @pl.when(j == 0)
    def _():
        token_ref[...] = jnp.zeros_like(token_ref)
        for q in range(count):
            mine_ref[span, q * depth : (q + 1) * depth] = mine[q][0, :depth, :].T
            place = pl.multiple_of(places_ref[PLACES + q] * side, side)
            first_ref[pl.ds(place, side), :] = mine[q][0, depth : depth + side, :].astype(F32)
        source = first_ref[...].T
        if cols == LEAD:
            source = jnp.where(column == 0, factor_ref[...], source)
        gram = jnp.dot(mine_ref[span, :], lead_ref[...], preferred_element_type=F32)
        row = base + i * height + lax.broadcasted_iota(jnp.int32, (height, LEAD), 0)
        col = lax.broadcasted_iota(jnp.int32, (height, LEAD), 1)
        source = DECAY * source + share * gram
        source = source + jnp.where(row == col, damp, 0.0)
        rows_ref[span, :] = dot_split(source, inverse_ref[...], ((1,), (1,)))

    panel = rows_ref[span, :].astype(BF16)

    @pl.when(j < gram_steps)
    def _():
        gram = jnp.dot(mine_ref[span, :], across_ref[...], preferred_element_type=F32)
        running = DECAY * factor_ref[...] + share * gram
        running_ref[...] = running
        row = base + i * height + lax.broadcasted_iota(jnp.int32, (height, cols), 0)
        col = (column * gram_steps + j) * cols + lax.broadcasted_iota(jnp.int32, (height, cols), 1)
        matrix = running + jnp.where(row == col, damp, 0.0)
        factored = matrix - jnp.dot(panel, panel_ref[...], preferred_element_type=F32)
        factored_ref[...] = jnp.where(head, 0.0, factored)

        for part in range(LEAD // cols):
            edge = slice(part * cols, (part + 1) * cols)

            @pl.when((column == 0) & (j == part))
            def _():
                factored_ref[...] = rows_ref[span, edge]

                if first_chunk:

                    @pl.when(head)
                    def _():
                        factored_ref[...] = lower_ref[span, edge]

    product = jnp.dot(panel, high_ref[...], preferred_element_type=F32)
    precond_ref[...] = grad_ref[...].astype(F32) - product

    if first_chunk:

        @pl.when(head)
        def _():
            precond_ref[...] = high_ref[span, :].astype(F32) + low_ref[span, :].astype(F32)


def finish_rows(
    begin, places, damp, share, factor, grad, panel, inverse, lower, high, low,
    lead, across, mine, results, earlier,
):
    count = len(mine)
    deep, rows = mine[0].shape[1:]
    width, grad_cols = factor.shape[0], grad.shape[1]
    tall = lead.shape[0]
    height = min(rows, COLS)
    tiles = rows // height
    start = begin // height
    cols = COLS if width % COLS == 0 else ROWS
    gram_steps, steps = width // cols, grad_cols // cols
    assert steps >= gram_steps and rows % height == 0 and begin % height == 0

    def mine_spec(q):
        return pl.BlockSpec(
            (1, deep, height),
            lambda j, i, p: (p[PLACES + count + q], 0, jnp.where(j == 0, i, tiles - 1)),
        )

    def gram_col(j):
        return jnp.minimum(j, gram_steps - 1)

    def gram_tile(j, i, p):
        return (start + jnp.where(j < gram_steps, i, tiles - 1), gram_col(j))

    grad_spec = pl.BlockSpec((height, cols), lambda j, i, p: (start + i, j))
    factor_spec = pl.BlockSpec((height, cols), gram_tile)
    lead_whole = pl.BlockSpec((LEAD, LEAD), lambda j, i, p: (0, 0))
    small = pl.BlockSpec((GROUP, TILE), lambda j, i, p: (0, 0))
    in_specs = [
        pl.BlockSpec(memory_space=pltpu.SMEM),
        small,
        factor_spec,
        grad_spec,
        pl.BlockSpec((LEAD, cols), lambda j, i, p: (0, gram_col(j))),
        lead_whole,
        pl.BlockSpec((LEAD, cols), lambda j, i, p: (0, j)),
        pl.BlockSpec((tall, LEAD), lambda j, i, p: (0, 0)),
        pl.BlockSpec((tall, cols), lambda j, i, p: (0, gram_col(j))),
    ]
    operands = [damp, share, factor, grad, panel, inverse, high, lead, across]
    if begin == 0:
        in_specs += [lead_whole, pl.BlockSpec((LEAD, cols), lambda j, i, p: (0, j))]
        operands += [lower, low]
    in_specs += [mine_spec(q) for q in range(count)]
    operands += mine
    aliases = {1 + len(operands) + k: k for k in range(len(results))}
    operands += [*results, *earlier]
    unread = len(results) + len(earlier)
    in_specs += [ANYWHERE] * unread
    return pl.pallas_call(
        lambda *refs: finish_kernel(count, gram_steps, begin, unread, *refs),
        grid_spec=pltpu.PrefetchScalarGridSpec(
            num_scalar_prefetch=1,
            grid=(steps, tiles),
            in_specs=in_specs,
            out_specs=(factor_spec, factor_spec, grad_spec, small),
            scratch_shapes=[
                pltpu.VMEM((rows, tall), BF16),
                pltpu.VMEM((rows, LEAD), F32),
                pltpu.VMEM((LEAD, height), F32),
            ],
        ),
        out_shape=(
            jax.ShapeDtypeStruct(factor.shape, F32),
            jax.ShapeDtypeStruct(factor.shape, F32),
            jax.ShapeDtypeStruct(grad.shape, F32),
            jax.ShapeDtypeStruct((GROUP, TILE), F32),
        ),
        input_output_aliases=aliases,
        compiler_params=pltpu.CompilerParams(vmem_limit_bytes=VMEM_BYTES),
        cost_estimate=NO_COST,
    )(places, *operands)


def swapped(value, mask):
    size = lax.axis_size("tok")
    return lax.ppermute(value, "tok", [(source, source ^ mask) for source in range(size)])


def gather_members(value, bits):
    pieces = [value]
    for bit in reversed(range(bits)):
        pieces = pieces + [swapped(piece, 1 << bit) for piece in pieces]
    return pieces


def copy_kernel(count, places_ref, *refs):
    for source, out in zip(refs[:count], refs[-count:]):
        out[...] = source[...].astype(BF16)


def copied(requests, earlier):
    in_specs, out_specs, shapes, places = [], [], [], []
    for array, block, place in requests:
        at = len(places)
        places += place
        shape = tuple(size for size in block if size is not None)
        shapes.append(shape)
        in_specs.append(
            pl.BlockSpec(block, lambda i, p, a=at, n=len(block): tuple(p[a + k] for k in range(n)))
        )
        out_specs.append(pl.BlockSpec(shape, lambda i, p: (0, 0)))
    arrays = [array for array, _, _ in requests]
    return pl.pallas_call(
        lambda *refs: copy_kernel(len(arrays), *refs),
        grid_spec=pltpu.PrefetchScalarGridSpec(
            num_scalar_prefetch=1,
            grid=(1,),
            in_specs=in_specs + [ANYWHERE] * len(earlier),
            out_specs=out_specs,
        ),
        out_shape=[jax.ShapeDtypeStruct(shape, BF16) for shape in shapes],
        compiler_params=pltpu.CompilerParams(vmem_limit_bytes=VMEM_BYTES),
        cost_estimate=NO_COST,
    )(jnp.stack([jnp.int32(place) for place in places]), *arrays, *earlier)


def choose_kernel(flag_ref, first_ref, second_ref, *refs):
    refs[-1][...] = jnp.where(flag_ref[0] == 1, first_ref[...], second_ref[...])


def chosen(flag, first, second, earlier):
    tiled = pl.BlockSpec((first.shape[0] // 2, first.shape[1]), lambda i: (i, 0))
    return pl.pallas_call(
        choose_kernel,
        grid=(2,),
        out_shape=jax.ShapeDtypeStruct(first.shape, first.dtype),
        in_specs=[pl.BlockSpec(memory_space=pltpu.SMEM), tiled, tiled] + [ANYWHERE] * len(earlier),
        out_specs=tiled,
        compiler_params=pltpu.CompilerParams(vmem_limit_bytes=VMEM_BYTES),
        cost_estimate=NO_COST,
    )(flag, first, second, *earlier)


def member_blocks(blocks, member, group):
    _, rows, width = blocks.shape
    return [(blocks, (None, rows, width), [member ^ other, 0, 0]) for other in range(1, group)]


def exchange_members(blocks, sent, bits, requests, earlier):
    held = [[blocks]] + [[part] for part in sent]
    copies = None
    for bit in reversed(range(bits)):
        half = 1 << bit
        arrived = [(part, part.shape, [0, 0]) for passed in held[half:] for part in passed[1:]]
        if arrived:
            passing = copied(
                requests + arrived if copies is None else arrived, earlier + held[0][1:]
            )
            if copies is None:
                copies, passing = passing[: len(requests)], passing[len(requests) :]
            for passed in held[half:]:
                count = len(passed) - 1
                passed[1:], passing = passing[:count], passing[count:]
        held = [
            kept + [swapped(part, half) for part in passed]
            for kept, passed in zip(held[:half], held[half:])
        ]
    first, *others = held[0]
    return [first] + [part[None] for part in others], copies


def member_order(bits):
    order = [0]
    for bit in reversed(range(bits)):
        order = order + [other ^ (1 << bit) for other in order]
    return order


def down_pairs(bit, group):
    mask = 1 << bit
    return [
        (source, source + mask)
        for source in range(lax.axis_size("tok"))
        if source % group % (2 * mask) == 0
    ]


def share_of_first(lower, upper, member, group, bits):
    for bit in reversed(range(bits)):
        moved = lax.ppermute(upper, "tok", down_pairs(bit, group))
        blocks = jnp.where(member >> bit & 1 == 1, moved, lower)
        half = blocks.shape[0] // 2
        lower, upper = blocks[:half], blocks[half:]
    return blocks


def count_rows(number, row, width):
    index = lax.broadcasted_iota(jnp.int32, (16, width), 0)
    rest = jnp.where(index == row + 1, number % 256, 0)
    return jnp.where(index == row, number // 256, rest).astype(BF16)


def local(grad_rows, routes, counts, factor_old, damping, weight_grad):
    group = lax.axis_size("tok") // 2
    bits = group.bit_length() - 1
    position = lax.axis_index("tok")
    expert = position // group
    member = position % group
    column = lax.axis_index("fac")
    tok_rows, width = grad_rows.shape
    damp = jnp.where(expert == 0, damping[0], damping[1])[None]
    order = [member ^ other for other in member_order(bits)]

    side = LEAD // 2
    halves = [(factor_old, (side, width), [place, 0]) for place in range(2)]
    lead_factor = share_of_first(*copied(halves, []), member, group, bits)

    live = jnp.arange(tok_rows) < counts[0]
    named = routes[:, 0]
    own = live & (named == expert)
    away = live & (named != expert)
    flags = jnp.stack([own, away])
    ranks = jnp.cumsum(flags.astype(jnp.int32), 1) - 1
    picker = (ranks[:, None, :] == jnp.arange(CAP)[None, :, None]) & flags[:, None, :]
    packed = jnp.dot(
        picker.reshape(2 * CAP, tok_rows).astype(BF16), grad_rows, preferred_element_type=F32
    ).astype(BF16)
    tally = jnp.sum(flags.astype(jnp.int32), 1)
    front = swapped(
        jnp.concatenate([packed[CAP:, :LEAD], count_rows(tally[1], 2, LEAD)], 0), group
    )
    first_part = jnp.concatenate(
        [
            packed[:CAP, :LEAD],
            front[:CAP],
            lead_factor[:, :LEAD],
            front[CAP:] + count_rows(tally[0], 0, LEAD),
        ],
        0,
    )
    away_rows = copied([(packed, (CAP, width), [1, 0])], [front])[0]
    incoming = swapped(away_rows, group)
    outgoing = jnp.concatenate([packed[:CAP], lead_factor], 0)
    quarter = jnp.concatenate([packed[:CAP], incoming, lead_factor], 0)
    across_own = gather_members(outgoing, bits)
    across_other = gather_members(incoming, bits)

    ends = [end for end in (LEAD, 2 * LEAD, 2 * LEAD + ROWS) if end < width] + [width]
    chunks = list(zip([0, *ends], ends))
    rows = quarter.shape[0]
    later = [
        (quarter, (rows, end - begin), [0, begin // (end - begin)]) for begin, end in chunks[1:]
    ]
    parts = [first_part, *copied(later, [across_own[1]])]
    spread = [lax.all_gather(part, "fac") for part in parts]
    rows = first_part.shape[0]
    earlier = [across_other[1], *parts[1:]]
    lead = copied([(spread[0], (None, rows, LEAD), [0, 0, 0])], earlier)[0]
    slots = [member, column, member * width] + order + [member] + [0] * (group - 1)
    assert len(slots) == PLACES + 2 * group
    slots = jnp.stack([jnp.int32(slot) for slot in slots])
    across, near_factor = stacked(slots, across_own, across_other, [lead])
    lead = gather_members(lead, bits)
    grad_cols = weight_grad.shape[1]
    requests = member_blocks(spread[0], member, group)
    requests += [(weight_grad, (LEAD, grad_cols), [0, 0])]
    *sent, near = copied(requests, [lead[1], across])

    lower, inverse, share = factor_lead(slots, damp, factor_old, lead, sent[:1])
    panel, lead_stack = panel_columns(
        share, inverse, near_factor, lead, across, spread[1:2]
    )

    token = panel
    results = []
    for number, (begin, _) in enumerate(chunks):
        requests = []
        if number + 1 < len(chunks):
            requests = member_blocks(spread[number + 1], member, group)
        pieces, sent = exchange_members(spread[number], sent, bits, requests, [token])
        if number == 0:
            for bit in reversed(range(bits)):
                moved = lax.ppermute(near, "tok", down_pairs(bit, group))
                flag = (member >> bit & 1)[None]
                if bit:
                    near = chosen(flag, moved, near, sent[:1])
            high, low = solve_lead(flag, inverse, moved, near, spread[2:3])
        *results, token = finish_rows(
            begin,
            slots,
            damp,
            share,
            factor_old,
            weight_grad,
            panel,
            inverse,
            lower,
            high,
            low,
            lead_stack,
            across,
            pieces,
            results,
            sent[:1],
        )
    return tuple(results)


def solution(mesh):
    placed = (P("tok", "fac"), P("tok", None), P("tok"), P("tok", "fac"), P(), P("tok", "fac"))
    return jax.shard_map(
        local,
        mesh=mesh,
        in_specs=placed,
        out_specs=(P("tok", "fac"), P("tok", "fac"), P("tok", "fac")),
        check_vma=False,
    )
```

```python
import jax
import jax.numpy as jnp
from jax import lax
from jax.experimental import pallas as pl
from jax.experimental.pallas import tpu as pltpu
from jax.sharding import PartitionSpec as P

CAP = 320
LEAD = 512
TILE = 128
GROUP = 8
ROWS = 256
COLS = 512
PLACES = 3
VMEM_BYTES = 60 * 1024 * 1024
ANYWHERE = pl.BlockSpec(memory_space=pl.ANY)
NO_COST = pl.CostEstimate(flops=1, bytes_accessed=1, transcendentals=0)
DECAY = 0.8

HIGHEST = lax.Precision.HIGHEST
BF16 = jnp.bfloat16
F32 = jnp.float32


def dot_t(left, right, precision=None):
    return lax.dot_general(
        left, right, (((0,), (0,)), ((), ())), precision=precision, preferred_element_type=F32
    )


def split(value):
    high = value.astype(BF16)
    return high, (value - high.astype(F32)).astype(BF16)


def dot_split(left, right, contract):
    (left_high, left_low), (right_high, right_low) = split(left), split(right)
    product = lambda a, b: lax.dot_general(
        a, b, (contract, ((), ())), preferred_element_type=F32
    )
    return product(left_high, right_high) + (
        product(left_high, right_low) + product(left_low, right_high)
    )


def splat(rows, lane):
    return jnp.broadcast_to(rows[:, lane : lane + 1], rows.shape)


def eliminate_tile(rows):
    lanes = lax.broadcasted_iota(jnp.int32, (GROUP, TILE), 1)
    subs = lax.broadcasted_iota(jnp.int32, (GROUP, TILE), 0)
    upper, inverse = [], []
    for step in range(TILE // GROUP):
        base = step * GROUP
        inside = (lanes >= base) & (lanes < base + GROUP)
        block = rows[step]
        first = [jnp.broadcast_to(block[t : t + 1, :], (GROUP, TILE)) for t in range(GROUP)]
        second = [
            jnp.where(inside, jnp.where(lanes == base + t, 1.0, 0.0), first[t])
            for t in range(GROUP)
        ]
        pivot = [
            [splat(first[t], base + u) if u >= t else None for u in range(GROUP)]
            for t in range(GROUP)
        ]
        coming = rows[step + 1] if step + 1 < TILE // GROUP else block
        factors = [splat(coming, base + u) for u in range(GROUP)]
        coming = jnp.where(inside, 0.0, coming)
        scale = [None] * GROUP
        for t in range(GROUP):
            scale[t] = lax.rsqrt(pivot[t][t])
            for u in range(t + 1, GROUP):
                pivot[t][u] = pivot[t][u] * scale[t]
            for u in range(t + 1, GROUP):
                for w in range(u, GROUP):
                    pivot[u][w] = pivot[u][w] - pivot[t][u] * pivot[t][w]
            first[t] = first[t] * scale[t]
            second[t] = second[t] * scale[t]
            factors[t] = factors[t] * scale[t]
            coming = coming - factors[t] * second[t]
            for u in range(t + 1, GROUP):
                first[u] = first[u] - pivot[t][u] * first[t]
                second[u] = second[u] - pivot[t][u] * second[t]
                factors[u] = factors[u] - pivot[t][u] * factors[t]
        solved = [None] * GROUP
        for t in reversed(range(GROUP)):
            value = second[t]
            for u in range(t + 1, GROUP):
                value = value - pivot[t][u] * solved[u]
            solved[t] = value * scale[t]
        if step + 1 < TILE // GROUP:
            rows[step + 1] = coming
        for later in range(step + 2, TILE // GROUP):
            value = jnp.where(inside, 0.0, rows[later])
            for t in range(GROUP):
                value = value - splat(rows[later], base + t) * solved[t]
            rows[later] = value
        upper_rows, inverse_rows = first[0], second[0]
        for t in range(1, GROUP):
            upper_rows = jnp.where(subs == t, first[t], upper_rows)
            inverse_rows = jnp.where(subs == t, second[t], inverse_rows)
        upper.append(upper_rows)
        inverse.append(inverse_rows)
    return upper, inverse


def factor_kernel(count, places_ref, damp_ref, exact_ref, *refs):
    lead_refs = refs[:count]
    lower_ref, inverse_ref, share_ref, work_ref, upper_ref = refs[-5:]
    steps = LEAD // TILE
    side = LEAD // count
    marks = sum(lead[2 * CAP + side :, :].astype(F32) for lead in lead_refs)
    row = lax.broadcasted_iota(jnp.int32, marks.shape, 0)
    weight = jnp.where(row < 4, jnp.where(row % 2 == 0, 256.0, 1.0), 0.0)
    total = jnp.sum(marks * weight, axis=0, keepdims=True)[:, :1]
    share = (1.0 - DECAY) / total
    share_ref[...] = jnp.broadcast_to(share, share_ref.shape)
    for q, lead in enumerate(lead_refs):
        begin = pl.multiple_of(places_ref[PLACES + q] * side, side)
        work_ref[pl.ds(begin, side), :] = lead[2 * CAP : 2 * CAP + side, :].astype(F32)

    @pl.when((places_ref[0] == 0) & (places_ref[1] == 0))
    def _():
        work_ref[...] = exact_ref[...]

    gram = sum(dot_t(lead[: 2 * CAP, :], lead[: 2 * CAP, :]) for lead in lead_refs)
    rows = lax.broadcasted_iota(jnp.int32, (LEAD, LEAD), 0)
    cols = lax.broadcasted_iota(jnp.int32, (LEAD, LEAD), 1)
    work_ref[...] = (
        DECAY * work_ref[...] + share * gram + jnp.where(rows == cols, damp_ref[0], 0.0)
    )
    lanes = lax.broadcasted_iota(jnp.int32, (GROUP, TILE), 1)
    subs = lax.broadcasted_iota(jnp.int32, (GROUP, TILE), 0)

    def tile_step(k, carry):
        begin = pl.multiple_of(k * TILE, TILE)
        rows = [
            work_ref[pl.ds(begin + g * GROUP, GROUP), pl.ds(begin, TILE)]
            for g in range(TILE // GROUP)
        ]
        upper, inverse = eliminate_tile(rows)
        upper_tile = jnp.concatenate(
            [jnp.where(lanes >= subs + g * GROUP, part, 0.0) for g, part in enumerate(upper)], 0
        )
        inverse_tile = jnp.concatenate(
            [jnp.where(lanes <= subs + g * GROUP, part, 0.0) for g, part in enumerate(inverse)], 0
        )
        band = dot_split(inverse_tile, work_ref[pl.ds(begin, TILE), :], ((1,), (0,)))
        work_ref[pl.ds(begin, TILE), :] = band
        work_ref[pl.ds(begin, TILE), pl.ds(begin, TILE)] = inverse_tile
        band = work_ref[pl.ds(begin, TILE), :]
        at = lax.broadcasted_iota(jnp.int32, (TILE, LEAD), 1)
        right = jnp.where(at >= begin + TILE, band, 0.0)
        inverse_ref[pl.ds(begin, TILE), :] = jnp.where(at < begin + TILE, band, 0.0)
        upper_ref[pl.ds(begin, TILE), :] = right
        upper_ref[pl.ds(begin, TILE), pl.ds(begin, TILE)] = upper_tile
        down = lax.broadcasted_iota(jnp.int32, (LEAD, TILE), 0)
        column = work_ref[:, pl.ds(begin, TILE)]
        work_ref[:, pl.ds(begin, TILE)] = jnp.where(down >= begin + TILE, 0.0, column)
        work_ref[...] = work_ref[...] - dot_split(right, band, ((0,), (0,)))
        return carry

    lax.fori_loop(0, steps, tile_step, 0)
    lower_ref[...] = upper_ref[...].T


def factor_lead(places, damp, exact, lead, earlier):
    shape = jax.ShapeDtypeStruct((LEAD, LEAD), F32)
    vmem = pl.BlockSpec(memory_space=pltpu.VMEM)
    smem = pl.BlockSpec(memory_space=pltpu.SMEM)
    return pl.pallas_call(
        lambda *refs: factor_kernel(len(lead), *refs),
        grid=(1,),
        out_shape=(shape, shape, jax.ShapeDtypeStruct((GROUP, TILE), F32)),
        in_specs=[smem, smem, pl.BlockSpec((LEAD, LEAD), lambda i: (0, 0))]
        + [vmem] * len(lead)
        + [ANYWHERE] * len(earlier),
        out_specs=(vmem, vmem, vmem),
        scratch_shapes=[pltpu.VMEM((LEAD, LEAD), F32)] * 2,
        compiler_params=pltpu.CompilerParams(vmem_limit_bytes=VMEM_BYTES),
        cost_estimate=NO_COST,
    )(places, damp, exact, *lead, *earlier)


def stack_kernel(count, places_ref, *refs):
    own, other = refs[:count], refs[count : 2 * count]
    stack_ref, near_ref = refs[-2:]
    depth, side = 2 * CAP, LEAD // count
    for q in range(count):
        stack_ref[q * depth : q * depth + CAP, :] = own[q][:CAP, :]
        stack_ref[q * depth + CAP : (q + 1) * depth, :] = other[q][...]
        begin = pl.multiple_of(places_ref[PLACES + q] * side, side)
        near_ref[pl.ds(begin, side), :] = own[q][CAP:, :]


def stacked(places, own, other, earlier):
    count = len(own)
    rows, width = own[0].shape
    cols = COLS if width % COLS == 0 else ROWS
    tiled = lambda height: pl.BlockSpec((height, cols), lambda j: (0, j))
    return pl.pallas_call(
        lambda *refs: stack_kernel(count, *refs),
        grid=(width // cols,),
        out_shape=(
            jax.ShapeDtypeStruct((2 * CAP * count, width), BF16),
            jax.ShapeDtypeStruct((LEAD, width), BF16),
        ),
        in_specs=[pl.BlockSpec(memory_space=pltpu.SMEM)]
        + [tiled(rows)] * count
        + [tiled(CAP)] * count
        + [ANYWHERE] * len(earlier),
        out_specs=(tiled(2 * CAP * count), tiled(LEAD)),
        compiler_params=pltpu.CompilerParams(vmem_limit_bytes=VMEM_BYTES),
        cost_estimate=NO_COST,
    )(places, *own, *other, *earlier)


def panel_kernel(count, share_ref, inverse_ref, near_ref, across_ref, *refs):
    lead = refs[:count]
    out_ref, lead_ref = refs[-2:]
    depth = 2 * CAP

    @pl.when(pl.program_id(0) == 0)
    def _():
        for q in range(count):
            lead_ref[q * depth : (q + 1) * depth, :] = lead[q][:depth, :]

    gram = dot_t(lead_ref[...], across_ref[...])
    beside = DECAY * near_ref[...].astype(F32) + share_ref[:1, :1] * gram
    out_ref[...] = dot_split(inverse_ref[...], beside, ((1,), (0,))).astype(BF16)


def panel_columns(share, inverse, near, lead, across, earlier):
    count = len(lead)
    tall, width = across.shape
    cols = COLS if width % COLS == 0 else ROWS
    whole = lambda height: pl.BlockSpec((height, LEAD), lambda j: (0, 0))
    tiled = lambda height: pl.BlockSpec((height, cols), lambda j: (0, j))
    return pl.pallas_call(
        lambda *refs: panel_kernel(count, *refs),
        grid=(width // cols,),
        out_shape=(
            jax.ShapeDtypeStruct((LEAD, width), BF16),
            jax.ShapeDtypeStruct((tall, LEAD), BF16),
        ),
        in_specs=[
            pl.BlockSpec((GROUP, TILE), lambda j: (0, 0)),
            whole(LEAD),
            tiled(LEAD),
            tiled(tall),
        ]
        + [whole(lead[0].shape[0])] * count
        + [ANYWHERE] * len(earlier),
        out_specs=(tiled(LEAD), whole(tall)),
        compiler_params=pltpu.CompilerParams(vmem_limit_bytes=VMEM_BYTES),
        cost_estimate=NO_COST,
    )(share, inverse, near, across, *lead, *earlier)


def solve_kernel(flag_ref, inverse_ref, first_ref, second_ref, *refs):
    high_ref, low_ref, parts_ref = refs[-3:]

    @pl.when(pl.program_id(0) == 0)
    def _():
        parts_ref[0], parts_ref[1] = split(inverse_ref[...])

    values = jnp.where(flag_ref[0] == 1, first_ref[...], second_ref[...])
    solved = jnp.dot(parts_ref[0], values, preferred_element_type=F32)
    solved = solved + jnp.dot(parts_ref[1], values, preferred_element_type=F32)
    high_ref[...], low_ref[...] = split(solved)


def solve_lead(flag, inverse, first, second, earlier):
    tiled = pl.BlockSpec((LEAD, COLS), lambda j: (0, j))
    return pl.pallas_call(
        solve_kernel,
        grid=(first.shape[1] // COLS,),
        out_shape=(jax.ShapeDtypeStruct(first.shape, BF16),) * 2,
        in_specs=[
            pl.BlockSpec(memory_space=pltpu.SMEM),
            pl.BlockSpec((LEAD, LEAD), lambda j: (0, 0)),
            tiled,
            tiled,
        ]
        + [ANYWHERE] * len(earlier),
        out_specs=(tiled, tiled),
        scratch_shapes=[pltpu.VMEM((2, LEAD, LEAD), BF16)],
        compiler_params=pltpu.CompilerParams(vmem_limit_bytes=VMEM_BYTES),
        cost_estimate=NO_COST,
    )(flag, inverse, first, second, *earlier)


def finish_kernel(
    count,
    gram_steps,
    begin,
    unread,
    places_ref,
    damp_ref,
    share_ref,
    factor_ref,
    grad_ref,
    panel_ref,
    inverse_ref,
    high_ref,
    lead_ref,
    across_ref,
    *refs,
):
    first_chunk = begin == 0
    if first_chunk:
        lower_ref, low_ref, *refs = refs
    mine = refs[:count]
    outs = refs[count + unread :]
    running_ref, factored_ref, precond_ref, token_ref, mine_ref, rows_ref, first_ref = outs
    j, i = pl.program_id(0), pl.program_id(1)
    member, column, base = places_ref[0], places_ref[1], places_ref[2] + begin
    share, damp = share_ref[:1, :1], damp_ref[0]
    height, cols = running_ref.shape
    depth = 2 * CAP
    side = LEAD // count
    span = pl.ds(pl.multiple_of(i * height, height), height)
    head = (member == 0) & first_chunk

    @pl.when(j == 0)
    def _():
        token_ref[...] = jnp.zeros_like(token_ref)
        for q in range(count):
            mine_ref[span, q * depth : (q + 1) * depth] = mine[q][0, :depth, :].T
            place = pl.multiple_of(places_ref[PLACES + q] * side, side)
            first_ref[pl.ds(place, side), :] = mine[q][0, depth : depth + side, :].astype(F32)
        source = first_ref[...].T
        if cols == LEAD:
            source = jnp.where(column == 0, factor_ref[...], source)
        gram = jnp.dot(mine_ref[span, :], lead_ref[...], preferred_element_type=F32)
        row = base + i * height + lax.broadcasted_iota(jnp.int32, (height, LEAD), 0)
        col = lax.broadcasted_iota(jnp.int32, (height, LEAD), 1)
        source = DECAY * source + share * gram
        source = source + jnp.where(row == col, damp, 0.0)
        rows_ref[span, :] = dot_split(source, inverse_ref[...], ((1,), (1,)))

    panel = rows_ref[span, :].astype(BF16)

    @pl.when(j < gram_steps)
    def _():
        gram = jnp.dot(mine_ref[span, :], across_ref[...], preferred_element_type=F32)
        running = DECAY * factor_ref[...] + share * gram
        running_ref[...] = running
        row = base + i * height + lax.broadcasted_iota(jnp.int32, (height, cols), 0)
        col = (column * gram_steps + j) * cols + lax.broadcasted_iota(jnp.int32, (height, cols), 1)
        matrix = running + jnp.where(row == col, damp, 0.0)
        factored = matrix - jnp.dot(panel, panel_ref[...], preferred_element_type=F32)
        factored_ref[...] = jnp.where(head, 0.0, factored)

        for part in range(LEAD // cols):
            edge = slice(part * cols, (part + 1) * cols)

            @pl.when((column == 0) & (j == part))
            def _():
                factored_ref[...] = rows_ref[span, edge]

                if first_chunk:

                    @pl.when(head)
                    def _():
                        factored_ref[...] = lower_ref[span, edge]

    product = jnp.dot(panel, high_ref[...], preferred_element_type=F32)
    precond_ref[...] = grad_ref[...].astype(F32) - product

    if first_chunk:

        @pl.when(head)
        def _():
            precond_ref[...] = high_ref[span, :].astype(F32) + low_ref[span, :].astype(F32)


def finish_rows(
    begin, places, damp, share, factor, grad, panel, inverse, lower, high, low,
    lead, across, mine, results, earlier,
):
    count = len(mine)
    deep, rows = mine[0].shape[1:]
    width, grad_cols = factor.shape[0], grad.shape[1]
    tall = lead.shape[0]
    height = min(rows, COLS)
    tiles = rows // height
    start = begin // height
    cols = COLS if width % COLS == 0 else ROWS
    gram_steps, steps = width // cols, grad_cols // cols
    assert steps >= gram_steps and rows % height == 0 and begin % height == 0

    def mine_spec(q):
        return pl.BlockSpec(
            (1, deep, height),
            lambda j, i, p: (p[PLACES + count + q], 0, jnp.where(j == 0, i, tiles - 1)),
        )

    def gram_col(j):
        return jnp.minimum(j, gram_steps - 1)

    def gram_tile(j, i, p):
        return (start + jnp.where(j < gram_steps, i, tiles - 1), gram_col(j))

    grad_spec = pl.BlockSpec((height, cols), lambda j, i, p: (start + i, j))
    factor_spec = pl.BlockSpec((height, cols), gram_tile)
    lead_whole = pl.BlockSpec((LEAD, LEAD), lambda j, i, p: (0, 0))
    small = pl.BlockSpec((GROUP, TILE), lambda j, i, p: (0, 0))
    in_specs = [
        pl.BlockSpec(memory_space=pltpu.SMEM),
        small,
        factor_spec,
        grad_spec,
        pl.BlockSpec((LEAD, cols), lambda j, i, p: (0, gram_col(j))),
        lead_whole,
        pl.BlockSpec((LEAD, cols), lambda j, i, p: (0, j)),
        pl.BlockSpec((tall, LEAD), lambda j, i, p: (0, 0)),
        pl.BlockSpec((tall, cols), lambda j, i, p: (0, gram_col(j))),
    ]
    operands = [damp, share, factor, grad, panel, inverse, high, lead, across]
    if begin == 0:
        in_specs += [lead_whole, pl.BlockSpec((LEAD, cols), lambda j, i, p: (0, j))]
        operands += [lower, low]
    in_specs += [mine_spec(q) for q in range(count)]
    operands += mine
    aliases = {1 + len(operands) + k: k for k in range(len(results))}
    operands += [*results, *earlier]
    unread = len(results) + len(earlier)
    in_specs += [ANYWHERE] * unread
    return pl.pallas_call(
        lambda *refs: finish_kernel(count, gram_steps, begin, unread, *refs),
        grid_spec=pltpu.PrefetchScalarGridSpec(
            num_scalar_prefetch=1,
            grid=(steps, tiles),
            in_specs=in_specs,
            out_specs=(factor_spec, factor_spec, grad_spec, small),
            scratch_shapes=[
                pltpu.VMEM((rows, tall), BF16),
                pltpu.VMEM((rows, LEAD), F32),
                pltpu.VMEM((LEAD, height), F32),
            ],
        ),
        out_shape=(
            jax.ShapeDtypeStruct(factor.shape, F32),
            jax.ShapeDtypeStruct(factor.shape, F32),
            jax.ShapeDtypeStruct(grad.shape, F32),
            jax.ShapeDtypeStruct((GROUP, TILE), F32),
        ),
        input_output_aliases=aliases,
        compiler_params=pltpu.CompilerParams(vmem_limit_bytes=VMEM_BYTES),
        cost_estimate=NO_COST,
    )(places, *operands)


def swapped(value, mask):
    size = lax.axis_size("tok")
    return lax.ppermute(value, "tok", [(source, source ^ mask) for source in range(size)])


def gather_members(value, bits):
    pieces = [value]
    for bit in reversed(range(bits)):
        pieces = pieces + [swapped(piece, 1 << bit) for piece in pieces]
    return pieces


def copy_kernel(count, places_ref, *refs):
    for source, out in zip(refs[:count], refs[-count:]):
        out[...] = source[...].astype(BF16)


def copied(requests, earlier):
    in_specs, out_specs, shapes, places = [], [], [], []
    for array, block, place in requests:
        at = len(places)
        places += place
        shape = tuple(size for size in block if size is not None)
        shapes.append(shape)
        in_specs.append(
            pl.BlockSpec(block, lambda i, p, a=at, n=len(block): tuple(p[a + k] for k in range(n)))
        )
        out_specs.append(pl.BlockSpec(shape, lambda i, p: (0, 0)))
    arrays = [array for array, _, _ in requests]
    return pl.pallas_call(
        lambda *refs: copy_kernel(len(arrays), *refs),
        grid_spec=pltpu.PrefetchScalarGridSpec(
            num_scalar_prefetch=1,
            grid=(1,),
            in_specs=in_specs + [ANYWHERE] * len(earlier),
            out_specs=out_specs,
        ),
        out_shape=[jax.ShapeDtypeStruct(shape, BF16) for shape in shapes],
        compiler_params=pltpu.CompilerParams(vmem_limit_bytes=VMEM_BYTES),
        cost_estimate=NO_COST,
    )(jnp.stack([jnp.int32(place) for place in places]), *arrays, *earlier)


def choose_kernel(flag_ref, first_ref, second_ref, *refs):
    refs[-1][...] = jnp.where(flag_ref[0] == 1, first_ref[...], second_ref[...])


def chosen(flag, first, second, earlier):
    tiled = pl.BlockSpec((first.shape[0] // 2, first.shape[1]), lambda i: (i, 0))
    return pl.pallas_call(
        choose_kernel,
        grid=(2,),
        out_shape=jax.ShapeDtypeStruct(first.shape, first.dtype),
        in_specs=[pl.BlockSpec(memory_space=pltpu.SMEM), tiled, tiled] + [ANYWHERE] * len(earlier),
        out_specs=tiled,
        compiler_params=pltpu.CompilerParams(vmem_limit_bytes=VMEM_BYTES),
        cost_estimate=NO_COST,
    )(flag, first, second, *earlier)


def member_blocks(blocks, member, group):
    _, rows, width = blocks.shape
    return [(blocks, (None, rows, width), [member ^ other, 0, 0]) for other in range(1, group)]


def exchange_members(blocks, sent, bits, requests, earlier):
    held = [[blocks]] + [[part] for part in sent]
    copies = None
    for bit in reversed(range(bits)):
        half = 1 << bit
        arrived = [(part, part.shape, [0, 0]) for passed in held[half:] for part in passed[1:]]
        if arrived:
            passing = copied(
                requests + arrived if copies is None else arrived, earlier + held[0][1:]
            )
            if copies is None:
                copies, passing = passing[: len(requests)], passing[len(requests) :]
            for passed in held[half:]:
                count = len(passed) - 1
                passed[1:], passing = passing[:count], passing[count:]
        held = [
            kept + [swapped(part, half) for part in passed]
            for kept, passed in zip(held[:half], held[half:])
        ]
    first, *others = held[0]
    return [first] + [part[None] for part in others], copies


def member_order(bits):
    order = [0]
    for bit in reversed(range(bits)):
        order = order + [other ^ (1 << bit) for other in order]
    return order


def down_pairs(bit, group):
    mask = 1 << bit
    return [
        (source, source + mask)
        for source in range(lax.axis_size("tok"))
        if source % group % (2 * mask) == 0
    ]


def share_of_first(lower, upper, member, group, bits):
    for bit in reversed(range(bits)):
        moved = lax.ppermute(upper, "tok", down_pairs(bit, group))
        blocks = jnp.where(member >> bit & 1 == 1, moved, lower)
        half = blocks.shape[0] // 2
        lower, upper = blocks[:half], blocks[half:]
    return blocks


def count_rows(number, row, width):
    index = lax.broadcasted_iota(jnp.int32, (16, width), 0)
    rest = jnp.where(index == row + 1, number % 256, 0)
    return jnp.where(index == row, number // 256, rest).astype(BF16)


def local(grad_rows, routes, counts, factor_old, damping, weight_grad):
    group = lax.axis_size("tok") // 2
    bits = group.bit_length() - 1
    position = lax.axis_index("tok")
    expert = position // group
    member = position % group
    column = lax.axis_index("fac")
    tok_rows, width = grad_rows.shape
    damp = jnp.where(expert == 0, damping[0], damping[1])[None]
    order = [member ^ other for other in member_order(bits)]

    side = LEAD // 2
    halves = [(factor_old, (side, width), [place, 0]) for place in range(2)]
    halves = copied(halves, [])
    lead_factor = share_of_first(*halves, member, group, bits)

    near = copied([(weight_grad, (LEAD, weight_grad.shape[1]), [0, 0])], halves[:1])[0]
    moved = lax.ppermute(near, "tok", down_pairs(bits - 1, group))

    live = jnp.arange(tok_rows) < counts[0]
    named = routes[:, 0]
    own = live & (named == expert)
    away = live & (named != expert)
    flags = jnp.stack([own, away])
    ranks = jnp.cumsum(flags.astype(jnp.int32), 1) - 1
    picker = (ranks[:, None, :] == jnp.arange(CAP)[None, :, None]) & flags[:, None, :]
    packed = jnp.dot(
        picker.reshape(2 * CAP, tok_rows).astype(BF16), grad_rows, preferred_element_type=F32
    ).astype(BF16)
    tally = jnp.sum(flags.astype(jnp.int32), 1)
    front = swapped(
        jnp.concatenate([packed[CAP:, :LEAD], count_rows(tally[1], 2, LEAD)], 0), group
    )
    first_part = jnp.concatenate(
        [
            packed[:CAP, :LEAD],
            front[:CAP],
            lead_factor[:, :LEAD],
            front[CAP:] + count_rows(tally[0], 0, LEAD),
        ],
        0,
    )
    away_rows = copied([(packed, (CAP, width), [1, 0])], [front, moved])[0]
    incoming = swapped(away_rows, group)
    outgoing = jnp.concatenate([packed[:CAP], lead_factor], 0)
    quarter = jnp.concatenate([packed[:CAP], incoming, lead_factor], 0)
    across_own = gather_members(outgoing, bits)
    across_other = gather_members(incoming, bits)

    ends = [end for end in (LEAD, 2 * LEAD, 2 * LEAD + ROWS) if end < width] + [width]
    chunks = list(zip([0, *ends], ends))
    rows = quarter.shape[0]
    later = [
        (quarter, (rows, end - begin), [0, begin // (end - begin)]) for begin, end in chunks[1:]
    ]
    parts = [first_part, *copied(later, [across_own[1]])]
    spread = [lax.all_gather(part, "fac") for part in parts]
    rows = first_part.shape[0]
    earlier = [across_other[1], *parts[1:]]
    lead = copied([(spread[0], (None, rows, LEAD), [0, 0, 0])], earlier)[0]
    slots = [member, column, member * width] + order + [member] + [0] * (group - 1)
    assert len(slots) == PLACES + 2 * group
    slots = jnp.stack([jnp.int32(slot) for slot in slots])
    across, near_factor = stacked(slots, across_own, across_other, [lead])
    lead = gather_members(lead, bits)
    flag = (member >> (bits - 1) & 1)[None]
    for bit in reversed(range(bits - 1)):
        near = chosen(flag, moved, near, [across])
        moved = lax.ppermute(near, "tok", down_pairs(bit, group))
        flag = (member >> bit & 1)[None]
    sent = copied(member_blocks(spread[0], member, group), [lead[1], near])

    lower, inverse, share = factor_lead(slots, damp, factor_old, lead, sent[:1])
    panel, lead_stack = panel_columns(
        share, inverse, near_factor, lead, across, spread[1:2]
    )

    token = panel
    results = []
    for number, (begin, _) in enumerate(chunks):
        requests = []
        if number + 1 < len(chunks):
            requests = member_blocks(spread[number + 1], member, group)
        pieces, sent = exchange_members(spread[number], sent, bits, requests, [token])
        if number == 0:
            high, low = solve_lead(flag, inverse, moved, near, spread[2:3])
        *results, token = finish_rows(
            begin,
            slots,
            damp,
            share,
            factor_old,
            weight_grad,
            panel,
            inverse,
            lower,
            high,
            low,
            lead_stack,
            across,
            pieces,
            results,
            sent[:1],
        )
    return tuple(results)


def solution(mesh):
    placed = (P("tok", "fac"), P("tok", None), P("tok"), P("tok", "fac"), P(), P("tok", "fac"))
    return jax.shard_map(
        local,
        mesh=mesh,
        in_specs=placed,
        out_specs=(P("tok", "fac"), P("tok", "fac"), P("tok", "fac")),
        check_vma=False,
    )
```

```python
import jax
import jax.numpy as jnp
from jax import lax
from jax.experimental import pallas as pl
from jax.experimental.pallas import tpu as pltpu
from jax.sharding import PartitionSpec as P

CAP = 320
LEAD = 512
TILE = 128
GROUP = 8
ROWS = 256
COLS = 512
PLACES = 3
VMEM_BYTES = 60 * 1024 * 1024
ANYWHERE = pl.BlockSpec(memory_space=pl.ANY)
NO_COST = pl.CostEstimate(flops=1, bytes_accessed=1, transcendentals=0)
DECAY = 0.8

HIGHEST = lax.Precision.HIGHEST
BF16 = jnp.bfloat16
F32 = jnp.float32


def dot_t(left, right, precision=None):
    return lax.dot_general(
        left, right, (((0,), (0,)), ((), ())), precision=precision, preferred_element_type=F32
    )


def split(value):
    high = value.astype(BF16)
    return high, (value - high.astype(F32)).astype(BF16)


def dot_split(left, right, contract):
    (left_high, left_low), (right_high, right_low) = split(left), split(right)
    product = lambda a, b: lax.dot_general(
        a, b, (contract, ((), ())), preferred_element_type=F32
    )
    return product(left_high, right_high) + (
        product(left_high, right_low) + product(left_low, right_high)
    )


def splat(rows, lane):
    return jnp.broadcast_to(rows[:, lane : lane + 1], rows.shape)


def eliminate_tile(rows):
    lanes = lax.broadcasted_iota(jnp.int32, (GROUP, TILE), 1)
    subs = lax.broadcasted_iota(jnp.int32, (GROUP, TILE), 0)
    upper, inverse = [], []
    for step in range(TILE // GROUP):
        base = step * GROUP
        inside = (lanes >= base) & (lanes < base + GROUP)
        block = rows[step]
        first = [jnp.broadcast_to(block[t : t + 1, :], (GROUP, TILE)) for t in range(GROUP)]
        second = [
            jnp.where(inside, jnp.where(lanes == base + t, 1.0, 0.0), first[t])
            for t in range(GROUP)
        ]
        pivot = [
            [splat(first[t], base + u) if u >= t else None for u in range(GROUP)]
            for t in range(GROUP)
        ]
        coming = rows[step + 1] if step + 1 < TILE // GROUP else block
        factors = [splat(coming, base + u) for u in range(GROUP)]
        coming = jnp.where(inside, 0.0, coming)
        scale = [None] * GROUP
        for t in range(GROUP):
            scale[t] = lax.rsqrt(pivot[t][t])
            for u in range(t + 1, GROUP):
                pivot[t][u] = pivot[t][u] * scale[t]
            for u in range(t + 1, GROUP):
                for w in range(u, GROUP):
                    pivot[u][w] = pivot[u][w] - pivot[t][u] * pivot[t][w]
            first[t] = first[t] * scale[t]
            second[t] = second[t] * scale[t]
            factors[t] = factors[t] * scale[t]
            coming = coming - factors[t] * second[t]
            for u in range(t + 1, GROUP):
                first[u] = first[u] - pivot[t][u] * first[t]
                second[u] = second[u] - pivot[t][u] * second[t]
                factors[u] = factors[u] - pivot[t][u] * factors[t]
        solved = [None] * GROUP
        for t in reversed(range(GROUP)):
            value = second[t]
            for u in range(t + 1, GROUP):
                value = value - pivot[t][u] * solved[u]
            solved[t] = value * scale[t]
        if step + 1 < TILE // GROUP:
            rows[step + 1] = coming
        for later in range(step + 2, TILE // GROUP):
            value = jnp.where(inside, 0.0, rows[later])
            for t in range(GROUP):
                value = value - splat(rows[later], base + t) * solved[t]
            rows[later] = value
        upper_rows, inverse_rows = first[0], second[0]
        for t in range(1, GROUP):
            upper_rows = jnp.where(subs == t, first[t], upper_rows)
            inverse_rows = jnp.where(subs == t, second[t], inverse_rows)
        upper.append(upper_rows)
        inverse.append(inverse_rows)
    return upper, inverse


def factor_kernel(count, places_ref, damp_ref, exact_ref, *refs):
    lead_refs = refs[:count]
    lower_ref, inverse_ref, share_ref, work_ref, upper_ref = refs[-5:]
    steps = LEAD // TILE
    side = LEAD // count
    marks = sum(lead[2 * CAP + side :, :].astype(F32) for lead in lead_refs)
    row = lax.broadcasted_iota(jnp.int32, marks.shape, 0)
    weight = jnp.where(row < 4, jnp.where(row % 2 == 0, 256.0, 1.0), 0.0)
    total = jnp.sum(marks * weight, axis=0, keepdims=True)[:, :1]
    share = (1.0 - DECAY) / total
    share_ref[...] = jnp.broadcast_to(share, share_ref.shape)
    for q, lead in enumerate(lead_refs):
        begin = pl.multiple_of(places_ref[PLACES + q] * side, side)
        work_ref[pl.ds(begin, side), :] = lead[2 * CAP : 2 * CAP + side, :].astype(F32)

    @pl.when((places_ref[0] == 0) & (places_ref[1] == 0))
    def _():
        work_ref[...] = exact_ref[...]

    gram = sum(dot_t(lead[: 2 * CAP, :], lead[: 2 * CAP, :]) for lead in lead_refs)
    rows = lax.broadcasted_iota(jnp.int32, (LEAD, LEAD), 0)
    cols = lax.broadcasted_iota(jnp.int32, (LEAD, LEAD), 1)
    work_ref[...] = (
        DECAY * work_ref[...] + share * gram + jnp.where(rows == cols, damp_ref[0], 0.0)
    )
    lanes = lax.broadcasted_iota(jnp.int32, (GROUP, TILE), 1)
    subs = lax.broadcasted_iota(jnp.int32, (GROUP, TILE), 0)

    def tile_step(k, carry):
        begin = pl.multiple_of(k * TILE, TILE)
        rows = [
            work_ref[pl.ds(begin + g * GROUP, GROUP), pl.ds(begin, TILE)]
            for g in range(TILE // GROUP)
        ]
        upper, inverse = eliminate_tile(rows)
        upper_tile = jnp.concatenate(
            [jnp.where(lanes >= subs + g * GROUP, part, 0.0) for g, part in enumerate(upper)], 0
        )
        inverse_tile = jnp.concatenate(
            [jnp.where(lanes <= subs + g * GROUP, part, 0.0) for g, part in enumerate(inverse)], 0
        )
        band = dot_split(inverse_tile, work_ref[pl.ds(begin, TILE), :], ((1,), (0,)))
        work_ref[pl.ds(begin, TILE), :] = band
        work_ref[pl.ds(begin, TILE), pl.ds(begin, TILE)] = inverse_tile
        band = work_ref[pl.ds(begin, TILE), :]
        at = lax.broadcasted_iota(jnp.int32, (TILE, LEAD), 1)
        right = jnp.where(at >= begin + TILE, band, 0.0)
        inverse_ref[pl.ds(begin, TILE), :] = jnp.where(at < begin + TILE, band, 0.0)
        upper_ref[pl.ds(begin, TILE), :] = right
        upper_ref[pl.ds(begin, TILE), pl.ds(begin, TILE)] = upper_tile
        down = lax.broadcasted_iota(jnp.int32, (LEAD, TILE), 0)
        column = work_ref[:, pl.ds(begin, TILE)]
        work_ref[:, pl.ds(begin, TILE)] = jnp.where(down >= begin + TILE, 0.0, column)
        work_ref[...] = work_ref[...] - dot_split(right, band, ((0,), (0,)))
        return carry

    lax.fori_loop(0, steps, tile_step, 0)
    lower_ref[...] = upper_ref[...].T


def factor_lead(places, damp, exact, lead, earlier):
    shape = jax.ShapeDtypeStruct((LEAD, LEAD), F32)
    vmem = pl.BlockSpec(memory_space=pltpu.VMEM)
    smem = pl.BlockSpec(memory_space=pltpu.SMEM)
    return pl.pallas_call(
        lambda *refs: factor_kernel(len(lead), *refs),
        grid=(1,),
        out_shape=(shape, shape, jax.ShapeDtypeStruct((GROUP, TILE), F32)),
        in_specs=[smem, smem, pl.BlockSpec((LEAD, LEAD), lambda i: (0, 0))]
        + [vmem] * len(lead)
        + [ANYWHERE] * len(earlier),
        out_specs=(vmem, vmem, vmem),
        scratch_shapes=[pltpu.VMEM((LEAD, LEAD), F32)] * 2,
        compiler_params=pltpu.CompilerParams(vmem_limit_bytes=VMEM_BYTES),
        cost_estimate=NO_COST,
    )(places, damp, exact, *lead, *earlier)


def stack_kernel(count, places_ref, *refs):
    own, other = refs[:count], refs[count : 2 * count]
    stack_ref, near_ref = refs[-2:]
    depth, side = 2 * CAP, LEAD // count
    for q in range(count):
        stack_ref[q * depth : q * depth + CAP, :] = own[q][:CAP, :]
        stack_ref[q * depth + CAP : (q + 1) * depth, :] = other[q][...]
        begin = pl.multiple_of(places_ref[PLACES + q] * side, side)
        near_ref[pl.ds(begin, side), :] = own[q][CAP:, :]


def stacked(places, own, other, earlier):
    count = len(own)
    rows, width = own[0].shape
    cols = COLS if width % COLS == 0 else ROWS
    tiled = lambda height: pl.BlockSpec((height, cols), lambda j: (0, j))
    return pl.pallas_call(
        lambda *refs: stack_kernel(count, *refs),
        grid=(width // cols,),
        out_shape=(
            jax.ShapeDtypeStruct((2 * CAP * count, width), BF16),
            jax.ShapeDtypeStruct((LEAD, width), BF16),
        ),
        in_specs=[pl.BlockSpec(memory_space=pltpu.SMEM)]
        + [tiled(rows)] * count
        + [tiled(CAP)] * count
        + [ANYWHERE] * len(earlier),
        out_specs=(tiled(2 * CAP * count), tiled(LEAD)),
        compiler_params=pltpu.CompilerParams(vmem_limit_bytes=VMEM_BYTES),
        cost_estimate=NO_COST,
    )(places, *own, *other, *earlier)


def panel_kernel(count, share_ref, inverse_ref, near_ref, across_ref, *refs):
    lead = refs[:count]
    out_ref, lead_ref = refs[-2:]
    depth = 2 * CAP

    @pl.when(pl.program_id(0) == 0)
    def _():
        for q in range(count):
            lead_ref[q * depth : (q + 1) * depth, :] = lead[q][:depth, :]

    gram = dot_t(lead_ref[...], across_ref[...])
    beside = DECAY * near_ref[...].astype(F32) + share_ref[:1, :1] * gram
    out_ref[...] = dot_split(inverse_ref[...], beside, ((1,), (0,))).astype(BF16)


def panel_columns(share, inverse, near, lead, across, earlier):
    count = len(lead)
    tall, width = across.shape
    cols = COLS if width % COLS == 0 else ROWS
    whole = lambda height: pl.BlockSpec((height, LEAD), lambda j: (0, 0))
    tiled = lambda height: pl.BlockSpec((height, cols), lambda j: (0, j))
    return pl.pallas_call(
        lambda *refs: panel_kernel(count, *refs),
        grid=(width // cols,),
        out_shape=(
            jax.ShapeDtypeStruct((LEAD, width), BF16),
            jax.ShapeDtypeStruct((tall, LEAD), BF16),
        ),
        in_specs=[
            pl.BlockSpec((GROUP, TILE), lambda j: (0, 0)),
            whole(LEAD),
            tiled(LEAD),
            tiled(tall),
        ]
        + [whole(lead[0].shape[0])] * count
        + [ANYWHERE] * len(earlier),
        out_specs=(tiled(LEAD), whole(tall)),
        compiler_params=pltpu.CompilerParams(vmem_limit_bytes=VMEM_BYTES),
        cost_estimate=NO_COST,
    )(share, inverse, near, across, *lead, *earlier)


def solve_kernel(flag_ref, inverse_ref, first_ref, second_ref, *refs):
    high_ref, low_ref, parts_ref = refs[-3:]

    @pl.when(pl.program_id(0) == 0)
    def _():
        parts_ref[0], parts_ref[1] = split(inverse_ref[...])

    values = jnp.where(flag_ref[0] == 1, first_ref[...], second_ref[...])
    solved = jnp.dot(parts_ref[0], values, preferred_element_type=F32)
    solved = solved + jnp.dot(parts_ref[1], values, preferred_element_type=F32)
    high_ref[...], low_ref[...] = split(solved)


def solve_lead(flag, inverse, first, second, earlier):
    tiled = pl.BlockSpec((LEAD, COLS), lambda j: (0, j))
    return pl.pallas_call(
        solve_kernel,
        grid=(first.shape[1] // COLS,),
        out_shape=(jax.ShapeDtypeStruct(first.shape, BF16),) * 2,
        in_specs=[
            pl.BlockSpec(memory_space=pltpu.SMEM),
            pl.BlockSpec((LEAD, LEAD), lambda j: (0, 0)),
            tiled,
            tiled,
        ]
        + [ANYWHERE] * len(earlier),
        out_specs=(tiled, tiled),
        scratch_shapes=[pltpu.VMEM((2, LEAD, LEAD), BF16)],
        compiler_params=pltpu.CompilerParams(vmem_limit_bytes=VMEM_BYTES),
        cost_estimate=NO_COST,
    )(flag, inverse, first, second, *earlier)


def finish_kernel(
    count,
    begin,
    unread,
    places_ref,
    damp_ref,
    share_ref,
    factor_ref,
    panel_ref,
    inverse_ref,
    lead_ref,
    across_ref,
    *refs,
):
    first_chunk = begin == 0
    if first_chunk:
        lower_ref, *refs = refs
    mine = refs[:count]
    running_ref, factored_ref, panels_ref, token_ref, mine_ref, rows_ref, first_ref = refs[
        count + unread :
    ]
    j = pl.program_id(0)
    member, column, base = places_ref[0], places_ref[1], places_ref[2] + begin
    share, damp = share_ref[:1, :1], damp_ref[0]
    height, cols = running_ref.shape
    depth = 2 * CAP
    side = LEAD // count
    head = (member == 0) & first_chunk

    @pl.when(j == 0)
    def _():
        token_ref[...] = jnp.zeros_like(token_ref)
        for q in range(count):
            mine_ref[:, q * depth : (q + 1) * depth] = mine[q][0, :depth, :].T
            place = pl.multiple_of(places_ref[PLACES + q] * side, side)
            first_ref[pl.ds(place, side), :] = mine[q][0, depth : depth + side, :].astype(F32)
        source = first_ref[...].T
        if cols == LEAD:
            source = jnp.where(column == 0, factor_ref[...], source)
        gram = jnp.dot(mine_ref[...], lead_ref[...], preferred_element_type=F32)
        row = base + lax.broadcasted_iota(jnp.int32, (height, LEAD), 0)
        col = lax.broadcasted_iota(jnp.int32, (height, LEAD), 1)
        source = DECAY * source + share * gram
        source = source + jnp.where(row == col, damp, 0.0)
        rows_ref[...] = dot_split(source, inverse_ref[...], ((1,), (1,)))
        panels_ref[...] = rows_ref[...].astype(BF16)

    gram = jnp.dot(mine_ref[...], across_ref[...], preferred_element_type=F32)
    running = DECAY * factor_ref[...] + share * gram
    running_ref[...] = running
    row = base + lax.broadcasted_iota(jnp.int32, (height, cols), 0)
    col = (column * pl.num_programs(0) + j) * cols
    col = col + lax.broadcasted_iota(jnp.int32, (height, cols), 1)
    matrix = running + jnp.where(row == col, damp, 0.0)
    factored = matrix - jnp.dot(panels_ref[...], panel_ref[...], preferred_element_type=F32)
    factored_ref[...] = jnp.where(head, 0.0, factored)

    for part in range(LEAD // cols):
        edge = slice(part * cols, (part + 1) * cols)

        @pl.when((column == 0) & (j == part))
        def _():
            factored_ref[...] = rows_ref[:, edge]

            if first_chunk:

                @pl.when(head)
                def _():
                    factored_ref[...] = lower_ref[:, edge]


def finish_rows(
    begin, places, damp, share, factor, panel, inverse, lower, lead, across, mine, results, earlier
):
    count = len(mine)
    deep, height = mine[0].shape[1:]
    width, tall = factor.shape[0], lead.shape[0]
    start = begin // height
    cols = COLS if width % COLS == 0 else ROWS
    assert begin % height == 0

    def mine_spec(q):
        return pl.BlockSpec((1, deep, height), lambda j, p: (p[PLACES + count + q], 0, 0))

    factor_spec = pl.BlockSpec((height, cols), lambda j, p: (start, j))
    rows_spec = pl.BlockSpec((height, LEAD), lambda j, p: (start, 0))
    lead_whole = pl.BlockSpec((LEAD, LEAD), lambda j, p: (0, 0))
    small = pl.BlockSpec((GROUP, TILE), lambda j, p: (0, 0))
    in_specs = [
        pl.BlockSpec(memory_space=pltpu.SMEM),
        small,
        factor_spec,
        pl.BlockSpec((LEAD, cols), lambda j, p: (0, j)),
        lead_whole,
        pl.BlockSpec((tall, LEAD), lambda j, p: (0, 0)),
        pl.BlockSpec((tall, cols), lambda j, p: (0, j)),
    ]
    operands = [damp, share, factor, panel, inverse, lead, across]
    if begin == 0:
        in_specs += [lead_whole]
        operands += [lower]
    in_specs += [mine_spec(q) for q in range(count)]
    operands += mine
    aliases = {1 + len(operands) + k: k for k in range(len(results))}
    operands += [*results, *earlier]
    unread = len(results) + len(earlier)
    in_specs += [ANYWHERE] * unread
    return pl.pallas_call(
        lambda *refs: finish_kernel(count, begin, unread, *refs),
        grid_spec=pltpu.PrefetchScalarGridSpec(
            num_scalar_prefetch=1,
            grid=(width // cols,),
            in_specs=in_specs,
            out_specs=(factor_spec, factor_spec, rows_spec, small),
            scratch_shapes=[
                pltpu.VMEM((height, tall), BF16),
                pltpu.VMEM((height, LEAD), F32),
                pltpu.VMEM((LEAD, height), F32),
            ],
        ),
        out_shape=(
            jax.ShapeDtypeStruct(factor.shape, F32),
            jax.ShapeDtypeStruct(factor.shape, F32),
            jax.ShapeDtypeStruct((width, LEAD), BF16),
            jax.ShapeDtypeStruct((GROUP, TILE), F32),
        ),
        input_output_aliases=aliases,
        compiler_params=pltpu.CompilerParams(vmem_limit_bytes=VMEM_BYTES),
        cost_estimate=NO_COST,
    )(places, *operands)


def precond_kernel(first, places_ref, grad_ref, panels_ref, high_ref, low_ref, *refs):
    out_ref = refs[-1]
    product = jnp.dot(panels_ref[...], high_ref[...], preferred_element_type=F32)
    out_ref[...] = grad_ref[...].astype(F32) - product
    if first:

        @pl.when((places_ref[0] == 0) & (pl.program_id(1) == 0))
        def _():
            out_ref[...] = high_ref[...].astype(F32) + low_ref[...].astype(F32)


def precond_rows(begin, end, places, grad, panels, high, low, results):
    height = min(LEAD, end - begin)
    start = begin // height
    cols = COLS
    rows_spec = pl.BlockSpec((height, cols), lambda j, i: (start + i, j))
    tiled = pl.BlockSpec((LEAD, cols), lambda j, i: (0, j))
    low_spec = tiled if begin == 0 else ANYWHERE
    return pl.pallas_call(
        lambda *refs: precond_kernel(begin == 0, *refs),
        grid=(grad.shape[1] // cols, (end - begin) // height),
        out_shape=jax.ShapeDtypeStruct(grad.shape, F32),
        in_specs=[
            pl.BlockSpec(memory_space=pltpu.SMEM),
            rows_spec,
            pl.BlockSpec((height, LEAD), lambda j, i: (start + i, 0)),
            tiled,
            low_spec,
        ]
        + [ANYWHERE] * len(results),
        out_specs=rows_spec,
        input_output_aliases={5: 0} if results else {},
        compiler_params=pltpu.CompilerParams(vmem_limit_bytes=VMEM_BYTES),
        cost_estimate=NO_COST,
    )(places, grad, panels, high, low, *results)


def swapped(value, mask):
    size = lax.axis_size("tok")
    return lax.ppermute(value, "tok", [(source, source ^ mask) for source in range(size)])


def gather_members(value, bits):
    pieces = [value]
    for bit in reversed(range(bits)):
        pieces = pieces + [swapped(piece, 1 << bit) for piece in pieces]
    return pieces


def copy_kernel(count, places_ref, *refs):
    for source, out in zip(refs[:count], refs[-count:]):
        out[...] = source[...].astype(BF16)


def copied(requests, earlier):
    in_specs, out_specs, shapes, places = [], [], [], []
    for array, block, place in requests:
        at = len(places)
        places += place
        shape = tuple(size for size in block if size is not None)
        shapes.append(shape)
        in_specs.append(
            pl.BlockSpec(block, lambda i, p, a=at, n=len(block): tuple(p[a + k] for k in range(n)))
        )
        out_specs.append(pl.BlockSpec(shape, lambda i, p: (0, 0)))
    arrays = [array for array, _, _ in requests]
    return pl.pallas_call(
        lambda *refs: copy_kernel(len(arrays), *refs),
        grid_spec=pltpu.PrefetchScalarGridSpec(
            num_scalar_prefetch=1,
            grid=(1,),
            in_specs=in_specs + [ANYWHERE] * len(earlier),
            out_specs=out_specs,
        ),
        out_shape=[jax.ShapeDtypeStruct(shape, BF16) for shape in shapes],
        compiler_params=pltpu.CompilerParams(vmem_limit_bytes=VMEM_BYTES),
        cost_estimate=NO_COST,
    )(jnp.stack([jnp.int32(place) for place in places]), *arrays, *earlier)


def choose_kernel(flag_ref, first_ref, second_ref, *refs):
    refs[-1][...] = jnp.where(flag_ref[0] == 1, first_ref[...], second_ref[...])


def chosen(flag, first, second, earlier):
    tiled = pl.BlockSpec((first.shape[0] // 2, first.shape[1]), lambda i: (i, 0))
    return pl.pallas_call(
        choose_kernel,
        grid=(2,),
        out_shape=jax.ShapeDtypeStruct(first.shape, first.dtype),
        in_specs=[pl.BlockSpec(memory_space=pltpu.SMEM), tiled, tiled] + [ANYWHERE] * len(earlier),
        out_specs=tiled,
        compiler_params=pltpu.CompilerParams(vmem_limit_bytes=VMEM_BYTES),
        cost_estimate=NO_COST,
    )(flag, first, second, *earlier)


def member_blocks(blocks, member, group):
    _, rows, width = blocks.shape
    return [(blocks, (None, rows, width), [member ^ other, 0, 0]) for other in range(1, group)]


def first_hop(blocks, sent, bits):
    held = [[blocks]] + [[part] for part in sent]
    return hop(held, bits - 1)


def hop(held, bit):
    half = 1 << bit
    return [
        kept + [swapped(part, half) for part in passed]
        for kept, passed in zip(held[:half], held[half:])
    ]


def exchange_members(held, bits, requests, earlier):
    copies = None
    for bit in reversed(range(bits - 1)):
        half = 1 << bit
        arrived = [(part, part.shape, [0, 0]) for passed in held[half:] for part in passed[1:]]
        if arrived:
            asked = requests + arrived if copies is None else arrived
            passing = list(copied(asked, earlier + held[0][1:]))
            if copies is None:
                copies, passing = passing[: len(requests)], passing[len(requests) :]
            for passed in held[half:]:
                count = len(passed) - 1
                passed[1:], passing = passing[:count], passing[count:]
        held = hop(held, bit)
    first, *others = held[0]
    return [first] + [part[None] for part in others], copies


def member_order(bits):
    order = [0]
    for bit in reversed(range(bits)):
        order = order + [other ^ (1 << bit) for other in order]
    return order


def down_pairs(bit, group):
    mask = 1 << bit
    return [
        (source, source + mask)
        for source in range(lax.axis_size("tok"))
        if source % group % (2 * mask) == 0
    ]


def share_of_first(lower, upper, member, group, bits):
    for bit in reversed(range(bits)):
        moved = lax.ppermute(upper, "tok", down_pairs(bit, group))
        blocks = jnp.where(member >> bit & 1 == 1, moved, lower)
        half = blocks.shape[0] // 2
        lower, upper = blocks[:half], blocks[half:]
    return blocks


def count_rows(number, row, width):
    index = lax.broadcasted_iota(jnp.int32, (16, width), 0)
    rest = jnp.where(index == row + 1, number % 256, 0)
    return jnp.where(index == row, number // 256, rest).astype(BF16)


def local(grad_rows, routes, counts, factor_old, damping, weight_grad):
    group = lax.axis_size("tok") // 2
    bits = group.bit_length() - 1
    position = lax.axis_index("tok")
    expert = position // group
    member = position % group
    column = lax.axis_index("fac")
    tok_rows, width = grad_rows.shape
    damp = jnp.where(expert == 0, damping[0], damping[1])[None]
    order = [member ^ other for other in member_order(bits)]

    side = LEAD // 2
    halves = [(factor_old, (side, width), [place, 0]) for place in range(2)]
    halves = copied(halves, [])
    lead_factor = share_of_first(*halves, member, group, bits)

    live = jnp.arange(tok_rows) < counts[0]
    named = routes[:, 0]
    own = live & (named == expert)
    away = live & (named != expert)
    flags = jnp.stack([own, away])
    ranks = jnp.cumsum(flags.astype(jnp.int32), 1) - 1
    picker = (ranks[:, None, :] == jnp.arange(CAP)[None, :, None]) & flags[:, None, :]
    packed = jnp.dot(
        picker.reshape(2 * CAP, tok_rows).astype(BF16), grad_rows, preferred_element_type=F32
    ).astype(BF16)
    tally = jnp.sum(flags.astype(jnp.int32), 1)
    front = swapped(
        jnp.concatenate([packed[CAP:, :LEAD], count_rows(tally[1], 2, LEAD)], 0), group
    )
    first_part = jnp.concatenate(
        [
            packed[:CAP, :LEAD],
            front[:CAP],
            lead_factor[:, :LEAD],
            front[CAP:] + count_rows(tally[0], 0, LEAD),
        ],
        0,
    )
    away_rows = copied([(packed, (CAP, width), [1, 0])], [front])[0]
    incoming = swapped(away_rows, group)
    outgoing = jnp.concatenate([packed[:CAP], lead_factor], 0)
    quarter = jnp.concatenate([packed[:CAP], incoming, lead_factor], 0)
    across_own = gather_members(outgoing, bits)
    across_other = gather_members(incoming, bits)

    ends = [end for end in (LEAD, 2 * LEAD, 2 * LEAD + ROWS) if end < width] + [width]
    chunks = list(zip([0, *ends], ends))
    rows = quarter.shape[0]
    later = [
        (quarter, (rows, end - begin), [0, begin // (end - begin)]) for begin, end in chunks[1:]
    ]
    parts = [first_part, *copied(later, [across_own[1]])]
    spread = [lax.all_gather(part, "fac") for part in parts]
    rows = first_part.shape[0]
    earlier = [across_other[1], *parts[1:]]
    requests = [(spread[0], (None, rows, LEAD), [0, 0, 0])]
    lead = copied(requests, earlier)[0]
    slots = [member, column, member * width] + order + [member] + [0] * (group - 1)
    assert len(slots) == PLACES + 2 * group
    slots = jnp.stack([jnp.int32(slot) for slot in slots])
    across, near_factor = stacked(slots, across_own, across_other, [lead])
    lead = gather_members(lead, bits)
    sent = copied(member_blocks(spread[0], member, group), [lead[1], across])
    held = first_hop(spread[0], sent, bits)
    near = copied([(weight_grad, (LEAD, weight_grad.shape[1]), [0, 0])], sent[:1])[0]
    lower, inverse, share = factor_lead(slots, damp, factor_old, lead, [near])
    panel, lead_stack = panel_columns(
        share, inverse, near_factor, lead, across, spread[1:2]
    )

    token = panel
    results, precond = [], []
    cut = LEAD * max(1, (width - 1) // LEAD)
    for number, (begin, _) in enumerate(chunks):
        requests = []
        if number + 1 < len(chunks):
            requests = member_blocks(spread[number + 1], member, group)
        if number:
            held = first_hop(spread[number], sent, bits)
        pieces, sent = exchange_members(held, bits, requests, [token])
        gates = sent[:1]
        if number == 0:
            for bit in reversed(range(bits)):
                moved = lax.ppermute(near, "tok", down_pairs(bit, group))
                flag = (member >> bit & 1)[None]
                if bit:
                    near = chosen(flag, moved, near, gates)
            high, low = solve_lead(flag, inverse, moved, near, [])
            gates = gates + [high]
        if number + 1 == len(chunks):
            precond = [precond_rows(0, cut, slots, weight_grad, results[2], high, low, [])]
        *results, token = finish_rows(
            begin,
            slots,
            damp,
            share,
            factor_old,
            panel,
            inverse,
            lower,
            lead_stack,
            across,
            pieces,
            results,
            gates + precond,
        )
    running, factored, panels = results
    precond = precond_rows(cut, width, slots, weight_grad, panels, high, low, precond)
    return (running, factored, precond)


def solution(mesh):
    placed = (P("tok", "fac"), P("tok", None), P("tok"), P("tok", "fac"), P(), P("tok", "fac"))
    return jax.shard_map(
        local,
        mesh=mesh,
        in_specs=placed,
        out_specs=(P("tok", "fac"), P("tok", "fac"), P("tok", "fac")),
        check_vma=False,
    )
```

```python
import jax
import jax.numpy as jnp
from jax import lax
from jax.experimental import pallas as pl
from jax.experimental.pallas import tpu as pltpu
from jax.sharding import PartitionSpec as P

CAP = 320
LEAD = 512
TILE = 128
GROUP = 8
ROWS = 256
COLS = 512
PLACES = 3
VMEM_BYTES = 60 * 1024 * 1024
ANYWHERE = pl.BlockSpec(memory_space=pl.ANY)
NO_COST = pl.CostEstimate(flops=1, bytes_accessed=1, transcendentals=0)
DECAY = 0.8

HIGHEST = lax.Precision.HIGHEST
BF16 = jnp.bfloat16
F32 = jnp.float32


def dot_t(left, right, precision=None):
    return lax.dot_general(
        left, right, (((0,), (0,)), ((), ())), precision=precision, preferred_element_type=F32
    )


def split(value):
    high = value.astype(BF16)
    return high, (value - high.astype(F32)).astype(BF16)


def dot_split(left, right, contract):
    (left_high, left_low), (right_high, right_low) = split(left), split(right)
    product = lambda a, b: lax.dot_general(
        a, b, (contract, ((), ())), preferred_element_type=F32
    )
    return product(left_high, right_high) + (
        product(left_high, right_low) + product(left_low, right_high)
    )


def splat(rows, lane):
    return jnp.broadcast_to(rows[:, lane : lane + 1], rows.shape)


def eliminate_tile(rows):
    lanes = lax.broadcasted_iota(jnp.int32, (GROUP, TILE), 1)
    subs = lax.broadcasted_iota(jnp.int32, (GROUP, TILE), 0)
    upper, inverse = [], []
    for step in range(TILE // GROUP):
        base = step * GROUP
        inside = (lanes >= base) & (lanes < base + GROUP)
        block = rows[step]
        first = [jnp.broadcast_to(block[t : t + 1, :], (GROUP, TILE)) for t in range(GROUP)]
        second = [
            jnp.where(inside, jnp.where(lanes == base + t, 1.0, 0.0), first[t])
            for t in range(GROUP)
        ]
        pivot = [
            [splat(first[t], base + u) if u >= t else None for u in range(GROUP)]
            for t in range(GROUP)
        ]
        coming = rows[step + 1] if step + 1 < TILE // GROUP else block
        factors = [splat(coming, base + u) for u in range(GROUP)]
        coming = jnp.where(inside, 0.0, coming)
        scale = [None] * GROUP
        for t in range(GROUP):
            scale[t] = lax.rsqrt(pivot[t][t])
            for u in range(t + 1, GROUP):
                pivot[t][u] = pivot[t][u] * scale[t]
            for u in range(t + 1, GROUP):
                for w in range(u, GROUP):
                    pivot[u][w] = pivot[u][w] - pivot[t][u] * pivot[t][w]
            first[t] = first[t] * scale[t]
            second[t] = second[t] * scale[t]
            factors[t] = factors[t] * scale[t]
            coming = coming - factors[t] * second[t]
            for u in range(t + 1, GROUP):
                first[u] = first[u] - pivot[t][u] * first[t]
                second[u] = second[u] - pivot[t][u] * second[t]
                factors[u] = factors[u] - pivot[t][u] * factors[t]
        solved = [None] * GROUP
        for t in reversed(range(GROUP)):
            value = second[t]
            for u in range(t + 1, GROUP):
                value = value - pivot[t][u] * solved[u]
            solved[t] = value * scale[t]
        if step + 1 < TILE // GROUP:
            rows[step + 1] = coming
        for later in range(step + 2, TILE // GROUP):
            value = jnp.where(inside, 0.0, rows[later])
            for t in range(GROUP):
                value = value - splat(rows[later], base + t) * solved[t]
            rows[later] = value
        upper_rows, inverse_rows = first[0], second[0]
        for t in range(1, GROUP):
            upper_rows = jnp.where(subs == t, first[t], upper_rows)
            inverse_rows = jnp.where(subs == t, second[t], inverse_rows)
        upper.append(upper_rows)
        inverse.append(inverse_rows)
    return upper, inverse


def factor_kernel(count, places_ref, damp_ref, exact_ref, *refs):
    lead_refs = refs[:count]
    lower_ref, inverse_ref, share_ref, work_ref, upper_ref = refs[-5:]
    steps = LEAD // TILE
    side = LEAD // count
    marks = sum(lead[2 * CAP + side :, :].astype(F32) for lead in lead_refs)
    row = lax.broadcasted_iota(jnp.int32, marks.shape, 0)
    weight = jnp.where(row < 4, jnp.where(row % 2 == 0, 256.0, 1.0), 0.0)
    total = jnp.sum(marks * weight, axis=0, keepdims=True)[:, :1]
    share = (1.0 - DECAY) / total
    share_ref[...] = jnp.broadcast_to(share, share_ref.shape)
    for q, lead in enumerate(lead_refs):
        begin = pl.multiple_of(places_ref[PLACES + q] * side, side)
        work_ref[pl.ds(begin, side), :] = lead[2 * CAP : 2 * CAP + side, :].astype(F32)

    @pl.when((places_ref[0] == 0) & (places_ref[1] == 0))
    def _():
        work_ref[...] = exact_ref[...]

    gram = sum(dot_t(lead[: 2 * CAP, :], lead[: 2 * CAP, :]) for lead in lead_refs)
    rows = lax.broadcasted_iota(jnp.int32, (LEAD, LEAD), 0)
    cols = lax.broadcasted_iota(jnp.int32, (LEAD, LEAD), 1)
    work_ref[...] = (
        DECAY * work_ref[...] + share * gram + jnp.where(rows == cols, damp_ref[0], 0.0)
    )
    lanes = lax.broadcasted_iota(jnp.int32, (GROUP, TILE), 1)
    subs = lax.broadcasted_iota(jnp.int32, (GROUP, TILE), 0)

    def tile_step(k, carry):
        begin = pl.multiple_of(k * TILE, TILE)
        rows = [
            work_ref[pl.ds(begin + g * GROUP, GROUP), pl.ds(begin, TILE)]
            for g in range(TILE // GROUP)
        ]
        upper, inverse = eliminate_tile(rows)
        upper_tile = jnp.concatenate(
            [jnp.where(lanes >= subs + g * GROUP, part, 0.0) for g, part in enumerate(upper)], 0
        )
        inverse_tile = jnp.concatenate(
            [jnp.where(lanes <= subs + g * GROUP, part, 0.0) for g, part in enumerate(inverse)], 0
        )
        band = dot_split(inverse_tile, work_ref[pl.ds(begin, TILE), :], ((1,), (0,)))
        work_ref[pl.ds(begin, TILE), :] = band
        work_ref[pl.ds(begin, TILE), pl.ds(begin, TILE)] = inverse_tile
        band = work_ref[pl.ds(begin, TILE), :]
        at = lax.broadcasted_iota(jnp.int32, (TILE, LEAD), 1)
        right = jnp.where(at >= begin + TILE, band, 0.0)
        inverse_ref[pl.ds(begin, TILE), :] = jnp.where(at < begin + TILE, band, 0.0)
        upper_ref[pl.ds(begin, TILE), :] = right
        upper_ref[pl.ds(begin, TILE), pl.ds(begin, TILE)] = upper_tile
        down = lax.broadcasted_iota(jnp.int32, (LEAD, TILE), 0)
        column = work_ref[:, pl.ds(begin, TILE)]
        work_ref[:, pl.ds(begin, TILE)] = jnp.where(down >= begin + TILE, 0.0, column)
        work_ref[...] = work_ref[...] - dot_split(right, band, ((0,), (0,)))
        return carry

    lax.fori_loop(0, steps, tile_step, 0)
    lower_ref[...] = upper_ref[...].T


def factor_lead(places, damp, exact, lead, earlier):
    shape = jax.ShapeDtypeStruct((LEAD, LEAD), F32)
    vmem = pl.BlockSpec(memory_space=pltpu.VMEM)
    smem = pl.BlockSpec(memory_space=pltpu.SMEM)
    return pl.pallas_call(
        lambda *refs: factor_kernel(len(lead), *refs),
        grid=(1,),
        out_shape=(shape, shape, jax.ShapeDtypeStruct((GROUP, TILE), F32)),
        in_specs=[smem, smem, pl.BlockSpec((LEAD, LEAD), lambda i: (0, 0))]
        + [vmem] * len(lead)
        + [ANYWHERE] * len(earlier),
        out_specs=(vmem, vmem, vmem),
        scratch_shapes=[pltpu.VMEM((LEAD, LEAD), F32)] * 2,
        compiler_params=pltpu.CompilerParams(vmem_limit_bytes=VMEM_BYTES),
        cost_estimate=NO_COST,
    )(places, damp, exact, *lead, *earlier)


def stack_kernel(count, places_ref, *refs):
    own, other = refs[:count], refs[count : 2 * count]
    stack_ref, near_ref = refs[-2:]
    depth, side = 2 * CAP, LEAD // count
    for q in range(count):
        stack_ref[q * depth : q * depth + CAP, :] = own[q][:CAP, :]
        stack_ref[q * depth + CAP : (q + 1) * depth, :] = other[q][...]
        begin = pl.multiple_of(places_ref[PLACES + q] * side, side)
        near_ref[pl.ds(begin, side), :] = own[q][CAP:, :]


def stacked(places, own, other, earlier):
    count = len(own)
    rows, width = own[0].shape
    cols = COLS if width % COLS == 0 else ROWS
    tiled = lambda height: pl.BlockSpec((height, cols), lambda j: (0, j))
    return pl.pallas_call(
        lambda *refs: stack_kernel(count, *refs),
        grid=(width // cols,),
        out_shape=(
            jax.ShapeDtypeStruct((2 * CAP * count, width), BF16),
            jax.ShapeDtypeStruct((LEAD, width), BF16),
        ),
        in_specs=[pl.BlockSpec(memory_space=pltpu.SMEM)]
        + [tiled(rows)] * count
        + [tiled(CAP)] * count
        + [ANYWHERE] * len(earlier),
        out_specs=(tiled(2 * CAP * count), tiled(LEAD)),
        compiler_params=pltpu.CompilerParams(vmem_limit_bytes=VMEM_BYTES),
        cost_estimate=NO_COST,
    )(places, *own, *other, *earlier)


def panel_kernel(count, share_ref, inverse_ref, near_ref, across_ref, *refs):
    lead = refs[:count]
    out_ref, lead_ref = refs[-2:]
    depth = 2 * CAP

    @pl.when(pl.program_id(0) == 0)
    def _():
        for q in range(count):
            lead_ref[q * depth : (q + 1) * depth, :] = lead[q][:depth, :]

    gram = dot_t(lead_ref[...], across_ref[...])
    beside = DECAY * near_ref[...].astype(F32) + share_ref[:1, :1] * gram
    out_ref[...] = dot_split(inverse_ref[...], beside, ((1,), (0,))).astype(BF16)


def panel_columns(share, inverse, near, lead, across, earlier):
    count = len(lead)
    tall, width = across.shape
    cols = COLS if width % COLS == 0 else ROWS
    whole = lambda height: pl.BlockSpec((height, LEAD), lambda j: (0, 0))
    tiled = lambda height: pl.BlockSpec((height, cols), lambda j: (0, j))
    return pl.pallas_call(
        lambda *refs: panel_kernel(count, *refs),
        grid=(width // cols,),
        out_shape=(
            jax.ShapeDtypeStruct((LEAD, width), BF16),
            jax.ShapeDtypeStruct((tall, LEAD), BF16),
        ),
        in_specs=[
            pl.BlockSpec((GROUP, TILE), lambda j: (0, 0)),
            whole(LEAD),
            tiled(LEAD),
            tiled(tall),
        ]
        + [whole(lead[0].shape[0])] * count
        + [ANYWHERE] * len(earlier),
        out_specs=(tiled(LEAD), whole(tall)),
        compiler_params=pltpu.CompilerParams(vmem_limit_bytes=VMEM_BYTES),
        cost_estimate=NO_COST,
    )(share, inverse, near, across, *lead, *earlier)


def solve_kernel(flag_ref, inverse_ref, first_ref, second_ref, *refs):
    high_ref, low_ref, parts_ref = refs[-3:]

    @pl.when(pl.program_id(0) == 0)
    def _():
        parts_ref[0], parts_ref[1] = split(inverse_ref[...])

    values = jnp.where(flag_ref[0] == 1, first_ref[...], second_ref[...])
    solved = jnp.dot(parts_ref[0], values, preferred_element_type=F32)
    solved = solved + jnp.dot(parts_ref[1], values, preferred_element_type=F32)
    high_ref[...], low_ref[...] = split(solved)


def solve_lead(flag, inverse, first, second, earlier):
    tiled = pl.BlockSpec((LEAD, COLS), lambda j: (0, j))
    return pl.pallas_call(
        solve_kernel,
        grid=(first.shape[1] // COLS,),
        out_shape=(jax.ShapeDtypeStruct(first.shape, BF16),) * 2,
        in_specs=[
            pl.BlockSpec(memory_space=pltpu.SMEM),
            pl.BlockSpec((LEAD, LEAD), lambda j: (0, 0)),
            tiled,
            tiled,
        ]
        + [ANYWHERE] * len(earlier),
        out_specs=(tiled, tiled),
        scratch_shapes=[pltpu.VMEM((2, LEAD, LEAD), BF16)],
        compiler_params=pltpu.CompilerParams(vmem_limit_bytes=VMEM_BYTES),
        cost_estimate=NO_COST,
    )(flag, inverse, first, second, *earlier)


def finish_kernel(
    count,
    gram_steps,
    begin,
    unread,
    places_ref,
    damp_ref,
    share_ref,
    factor_ref,
    grad_ref,
    panel_ref,
    inverse_ref,
    high_ref,
    lead_ref,
    across_ref,
    *refs,
):
    first_chunk = begin == 0
    if first_chunk:
        lower_ref, low_ref, *refs = refs
    mine = refs[:count]
    outs = refs[count + unread :]
    running_ref, factored_ref, precond_ref, token_ref, mine_ref, rows_ref, first_ref = outs
    j, i = pl.program_id(0), pl.program_id(1)
    member, column, base = places_ref[0], places_ref[1], places_ref[2] + begin
    share, damp = share_ref[:1, :1], damp_ref[0]
    height, cols = running_ref.shape
    depth = 2 * CAP
    side = LEAD // count
    span = pl.ds(pl.multiple_of(i * height, height), height)
    head = (member == 0) & first_chunk

    @pl.when(j == 0)
    def _():
        token_ref[...] = jnp.zeros_like(token_ref)
        for q in range(count):
            mine_ref[span, q * depth : (q + 1) * depth] = mine[q][0, :depth, :].T
            place = pl.multiple_of(places_ref[PLACES + q] * side, side)
            first_ref[pl.ds(place, side), :] = mine[q][0, depth : depth + side, :].astype(F32)
        source = first_ref[...].T
        if cols == LEAD:
            source = jnp.where(column == 0, factor_ref[...], source)
        gram = jnp.dot(mine_ref[span, :], lead_ref[...], preferred_element_type=F32)
        row = base + i * height + lax.broadcasted_iota(jnp.int32, (height, LEAD), 0)
        col = lax.broadcasted_iota(jnp.int32, (height, LEAD), 1)
        source = DECAY * source + share * gram
        source = source + jnp.where(row == col, damp, 0.0)
        rows_ref[span, :] = dot_split(source, inverse_ref[...], ((1,), (1,)))

    panel = rows_ref[span, :].astype(BF16)

    @pl.when(j < gram_steps)
    def _():
        gram = jnp.dot(mine_ref[span, :], across_ref[...], preferred_element_type=F32)
        running = DECAY * factor_ref[...] + share * gram
        running_ref[...] = running
        row = base + i * height + lax.broadcasted_iota(jnp.int32, (height, cols), 0)
        col = (column * gram_steps + j) * cols + lax.broadcasted_iota(jnp.int32, (height, cols), 1)
        matrix = running + jnp.where(row == col, damp, 0.0)
        factored = matrix - jnp.dot(panel, panel_ref[...], preferred_element_type=F32)
        factored_ref[...] = jnp.where(head, 0.0, factored)

        for part in range(LEAD // cols):
            edge = slice(part * cols, (part + 1) * cols)

            @pl.when((column == 0) & (j == part))
            def _():
                factored_ref[...] = rows_ref[span, edge]

                if first_chunk:

                    @pl.when(head)
                    def _():
                        factored_ref[...] = lower_ref[span, edge]

    product = jnp.dot(panel, high_ref[...], preferred_element_type=F32)
    precond_ref[...] = grad_ref[...].astype(F32) - product

    if first_chunk:

        @pl.when(head)
        def _():
            precond_ref[...] = high_ref[span, :].astype(F32) + low_ref[span, :].astype(F32)


def finish_rows(
    begin, places, damp, share, factor, grad, panel, inverse, lower, high, low,
    lead, across, mine, results, earlier,
):
    count = len(mine)
    deep, rows = mine[0].shape[1:]
    width, grad_cols = factor.shape[0], grad.shape[1]
    tall = lead.shape[0]
    height = min(rows, COLS)
    tiles = rows // height
    start = begin // height
    cols = COLS if width % COLS == 0 else ROWS
    gram_steps, steps = width // cols, grad_cols // cols
    assert steps >= gram_steps and rows % height == 0 and begin % height == 0

    def mine_spec(q):
        return pl.BlockSpec(
            (1, deep, height),
            lambda j, i, p: (p[PLACES + count + q], 0, jnp.where(j == 0, i, tiles - 1)),
        )

    def gram_col(j):
        return jnp.minimum(j, gram_steps - 1)

    def gram_tile(j, i, p):
        return (start + jnp.where(j < gram_steps, i, tiles - 1), gram_col(j))

    grad_spec = pl.BlockSpec((height, cols), lambda j, i, p: (start + i, j))
    factor_spec = pl.BlockSpec((height, cols), gram_tile)
    lead_whole = pl.BlockSpec((LEAD, LEAD), lambda j, i, p: (0, 0))
    small = pl.BlockSpec((GROUP, TILE), lambda j, i, p: (0, 0))
    in_specs = [
        pl.BlockSpec(memory_space=pltpu.SMEM),
        small,
        factor_spec,
        grad_spec,
        pl.BlockSpec((LEAD, cols), lambda j, i, p: (0, gram_col(j))),
        lead_whole,
        pl.BlockSpec((LEAD, cols), lambda j, i, p: (0, j)),
        pl.BlockSpec((tall, LEAD), lambda j, i, p: (0, 0)),
        pl.BlockSpec((tall, cols), lambda j, i, p: (0, gram_col(j))),
    ]
    operands = [damp, share, factor, grad, panel, inverse, high, lead, across]
    if begin == 0:
        in_specs += [lead_whole, pl.BlockSpec((LEAD, cols), lambda j, i, p: (0, j))]
        operands += [lower, low]
    in_specs += [mine_spec(q) for q in range(count)]
    operands += mine
    aliases = {1 + len(operands) + k: k for k in range(len(results))}
    operands += [*results, *earlier]
    unread = len(results) + len(earlier)
    in_specs += [ANYWHERE] * unread
    return pl.pallas_call(
        lambda *refs: finish_kernel(count, gram_steps, begin, unread, *refs),
        grid_spec=pltpu.PrefetchScalarGridSpec(
            num_scalar_prefetch=1,
            grid=(steps, tiles),
            in_specs=in_specs,
            out_specs=(factor_spec, factor_spec, grad_spec, small),
            scratch_shapes=[
                pltpu.VMEM((rows, tall), BF16),
                pltpu.VMEM((rows, LEAD), F32),
                pltpu.VMEM((LEAD, height), F32),
            ],
        ),
        out_shape=(
            jax.ShapeDtypeStruct(factor.shape, F32),
            jax.ShapeDtypeStruct(factor.shape, F32),
            jax.ShapeDtypeStruct(grad.shape, F32),
            jax.ShapeDtypeStruct((GROUP, TILE), F32),
        ),
        input_output_aliases=aliases,
        compiler_params=pltpu.CompilerParams(vmem_limit_bytes=VMEM_BYTES),
        cost_estimate=NO_COST,
    )(places, *operands)


def swapped(value, mask):
    size = lax.axis_size("tok")
    return lax.ppermute(value, "tok", [(source, source ^ mask) for source in range(size)])


def gather_members(value, bits):
    pieces = [value]
    for bit in reversed(range(bits)):
        pieces = pieces + [swapped(piece, 1 << bit) for piece in pieces]
    return pieces


def copy_kernel(count, places_ref, *refs):
    for source, out in zip(refs[:count], refs[-count:]):
        out[...] = source[...].astype(BF16)


def copied(requests, earlier):
    in_specs, out_specs, shapes, places = [], [], [], []
    for array, block, place in requests:
        at = len(places)
        places += place
        shape = tuple(size for size in block if size is not None)
        shapes.append(shape)
        in_specs.append(
            pl.BlockSpec(block, lambda i, p, a=at, n=len(block): tuple(p[a + k] for k in range(n)))
        )
        out_specs.append(pl.BlockSpec(shape, lambda i, p: (0, 0)))
    arrays = [array for array, _, _ in requests]
    return pl.pallas_call(
        lambda *refs: copy_kernel(len(arrays), *refs),
        grid_spec=pltpu.PrefetchScalarGridSpec(
            num_scalar_prefetch=1,
            grid=(1,),
            in_specs=in_specs + [ANYWHERE] * len(earlier),
            out_specs=out_specs,
        ),
        out_shape=[jax.ShapeDtypeStruct(shape, BF16) for shape in shapes],
        compiler_params=pltpu.CompilerParams(vmem_limit_bytes=VMEM_BYTES),
        cost_estimate=NO_COST,
    )(jnp.stack([jnp.int32(place) for place in places]), *arrays, *earlier)


def choose_kernel(flag_ref, first_ref, second_ref, *refs):
    refs[-1][...] = jnp.where(flag_ref[0] == 1, first_ref[...], second_ref[...])


def chosen(flag, first, second, earlier):
    tiled = pl.BlockSpec((first.shape[0] // 2, first.shape[1]), lambda i: (i, 0))
    return pl.pallas_call(
        choose_kernel,
        grid=(2,),
        out_shape=jax.ShapeDtypeStruct(first.shape, first.dtype),
        in_specs=[pl.BlockSpec(memory_space=pltpu.SMEM), tiled, tiled] + [ANYWHERE] * len(earlier),
        out_specs=tiled,
        compiler_params=pltpu.CompilerParams(vmem_limit_bytes=VMEM_BYTES),
        cost_estimate=NO_COST,
    )(flag, first, second, *earlier)


def member_blocks(blocks, member, group):
    _, rows, width = blocks.shape
    return [(blocks, (None, rows, width), [member ^ other, 0, 0]) for other in range(1, group)]


def exchange_members(blocks, sent, bits, requests, earlier):
    held = [[blocks]] + [[part] for part in sent]
    copies = None
    for bit in reversed(range(bits)):
        half = 1 << bit
        arrived = [(part, part.shape, [0, 0]) for passed in held[half:] for part in passed[1:]]
        if arrived:
            passing = copied(
                requests + arrived if copies is None else arrived, earlier + held[0][1:]
            )
            if copies is None:
                copies, passing = passing[: len(requests)], passing[len(requests) :]
            for passed in held[half:]:
                count = len(passed) - 1
                passed[1:], passing = passing[:count], passing[count:]
        held = [
            kept + [swapped(part, half) for part in passed]
            for kept, passed in zip(held[:half], held[half:])
        ]
    first, *others = held[0]
    return [first] + [part[None] for part in others], copies


def member_order(bits):
    order = [0]
    for bit in reversed(range(bits)):
        order = order + [other ^ (1 << bit) for other in order]
    return order


def down_pairs(bit, group):
    mask = 1 << bit
    return [
        (source, source + mask)
        for source in range(lax.axis_size("tok"))
        if source % group % (2 * mask) == 0
    ]


def share_of_first(lower, upper, member, group, bits):
    for bit in reversed(range(bits)):
        moved = lax.ppermute(upper, "tok", down_pairs(bit, group))
        blocks = jnp.where(member >> bit & 1 == 1, moved, lower)
        half = blocks.shape[0] // 2
        lower, upper = blocks[:half], blocks[half:]
    return blocks


def count_rows(number, row, width):
    index = lax.broadcasted_iota(jnp.int32, (16, width), 0)
    rest = jnp.where(index == row + 1, number % 256, 0)
    return jnp.where(index == row, number // 256, rest).astype(BF16)


def local(grad_rows, routes, counts, factor_old, damping, weight_grad):
    group = lax.axis_size("tok") // 2
    bits = group.bit_length() - 1
    position = lax.axis_index("tok")
    expert = position // group
    member = position % group
    column = lax.axis_index("fac")
    tok_rows, width = grad_rows.shape
    damp = jnp.where(expert == 0, damping[0], damping[1])[None]
    order = [member ^ other for other in member_order(bits)]

    side = LEAD // 2
    halves = [(factor_old, (side, width), [place, 0]) for place in range(2)]
    halves = copied(halves, [])
    lead_factor = share_of_first(*halves, member, group, bits)

    near = copied([(weight_grad, (LEAD, weight_grad.shape[1]), [0, 0])], halves[:1])[0]
    moved = lax.ppermute(near, "tok", down_pairs(bits - 1, group))

    live = jnp.arange(tok_rows) < counts[0]
    named = routes[:, 0]
    own = live & (named == expert)
    away = live & (named != expert)
    flags = jnp.stack([own, away])
    ranks = jnp.cumsum(flags.astype(jnp.int32), 1) - 1
    picker = (ranks[:, None, :] == jnp.arange(CAP)[None, :, None]) & flags[:, None, :]
    packed = jnp.dot(
        picker.reshape(2 * CAP, tok_rows).astype(BF16), grad_rows, preferred_element_type=F32
    ).astype(BF16)
    tally = jnp.sum(flags.astype(jnp.int32), 1)
    front = swapped(
        jnp.concatenate([packed[CAP:, :LEAD], count_rows(tally[1], 2, LEAD)], 0), group
    )
    first_part = jnp.concatenate(
        [
            packed[:CAP, :LEAD],
            front[:CAP],
            lead_factor[:, :LEAD],
            front[CAP:] + count_rows(tally[0], 0, LEAD),
        ],
        0,
    )
    away_rows = copied([(packed, (CAP, width), [1, 0])], [front])[0]
    incoming = swapped(away_rows, group)
    outgoing = jnp.concatenate([packed[:CAP], lead_factor], 0)
    quarter = jnp.concatenate([packed[:CAP], incoming, lead_factor], 0)
    across_own = gather_members(outgoing, bits)
    across_other = gather_members(incoming, bits)

    ends = [*range(LEAD, width, LEAD), width]
    chunks = list(zip([0, *ends], ends))
    rows = quarter.shape[0]
    later = [
        (quarter, (rows, end - begin), [0, begin // (end - begin)]) for begin, end in chunks[1:]
    ]
    parts = [first_part, *copied(later, [across_own[1]])]
    spread = [lax.all_gather(part, "fac") for part in parts]
    rows = first_part.shape[0]
    earlier = [across_other[1], moved, *parts[1:]]
    lead = copied([(spread[0], (None, rows, LEAD), [0, 0, 0])], earlier)[0]
    slots = [member, column, member * width] + order + [member] + [0] * (group - 1)
    assert len(slots) == PLACES + 2 * group
    slots = jnp.stack([jnp.int32(slot) for slot in slots])
    across, near_factor = stacked(slots, across_own, across_other, [lead])
    lead = gather_members(lead, bits)
    flag = (member >> (bits - 1) & 1)[None]
    for bit in reversed(range(bits - 1)):
        near = chosen(flag, moved, near, [across])
        moved = lax.ppermute(near, "tok", down_pairs(bit, group))
        flag = (member >> bit & 1)[None]
    sent = copied(member_blocks(spread[0], member, group), [lead[1], near])

    lower, inverse, share = factor_lead(slots, damp, factor_old, lead, sent[:1])
    panel, lead_stack = panel_columns(
        share, inverse, near_factor, lead, across, spread[1:2]
    )

    token = panel
    results = []
    for number, (begin, _) in enumerate(chunks):
        requests = []
        if number + 1 < len(chunks):
            requests = member_blocks(spread[number + 1], member, group)
        pieces, sent = exchange_members(spread[number], sent, bits, requests, [token])
        if number == 0:
            high, low = solve_lead(flag, inverse, moved, near, [])
        *results, token = finish_rows(
            begin,
            slots,
            damp,
            share,
            factor_old,
            weight_grad,
            panel,
            inverse,
            lower,
            high,
            low,
            lead_stack,
            across,
            pieces,
            results,
            sent[:1],
        )
    return tuple(results)


def solution(mesh):
    placed = (P("tok", "fac"), P("tok", None), P("tok"), P("tok", "fac"), P(), P("tok", "fac"))
    return jax.shard_map(
        local,
        mesh=mesh,
        in_specs=placed,
        out_specs=(P("tok", "fac"), P("tok", "fac"), P("tok", "fac")),
        check_vma=False,
    )
```

```python
import jax
import jax.numpy as jnp
from jax import lax
from jax.experimental import pallas as pl
from jax.experimental.pallas import tpu as pltpu
from jax.sharding import PartitionSpec as P

CAP = 320
LEAD = 512
TILE = 128
GROUP = 8
ROWS = 256
COLS = 512
PLACES = 3
VMEM_BYTES = 60 * 1024 * 1024
ANYWHERE = pl.BlockSpec(memory_space=pl.ANY)
NO_COST = pl.CostEstimate(flops=1, bytes_accessed=1, transcendentals=0)
DECAY = 0.8

HIGHEST = lax.Precision.HIGHEST
BF16 = jnp.bfloat16
F32 = jnp.float32


def dot_t(left, right, precision=None):
    return lax.dot_general(
        left, right, (((0,), (0,)), ((), ())), precision=precision, preferred_element_type=F32
    )


def split(value):
    high = value.astype(BF16)
    return high, (value - high.astype(F32)).astype(BF16)


def dot_split(left, right, contract):
    (left_high, left_low), (right_high, right_low) = split(left), split(right)
    product = lambda a, b: lax.dot_general(
        a, b, (contract, ((), ())), preferred_element_type=F32
    )
    return product(left_high, right_high) + (
        product(left_high, right_low) + product(left_low, right_high)
    )


def splat(rows, lane):
    return jnp.broadcast_to(rows[:, lane : lane + 1], rows.shape)


def eliminate_tile(rows):
    lanes = lax.broadcasted_iota(jnp.int32, (GROUP, TILE), 1)
    subs = lax.broadcasted_iota(jnp.int32, (GROUP, TILE), 0)
    upper, inverse = [], []
    for step in range(TILE // GROUP):
        base = step * GROUP
        inside = (lanes >= base) & (lanes < base + GROUP)
        block = rows[step]
        first = [jnp.broadcast_to(block[t : t + 1, :], (GROUP, TILE)) for t in range(GROUP)]
        second = [
            jnp.where(inside, jnp.where(lanes == base + t, 1.0, 0.0), first[t])
            for t in range(GROUP)
        ]
        pivot = [
            [splat(first[t], base + u) if u >= t else None for u in range(GROUP)]
            for t in range(GROUP)
        ]
        coming = rows[step + 1] if step + 1 < TILE // GROUP else block
        factors = [splat(coming, base + u) for u in range(GROUP)]
        coming = jnp.where(inside, 0.0, coming)
        scale = [None] * GROUP
        for t in range(GROUP):
            scale[t] = lax.rsqrt(pivot[t][t])
            for u in range(t + 1, GROUP):
                pivot[t][u] = pivot[t][u] * scale[t]
            for u in range(t + 1, GROUP):
                for w in range(u, GROUP):
                    pivot[u][w] = pivot[u][w] - pivot[t][u] * pivot[t][w]
            first[t] = first[t] * scale[t]
            second[t] = second[t] * scale[t]
            factors[t] = factors[t] * scale[t]
            coming = coming - factors[t] * second[t]
            for u in range(t + 1, GROUP):
                first[u] = first[u] - pivot[t][u] * first[t]
                second[u] = second[u] - pivot[t][u] * second[t]
                factors[u] = factors[u] - pivot[t][u] * factors[t]
        solved = [None] * GROUP
        for t in reversed(range(GROUP)):
            value = second[t]
            for u in range(t + 1, GROUP):
                value = value - pivot[t][u] * solved[u]
            solved[t] = value * scale[t]
        if step + 1 < TILE // GROUP:
            rows[step + 1] = coming
        for later in range(step + 2, TILE // GROUP):
            value = jnp.where(inside, 0.0, rows[later])
            for t in range(GROUP):
                value = value - splat(rows[later], base + t) * solved[t]
            rows[later] = value
        upper_rows, inverse_rows = first[0], second[0]
        for t in range(1, GROUP):
            upper_rows = jnp.where(subs == t, first[t], upper_rows)
            inverse_rows = jnp.where(subs == t, second[t], inverse_rows)
        upper.append(upper_rows)
        inverse.append(inverse_rows)
    return upper, inverse


def factor_kernel(count, places_ref, damp_ref, exact_ref, *refs):
    lead_refs = refs[:count]
    lower_ref, inverse_ref, share_ref, work_ref, upper_ref = refs[-5:]
    steps = LEAD // TILE
    side = LEAD // count
    marks = sum(lead[2 * CAP + side :, :].astype(F32) for lead in lead_refs)
    row = lax.broadcasted_iota(jnp.int32, marks.shape, 0)
    weight = jnp.where(row < 4, jnp.where(row % 2 == 0, 256.0, 1.0), 0.0)
    total = jnp.sum(marks * weight, axis=0, keepdims=True)[:, :1]
    share = (1.0 - DECAY) / total
    share_ref[...] = jnp.broadcast_to(share, share_ref.shape)
    for q, lead in enumerate(lead_refs):
        begin = pl.multiple_of(places_ref[PLACES + q] * side, side)
        work_ref[pl.ds(begin, side), :] = lead[2 * CAP : 2 * CAP + side, :].astype(F32)

    @pl.when((places_ref[0] == 0) & (places_ref[1] == 0))
    def _():
        work_ref[...] = exact_ref[...]

    gram = sum(dot_t(lead[: 2 * CAP, :], lead[: 2 * CAP, :]) for lead in lead_refs)
    rows = lax.broadcasted_iota(jnp.int32, (LEAD, LEAD), 0)
    cols = lax.broadcasted_iota(jnp.int32, (LEAD, LEAD), 1)
    work_ref[...] = (
        DECAY * work_ref[...] + share * gram + jnp.where(rows == cols, damp_ref[0], 0.0)
    )
    lanes = lax.broadcasted_iota(jnp.int32, (GROUP, TILE), 1)
    subs = lax.broadcasted_iota(jnp.int32, (GROUP, TILE), 0)

    def tile_step(k, carry):
        begin = pl.multiple_of(k * TILE, TILE)
        rows = [
            work_ref[pl.ds(begin + g * GROUP, GROUP), pl.ds(begin, TILE)]
            for g in range(TILE // GROUP)
        ]
        upper, inverse = eliminate_tile(rows)
        upper_tile = jnp.concatenate(
            [jnp.where(lanes >= subs + g * GROUP, part, 0.0) for g, part in enumerate(upper)], 0
        )
        inverse_tile = jnp.concatenate(
            [jnp.where(lanes <= subs + g * GROUP, part, 0.0) for g, part in enumerate(inverse)], 0
        )
        band = dot_split(inverse_tile, work_ref[pl.ds(begin, TILE), :], ((1,), (0,)))
        work_ref[pl.ds(begin, TILE), :] = band
        work_ref[pl.ds(begin, TILE), pl.ds(begin, TILE)] = inverse_tile
        band = work_ref[pl.ds(begin, TILE), :]
        at = lax.broadcasted_iota(jnp.int32, (TILE, LEAD), 1)
        right = jnp.where(at >= begin + TILE, band, 0.0)
        inverse_ref[pl.ds(begin, TILE), :] = jnp.where(at < begin + TILE, band, 0.0)
        upper_ref[pl.ds(begin, TILE), :] = right
        upper_ref[pl.ds(begin, TILE), pl.ds(begin, TILE)] = upper_tile
        down = lax.broadcasted_iota(jnp.int32, (LEAD, TILE), 0)
        column = work_ref[:, pl.ds(begin, TILE)]
        work_ref[:, pl.ds(begin, TILE)] = jnp.where(down >= begin + TILE, 0.0, column)
        work_ref[...] = work_ref[...] - dot_split(right, band, ((0,), (0,)))
        return carry

    lax.fori_loop(0, steps, tile_step, 0)
    lower_ref[...] = upper_ref[...].T


def factor_lead(places, damp, exact, lead, earlier):
    shape = jax.ShapeDtypeStruct((LEAD, LEAD), F32)
    vmem = pl.BlockSpec(memory_space=pltpu.VMEM)
    smem = pl.BlockSpec(memory_space=pltpu.SMEM)
    return pl.pallas_call(
        lambda *refs: factor_kernel(len(lead), *refs),
        grid=(1,),
        out_shape=(shape, shape, jax.ShapeDtypeStruct((GROUP, TILE), F32)),
        in_specs=[smem, smem, pl.BlockSpec((LEAD, LEAD), lambda i: (0, 0))]
        + [vmem] * len(lead)
        + [ANYWHERE] * len(earlier),
        out_specs=(vmem, vmem, vmem),
        scratch_shapes=[pltpu.VMEM((LEAD, LEAD), F32)] * 2,
        compiler_params=pltpu.CompilerParams(vmem_limit_bytes=VMEM_BYTES),
        cost_estimate=NO_COST,
    )(places, damp, exact, *lead, *earlier)


def stack_kernel(count, places_ref, *refs):
    own, other = refs[:count], refs[count : 2 * count]
    stack_ref, near_ref = refs[-2:]
    depth, side = 2 * CAP, LEAD // count
    for q in range(count):
        stack_ref[q * depth : q * depth + CAP, :] = own[q][:CAP, :]
        stack_ref[q * depth + CAP : (q + 1) * depth, :] = other[q][...]
        begin = pl.multiple_of(places_ref[PLACES + q] * side, side)
        near_ref[pl.ds(begin, side), :] = own[q][CAP:, :]


def stacked(places, own, other, earlier):
    count = len(own)
    rows, width = own[0].shape
    cols = COLS if width % COLS == 0 else ROWS
    tiled = lambda height: pl.BlockSpec((height, cols), lambda j: (0, j))
    return pl.pallas_call(
        lambda *refs: stack_kernel(count, *refs),
        grid=(width // cols,),
        out_shape=(
            jax.ShapeDtypeStruct((2 * CAP * count, width), BF16),
            jax.ShapeDtypeStruct((LEAD, width), BF16),
        ),
        in_specs=[pl.BlockSpec(memory_space=pltpu.SMEM)]
        + [tiled(rows)] * count
        + [tiled(CAP)] * count
        + [ANYWHERE] * len(earlier),
        out_specs=(tiled(2 * CAP * count), tiled(LEAD)),
        compiler_params=pltpu.CompilerParams(vmem_limit_bytes=VMEM_BYTES),
        cost_estimate=NO_COST,
    )(places, *own, *other, *earlier)


def panel_kernel(count, share_ref, inverse_ref, near_ref, across_ref, *refs):
    lead = refs[:count]
    out_ref, lead_ref = refs[-2:]
    depth = 2 * CAP

    @pl.when(pl.program_id(0) == 0)
    def _():
        for q in range(count):
            lead_ref[q * depth : (q + 1) * depth, :] = lead[q][:depth, :]

    gram = dot_t(lead_ref[...], across_ref[...])
    beside = DECAY * near_ref[...].astype(F32) + share_ref[:1, :1] * gram
    out_ref[...] = dot_split(inverse_ref[...], beside, ((1,), (0,))).astype(BF16)


def panel_columns(share, inverse, near, lead, across, earlier):
    count = len(lead)
    tall, width = across.shape
    cols = COLS if width % COLS == 0 else ROWS
    whole = lambda height: pl.BlockSpec((height, LEAD), lambda j: (0, 0))
    tiled = lambda height: pl.BlockSpec((height, cols), lambda j: (0, j))
    return pl.pallas_call(
        lambda *refs: panel_kernel(count, *refs),
        grid=(width // cols,),
        out_shape=(
            jax.ShapeDtypeStruct((LEAD, width), BF16),
            jax.ShapeDtypeStruct((tall, LEAD), BF16),
        ),
        in_specs=[
            pl.BlockSpec((GROUP, TILE), lambda j: (0, 0)),
            whole(LEAD),
            tiled(LEAD),
            tiled(tall),
        ]
        + [whole(lead[0].shape[0])] * count
        + [ANYWHERE] * len(earlier),
        out_specs=(tiled(LEAD), whole(tall)),
        compiler_params=pltpu.CompilerParams(vmem_limit_bytes=VMEM_BYTES),
        cost_estimate=NO_COST,
    )(share, inverse, near, across, *lead, *earlier)


def solve_kernel(flag_ref, inverse_ref, first_ref, second_ref, *refs):
    high_ref, low_ref, parts_ref = refs[-3:]

    @pl.when(pl.program_id(0) == 0)
    def _():
        parts_ref[0], parts_ref[1] = split(inverse_ref[...])

    values = jnp.where(flag_ref[0] == 1, first_ref[...], second_ref[...])
    solved = jnp.dot(parts_ref[0], values, preferred_element_type=F32)
    solved = solved + jnp.dot(parts_ref[1], values, preferred_element_type=F32)
    high_ref[...], low_ref[...] = split(solved)


def solve_lead(flag, inverse, first, second, earlier):
    tiled = pl.BlockSpec((LEAD, COLS), lambda j: (0, j))
    return pl.pallas_call(
        solve_kernel,
        grid=(first.shape[1] // COLS,),
        out_shape=(jax.ShapeDtypeStruct(first.shape, BF16),) * 2,
        in_specs=[
            pl.BlockSpec(memory_space=pltpu.SMEM),
            pl.BlockSpec((LEAD, LEAD), lambda j: (0, 0)),
            tiled,
            tiled,
        ]
        + [ANYWHERE] * len(earlier),
        out_specs=(tiled, tiled),
        scratch_shapes=[pltpu.VMEM((2, LEAD, LEAD), BF16)],
        compiler_params=pltpu.CompilerParams(vmem_limit_bytes=VMEM_BYTES),
        cost_estimate=NO_COST,
    )(flag, inverse, first, second, *earlier)


def finish_kernel(
    count,
    gram_steps,
    begin,
    unread,
    places_ref,
    damp_ref,
    share_ref,
    factor_ref,
    grad_ref,
    panel_ref,
    inverse_ref,
    high_ref,
    lead_ref,
    across_ref,
    *refs,
):
    first_chunk = begin == 0
    if first_chunk:
        lower_ref, low_ref, *refs = refs
    mine = refs[:count]
    outs = refs[count + unread :]
    running_ref, factored_ref, precond_ref, token_ref, mine_ref, rows_ref, first_ref = outs
    j, i = pl.program_id(0), pl.program_id(1)
    member, column, base = places_ref[0], places_ref[1], places_ref[2] + begin
    share, damp = share_ref[:1, :1], damp_ref[0]
    height, cols = running_ref.shape
    depth = 2 * CAP
    side = LEAD // count
    span = pl.ds(pl.multiple_of(i * height, height), height)
    head = (member == 0) & first_chunk

    @pl.when(j == 0)
    def _():
        token_ref[...] = jnp.zeros_like(token_ref)
        for q in range(count):
            mine_ref[span, q * depth : (q + 1) * depth] = mine[q][0, :depth, :].T
            place = pl.multiple_of(places_ref[PLACES + q] * side, side)
            first_ref[pl.ds(place, side), :] = mine[q][0, depth : depth + side, :].astype(F32)
        source = first_ref[...].T
        if cols == LEAD:
            source = jnp.where(column == 0, factor_ref[...], source)
        gram = jnp.dot(mine_ref[span, :], lead_ref[...], preferred_element_type=F32)
        row = base + i * height + lax.broadcasted_iota(jnp.int32, (height, LEAD), 0)
        col = lax.broadcasted_iota(jnp.int32, (height, LEAD), 1)
        source = DECAY * source + share * gram
        source = source + jnp.where(row == col, damp, 0.0)
        rows_ref[span, :] = dot_split(source, inverse_ref[...], ((1,), (1,)))

    panel = rows_ref[span, :].astype(BF16)

    @pl.when(j < gram_steps)
    def _():
        gram = jnp.dot(mine_ref[span, :], across_ref[...], preferred_element_type=F32)
        running = DECAY * factor_ref[...] + share * gram
        running_ref[...] = running
        row = base + i * height + lax.broadcasted_iota(jnp.int32, (height, cols), 0)
        col = (column * gram_steps + j) * cols + lax.broadcasted_iota(jnp.int32, (height, cols), 1)
        matrix = running + jnp.where(row == col, damp, 0.0)
        factored = matrix - jnp.dot(panel, panel_ref[...], preferred_element_type=F32)
        factored_ref[...] = jnp.where(head, 0.0, factored)

        for part in range(LEAD // cols):
            edge = slice(part * cols, (part + 1) * cols)

            @pl.when((column == 0) & (j == part))
            def _():
                factored_ref[...] = rows_ref[span, edge]

                if first_chunk:

                    @pl.when(head)
                    def _():
                        factored_ref[...] = lower_ref[span, edge]

    product = jnp.dot(panel, high_ref[...], preferred_element_type=F32)
    precond_ref[...] = grad_ref[...].astype(F32) - product

    if first_chunk:

        @pl.when(head)
        def _():
            precond_ref[...] = high_ref[span, :].astype(F32) + low_ref[span, :].astype(F32)


def finish_rows(
    begin, places, damp, share, factor, grad, panel, inverse, lower, high, low,
    lead, across, mine, results, earlier,
):
    count = len(mine)
    deep, rows = mine[0].shape[1:]
    width, grad_cols = factor.shape[0], grad.shape[1]
    tall = lead.shape[0]
    height = min(rows, COLS)
    tiles = rows // height
    start = begin // height
    cols = COLS if width % COLS == 0 else ROWS
    gram_steps, steps = width // cols, grad_cols // cols
    assert steps >= gram_steps and rows % height == 0 and begin % height == 0

    def mine_spec(q):
        return pl.BlockSpec(
            (1, deep, height),
            lambda j, i, p: (p[PLACES + count + q], 0, jnp.where(j == 0, i, tiles - 1)),
        )

    def gram_col(j):
        return jnp.minimum(j, gram_steps - 1)

    def gram_tile(j, i, p):
        return (start + jnp.where(j < gram_steps, i, tiles - 1), gram_col(j))

    grad_spec = pl.BlockSpec((height, cols), lambda j, i, p: (start + i, j))
    factor_spec = pl.BlockSpec((height, cols), gram_tile)
    lead_whole = pl.BlockSpec((LEAD, LEAD), lambda j, i, p: (0, 0))
    small = pl.BlockSpec((GROUP, TILE), lambda j, i, p: (0, 0))
    in_specs = [
        pl.BlockSpec(memory_space=pltpu.SMEM),
        small,
        factor_spec,
        grad_spec,
        pl.BlockSpec((LEAD, cols), lambda j, i, p: (0, gram_col(j))),
        lead_whole,
        pl.BlockSpec((LEAD, cols), lambda j, i, p: (0, j)),
        pl.BlockSpec((tall, LEAD), lambda j, i, p: (0, 0)),
        pl.BlockSpec((tall, cols), lambda j, i, p: (0, gram_col(j))),
    ]
    operands = [damp, share, factor, grad, panel, inverse, high, lead, across]
    if begin == 0:
        in_specs += [lead_whole, pl.BlockSpec((LEAD, cols), lambda j, i, p: (0, j))]
        operands += [lower, low]
    in_specs += [mine_spec(q) for q in range(count)]
    operands += mine
    aliases = {1 + len(operands) + k: k for k in range(len(results))}
    operands += [*results, *earlier]
    unread = len(results) + len(earlier)
    in_specs += [ANYWHERE] * unread
    return pl.pallas_call(
        lambda *refs: finish_kernel(count, gram_steps, begin, unread, *refs),
        grid_spec=pltpu.PrefetchScalarGridSpec(
            num_scalar_prefetch=1,
            grid=(steps, tiles),
            in_specs=in_specs,
            out_specs=(factor_spec, factor_spec, grad_spec, small),
            scratch_shapes=[
                pltpu.VMEM((rows, tall), BF16),
                pltpu.VMEM((rows, LEAD), F32),
                pltpu.VMEM((LEAD, height), F32),
            ],
        ),
        out_shape=(
            jax.ShapeDtypeStruct(factor.shape, F32),
            jax.ShapeDtypeStruct(factor.shape, F32),
            jax.ShapeDtypeStruct(grad.shape, F32),
            jax.ShapeDtypeStruct((GROUP, TILE), F32),
        ),
        input_output_aliases=aliases,
        compiler_params=pltpu.CompilerParams(vmem_limit_bytes=VMEM_BYTES),
        cost_estimate=NO_COST,
    )(places, *operands)


def swapped(value, mask):
    size = lax.axis_size("tok")
    return lax.ppermute(value, "tok", [(source, source ^ mask) for source in range(size)])


def gather_members(value, bits):
    pieces = [value]
    for bit in reversed(range(bits)):
        pieces = pieces + [swapped(piece, 1 << bit) for piece in pieces]
    return pieces


def copy_kernel(count, places_ref, *refs):
    for source, out in zip(refs[:count], refs[-count:]):
        out[...] = source[...].astype(BF16)


def copied(requests, earlier):
    in_specs, out_specs, shapes, places = [], [], [], []
    for array, block, place in requests:
        at = len(places)
        places += place
        shape = tuple(size for size in block if size is not None)
        shapes.append(shape)
        in_specs.append(
            pl.BlockSpec(block, lambda i, p, a=at, n=len(block): tuple(p[a + k] for k in range(n)))
        )
        out_specs.append(pl.BlockSpec(shape, lambda i, p: (0, 0)))
    arrays = [array for array, _, _ in requests]
    return pl.pallas_call(
        lambda *refs: copy_kernel(len(arrays), *refs),
        grid_spec=pltpu.PrefetchScalarGridSpec(
            num_scalar_prefetch=1,
            grid=(1,),
            in_specs=in_specs + [ANYWHERE] * len(earlier),
            out_specs=out_specs,
        ),
        out_shape=[jax.ShapeDtypeStruct(shape, BF16) for shape in shapes],
        compiler_params=pltpu.CompilerParams(vmem_limit_bytes=VMEM_BYTES),
        cost_estimate=NO_COST,
    )(jnp.stack([jnp.int32(place) for place in places]), *arrays, *earlier)


def choose_kernel(flag_ref, first_ref, second_ref, *refs):
    refs[-1][...] = jnp.where(flag_ref[0] == 1, first_ref[...], second_ref[...])


def chosen(flag, first, second, earlier):
    tiled = pl.BlockSpec((first.shape[0] // 2, first.shape[1]), lambda i: (i, 0))
    return pl.pallas_call(
        choose_kernel,
        grid=(2,),
        out_shape=jax.ShapeDtypeStruct(first.shape, first.dtype),
        in_specs=[pl.BlockSpec(memory_space=pltpu.SMEM), tiled, tiled] + [ANYWHERE] * len(earlier),
        out_specs=tiled,
        compiler_params=pltpu.CompilerParams(vmem_limit_bytes=VMEM_BYTES),
        cost_estimate=NO_COST,
    )(flag, first, second, *earlier)


def member_blocks(blocks, member, group):
    _, rows, width = blocks.shape
    return [(blocks, (None, rows, width), [member ^ other, 0, 0]) for other in range(1, group)]


def exchange_members(blocks, sent, bits, requests, earlier):
    held = [[blocks]] + [[part] for part in sent]
    copies = None
    for bit in reversed(range(bits)):
        half = 1 << bit
        arrived = [(part, part.shape, [0, 0]) for passed in held[half:] for part in passed[1:]]
        if arrived:
            passing = copied(
                requests + arrived if copies is None else arrived, earlier + held[0][1:]
            )
            if copies is None:
                copies, passing = passing[: len(requests)], passing[len(requests) :]
            for passed in held[half:]:
                count = len(passed) - 1
                passed[1:], passing = passing[:count], passing[count:]
        held = [
            kept + [swapped(part, half) for part in passed]
            for kept, passed in zip(held[:half], held[half:])
        ]
    first, *others = held[0]
    return [first] + [part[None] for part in others], copies


def member_order(bits):
    order = [0]
    for bit in reversed(range(bits)):
        order = order + [other ^ (1 << bit) for other in order]
    return order


def down_pairs(bit, group):
    mask = 1 << bit
    return [
        (source, source + mask)
        for source in range(lax.axis_size("tok"))
        if source % group % (2 * mask) == 0
    ]


def share_of_first(lower, upper, member, group, bits):
    for bit in reversed(range(bits)):
        moved = lax.ppermute(upper, "tok", down_pairs(bit, group))
        blocks = jnp.where(member >> bit & 1 == 1, moved, lower)
        half = blocks.shape[0] // 2
        lower, upper = blocks[:half], blocks[half:]
    return blocks


def count_rows(number, row, width):
    index = lax.broadcasted_iota(jnp.int32, (16, width), 0)
    rest = jnp.where(index == row + 1, number % 256, 0)
    return jnp.where(index == row, number // 256, rest).astype(BF16)


def local(grad_rows, routes, counts, factor_old, damping, weight_grad):
    group = lax.axis_size("tok") // 2
    bits = group.bit_length() - 1
    position = lax.axis_index("tok")
    expert = position // group
    member = position % group
    column = lax.axis_index("fac")
    tok_rows, width = grad_rows.shape
    damp = jnp.where(expert == 0, damping[0], damping[1])[None]
    order = [member ^ other for other in member_order(bits)]

    side = LEAD // 2
    halves = [(factor_old, (side, width), [place, 0]) for place in range(2)]
    halves = copied(halves, [])
    lead_factor = share_of_first(*halves, member, group, bits)

    live = jnp.arange(tok_rows) < counts[0]
    named = routes[:, 0]
    own = live & (named == expert)
    away = live & (named != expert)
    flags = jnp.stack([own, away])
    ranks = jnp.cumsum(flags.astype(jnp.int32), 1) - 1
    picker = (ranks[:, None, :] == jnp.arange(CAP)[None, :, None]) & flags[:, None, :]
    packed = jnp.dot(
        picker.reshape(2 * CAP, tok_rows).astype(BF16), grad_rows, preferred_element_type=F32
    ).astype(BF16)
    tally = jnp.sum(flags.astype(jnp.int32), 1)
    front = swapped(
        jnp.concatenate([packed[CAP:, :LEAD], count_rows(tally[1], 2, LEAD)], 0), group
    )
    first_part = jnp.concatenate(
        [
            packed[:CAP, :LEAD],
            front[:CAP],
            lead_factor[:, :LEAD],
            front[CAP:] + count_rows(tally[0], 0, LEAD),
        ],
        0,
    )
    away_rows = copied([(packed, (CAP, width), [1, 0])], [front])[0]
    incoming = swapped(away_rows, group)
    outgoing = jnp.concatenate([packed[:CAP], lead_factor], 0)
    quarter = jnp.concatenate([packed[:CAP], incoming, lead_factor], 0)
    across_own = gather_members(outgoing, bits)
    across_other = gather_members(incoming, bits)

    ends = [*range(LEAD, width, LEAD), width]
    chunks = list(zip([0, *ends], ends))
    rows = quarter.shape[0]
    later = [
        (quarter, (rows, end - begin), [0, begin // (end - begin)]) for begin, end in chunks[1:]
    ]
    parts = [first_part, *copied(later, [across_own[1]])]
    spread = [lax.all_gather(part, "fac") for part in parts]
    rows = first_part.shape[0]
    earlier = [across_other[1], *parts[1:]]
    lead = copied([(spread[0], (None, rows, LEAD), [0, 0, 0])], earlier)[0]
    slots = [member, column, member * width] + order + [member] + [0] * (group - 1)
    assert len(slots) == PLACES + 2 * group
    slots = jnp.stack([jnp.int32(slot) for slot in slots])
    across, near_factor = stacked(slots, across_own, across_other, [lead])
    lead = gather_members(lead, bits)
    sent = copied(member_blocks(spread[0], member, group), [lead[1], across])

    near = copied([(weight_grad, (LEAD, weight_grad.shape[1]), [0, 0])], [across_other[1]])[0]
    moved = lax.ppermute(near, "tok", down_pairs(bits - 1, group))
    flag = (member >> (bits - 1) & 1)[None]
    for bit in reversed(range(bits - 1)):
        near = chosen(flag, moved, near, sent[:1])
        moved = lax.ppermute(near, "tok", down_pairs(bit, group))
        flag = (member >> bit & 1)[None]

    lower, inverse, share = factor_lead(slots, damp, factor_old, lead, [near])
    panel, lead_stack = panel_columns(
        share, inverse, near_factor, lead, across, spread[1:2]
    )

    token = panel
    results = []
    for number, (begin, _) in enumerate(chunks):
        requests = []
        if number + 1 < len(chunks):
            requests = member_blocks(spread[number + 1], member, group)
        pieces, sent = exchange_members(spread[number], sent, bits, requests, [token])
        if number == 0:
            high, low = solve_lead(flag, inverse, moved, near, [])
        *results, token = finish_rows(
            begin,
            slots,
            damp,
            share,
            factor_old,
            weight_grad,
            panel,
            inverse,
            lower,
            high,
            low,
            lead_stack,
            across,
            pieces,
            results,
            sent[:1],
        )
    return tuple(results)


def solution(mesh):
    placed = (P("tok", "fac"), P("tok", None), P("tok"), P("tok", "fac"), P(), P("tok", "fac"))
    return jax.shard_map(
        local,
        mesh=mesh,
        in_specs=placed,
        out_specs=(P("tok", "fac"), P("tok", "fac"), P("tok", "fac")),
        check_vma=False,
    )
```
